32 devices in a mesh: seq: 8 (over z, x), head: 4 (over y, core).
Axes of the slice: x: 2, y: 2, z: 4, core: 2. Of those that a mesh axis runs over, the one named last changes fastest.
Arguments:
- activations: bfloat16 [2, 2, 1024, 1792], P(None, None, 'seq'), may hold values from -6 to 6
- offsets: int32 [2, 2], replicated, may hold values from 1 to 1023, as said below
- cotangent: bfloat16 [2, 2, 1024, 1792], P(None, None, 'seq'), may hold values from -6 to 6
- attn_query: bfloat16 [1792, 256], P('seq', 'head'), may hold values from -0.125 to 0.125
- attn_key: bfloat16 [1792, 256], P('seq', 'head'), may hold values from -0.125 to 0.125
- attn_value: bfloat16 [1792, 1792], P('seq', 'head'), may hold values from -0.125 to 0.125
- attn_output: bfloat16 [1792, 1792], P('head', 'seq'), may hold values from -3 to 3
- ffn1_gate: bfloat16 [1792, 4608], P('seq', 'head'), may hold values from -0.125 to 0.125
- ffn1_up: bfloat16 [1792, 4608], P('seq', 'head'), may hold values from -0.125 to 0.125
- ffn1_down: bfloat16 [4608, 1792], P('head', 'seq'), may hold values from -0.09375 to 0.09375
- conv_input: bfloat16 [1792, 1792], P('seq', 'head'), may hold values from -0.125 to 0.125
- conv_gate: bfloat16 [1792, 1792], P('seq', 'head'), may hold values from -0.125 to 0.125
- conv_output: bfloat16 [1792, 1792], P('head', 'seq'), may hold values from -0.125 to 0.125
- conv_kernel: bfloat16 [3, 1792], P(None, 'head'), may hold values from -3.5 to 3.5
- ffn2_gate: bfloat16 [1792, 4608], P('seq', 'head'), may hold values from -0.125 to 0.125
- ffn2_up: bfloat16 [1792, 4608], P('seq', 'head'), may hold values from -0.125 to 0.125
- ffn2_down: bfloat16 [4608, 1792], P('head', 'seq'), may hold values from -0.09375 to 0.09375
- norm_gains: bfloat16 [4, 1792], replicated, may hold values from 0.099609375 to 1.8984375
Outputs:
- block_output: bfloat16 [2, 2, 1024, 1792], P(None, None, 'seq')
- input_grad: float32 [2, 2, 1024, 1792], P(None, None, 'seq')
- query_grad: float32 [1792, 256], P('seq', 'head')
- key_grad: float32 [1792, 256], P('seq', 'head')
- value_grad: float32 [1792, 1792], P('seq', 'head')
- output_grad: float32 [1792, 1792], P('head', 'seq')
- ffn1_gate_grad: float32 [1792, 4608], P('seq', 'head')
- ffn1_up_grad: float32 [1792, 4608], P('seq', 'head')
- ffn1_down_grad: float32 [4608, 1792], P('head', 'seq')
- conv_input_grad: float32 [1792, 1792], P('seq', 'head')
- conv_gate_grad: float32 [1792, 1792], P('seq', 'head')
- conv_output_grad: float32 [1792, 1792], P('head', 'seq')
- conv_kernel_grad: float32 [3, 1792], P(None, 'head')
- ffn2_gate_grad: float32 [1792, 4608], P('seq', 'head')
- ffn2_up_grad: float32 [1792, 4608], P('seq', 'head')
- ffn2_down_grad: float32 [4608, 1792], P('head', 'seq')
- gains_grad: float32 [4, 1792], replicated
The draws below stay inside these ranges and needn't reach their ends.
Inputs may be any that keep to these rules, and one draw needn't show every extreme that they name: In micro-batch m, sequence r holds one document at positions before offsets[m, r] and a second from there on; in every micro-batch some sequence's second document begins before position 128.
All inputs are finite; a program needn't handle non-finite values.
Results may differ from the reference program's by a relative error of at most 0.03.
Values may be sent and summed in bfloat16 or wider, within the bound.
A program may use at most 256 MiB of HBM per device.

```python
import math
from functools import partial
import jax
import jax.numpy as jnp
from jax import lax

D = 1792
HEADS = 16
QK = 16
VH = 112
FF = 4608
KS = 3
TOK_ROW = 128
ROWS = 2
MICRO = 2
HQ = 256
LENGTH = 1024


def draw_offsets(key, part):
    key = jax.random.fold_in(key, 7)
    base_key, early_key, pick_key = jax.random.split(key, 3)
    offsets = jax.random.randint(base_key, (MICRO, ROWS), 1, LENGTH, dtype=jnp.int32)
    early_pos = jax.random.randint(early_key, (MICRO, 1), 1, TOK_ROW, dtype=jnp.int32)
    chosen = jax.random.randint(pick_key, (MICRO, 1), 0, ROWS, dtype=jnp.int32)
    row_ids = jnp.arange(ROWS, dtype=jnp.int32)[None, :]
    batch_ids = jnp.arange(MICRO, dtype=jnp.int32)[:, None]
    offsets = jnp.where(row_ids == chosen, early_pos, offsets)
    first_row = (row_ids == chosen) & (batch_ids == 0)
    other_row = (row_ids == (chosen + 1) % ROWS) & (batch_ids == 0)
    offsets = jnp.where(first_row, 1, offsets)
    offsets = jnp.where(other_row, LENGTH - 1, offsets)
    return offsets.astype(jnp.int32)


def block_levels(rng, dims, pieces, least, high):
    def one(axis_at, parts):
        heights = jax.random.uniform(jax.random.fold_in(jax.random.fold_in(rng, 6), axis_at), (parts,), jnp.float32, least / len(pieces), high / len(pieces))
        return jnp.repeat(jnp.exp(heights), dims[axis_at] // parts).reshape((-1,) + (1,) * (len(dims) - axis_at - 1))

    loudness = one(*pieces[0])
    for cut in pieces[1:]:
        loudness = loudness * one(*cut)
    return loudness


def gaussian(stream_key, extent, spread, reach, cuts=(), held_as=jnp.bfloat16):
    drawn = spread * jax.random.normal(stream_key, extent, jnp.float32)
    if cuts:
        drawn = drawn * block_levels(stream_key, extent, cuts, -0.22, 0.18)
    return jnp.clip(drawn, -reach, reach).astype(held_as)


def setup_inputs(seed: int = 0) -> dict:
    splits = jax.random.split(jax.random.key(seed), 19)
    return {
        "activations": gaussian(splits[0], (MICRO, ROWS, LENGTH, D), 1.0, 6.0, ((2, 8),)),
        "offsets": draw_offsets(jax.random.fold_in(splits[18], 71), 0),
        "cotangent": gaussian(splits[2], (MICRO, ROWS, LENGTH, D), 1.0, 6.0, ((2, 8),)),
        "attn_query": gaussian(splits[3], (D, HQ), D ** -0.5, 0.125, ((0, 8), (1, 4))),
        "attn_key": gaussian(splits[4], (D, HQ), D ** -0.5, 0.125, ((0, 8), (1, 4))),
        "attn_value": gaussian(splits[5], (D, D), D ** -0.5, 0.125, ((0, 8), (1, 4))),
        "attn_output": gaussian(splits[6], (D, D), (max(4, D // 512)) ** -0.5, 3.0, ((0, 4), (1, 8))),
        "ffn1_gate": gaussian(splits[7], (D, FF), D ** -0.5, 0.125, ((0, 8), (1, 4))),
        "ffn1_up": gaussian(splits[8], (D, FF), D ** -0.5, 0.125, ((0, 8), (1, 4))),
        "ffn1_down": gaussian(splits[9], (FF, D), FF ** -0.5, 0.09375, ((0, 4), (1, 8))),
        "conv_input": gaussian(splits[10], (D, D), D ** -0.5, 0.125, ((0, 8), (1, 4))),
        "conv_gate": gaussian(splits[11], (D, D), D ** -0.5, 0.125, ((0, 8), (1, 4))),
        "conv_output": gaussian(splits[12], (D, D), D ** -0.5, 0.125, ((0, 4), (1, 8))),
        "conv_kernel": gaussian(splits[13], (KS, D), KS ** -0.5, 3.5, ((1, 4),)),
        "ffn2_gate": gaussian(splits[14], (D, FF), D ** -0.5, 0.125, ((0, 8), (1, 4))),
        "ffn2_up": gaussian(splits[15], (D, FF), D ** -0.5, 0.125, ((0, 8), (1, 4))),
        "ffn2_down": gaussian(splits[16], (FF, D), FF ** -0.5, 0.09375, ((0, 4), (1, 8))),
        "norm_gains": jnp.clip(1.0 + 0.18 * jax.random.normal(splits[17], (4, D), jnp.float32), 0.099609375, 1.8984375).astype(jnp.bfloat16),
    }


EPSILON = 1e-05
PRECISE = lax.Precision.HIGHEST

@jax.custom_vjp
def low(v):
    return lax.optimization_barrier(v.astype(jnp.bfloat16)).astype(jnp.float32)

@jax.custom_vjp
def low_back(v):
    return v

def low_keep(v):
    return (low(v), None)

def low_pass(kept, grad):
    return (grad,)

def back_keep(v):
    return (v, None)

def back_low(kept, grad):
    return (low(grad),)
low.defvjp(low_keep, low_pass)
low_back.defvjp(back_keep, back_low)

def matmul(left, right):
    return jnp.dot(left, right, precision=PRECISE)

def rms_norm(values, gain):
    scale = lax.rsqrt(lax.optimization_barrier(jnp.mean(values * values, axis=-1, keepdims=True)) + EPSILON)
    return values * scale * gain

def taylor_map(feature):
    width = feature.shape[-1]
    square = (feature[..., :, None] * feature[..., None, :]).reshape(feature.shape[:-1] + (width * width,))
    ones_col = jnp.ones(feature.shape[:-1] + (1,), jnp.float32)
    return jnp.concatenate([ones_col, feature / width ** 0.25, square / math.sqrt(2.0 * width)], axis=-1)

def doc_masks(offsets, start_pos, tok_count):
    position = start_pos + jnp.arange(tok_count, dtype=jnp.int32)
    current = position[None, :] >= offsets[:, None]
    before = start_pos - 1 >= offsets
    last_doc = current[:, -1]
    use_in = (current == before[:, None]).astype(jnp.float32)
    end_mask = (current == last_doc[:, None]).astype(jnp.float32)
    carry_on = (last_doc == before).astype(jnp.float32)
    causal = position[:, None] >= position[None, :]
    pair_mask = (causal[None, :, :] & (current[:, :, None] == current[:, None, :])).astype(jnp.float32)
    return (use_in, end_mask, carry_on, pair_mask)

def local_state(keys_f, values_f, end_mask):
    feats = taylor_map(keys_f) * end_mask[:, :, None, None]
    state = jnp.einsum('rthf,rthv->rhfv', feats, values_f, precision=PRECISE)
    return (state, lax.optimization_barrier(jnp.sum(feats, axis=1)))

def attend_local(query_f, keys_f, values_f, state_in, norm_in, use_in, pair_mask):
    qk_width = query_f.shape[-1]
    scores = jnp.einsum('rphf,rjhf->rhpj', query_f, keys_f, precision=PRECISE) / math.sqrt(qk_width)
    weights = (1.0 + scores + 0.5 * scores * scores) * pair_mask[:, None, :, :]
    feats = taylor_map(query_f)
    numer = jnp.einsum('rhpj,rjhv->rphv', weights, values_f, precision=PRECISE)
    numer = numer + use_in[:, :, None, None] * jnp.einsum('rphf,rhfv->rphv', feats, state_in, precision=PRECISE)
    denom = jnp.swapaxes(lax.optimization_barrier(jnp.sum(weights, axis=-1)), 1, 2)
    denom = denom + use_in[:, :, None] * jnp.einsum('rphf,rhf->rph', feats, norm_in, precision=PRECISE)
    return numer / denom[..., None]

def linear_attention(query, keys, values, offsets):
    row_count, length, head_count, qk_width = query.shape
    value_width = values.shape[-1]
    block = math.gcd(512, length)
    count = length // block

    def split_blocks(array):
        return jnp.moveaxis(array.reshape((row_count, count, block) + array.shape[2:]), 1, 0)

    def block_step(carry, inputs):
        state, norm = carry
        query_b, keys_b, values_b, index = inputs
        start_pos = index * block
        use_in, end_mask, carry_on, pair_mask = doc_masks(offsets, start_pos, block)
        result = attend_local(query_b, keys_b, values_b, state, norm, use_in, pair_mask)
        new_state, new_norm = local_state(keys_b, values_b, end_mask)
        state = carry_on[:, None, None, None] * state + new_state
        norm = carry_on[:, None, None] * norm + new_norm
        return ((state, norm), result)
    features = 1 + qk_width + qk_width * qk_width
    init = (jnp.zeros((row_count, head_count, features, value_width), jnp.float32), jnp.zeros((row_count, head_count, features), jnp.float32))
    blocks = (split_blocks(query), split_blocks(keys), split_blocks(values), jnp.arange(count, dtype=jnp.int32))
    results = lax.scan(jax.checkpoint(block_step), init, blocks)[1]
    return jnp.moveaxis(results, 0, 1).reshape(row_count, length, head_count, value_width)

def conv_local(start_pos, offsets, extended, kernel):
    tap_count = kernel.shape[0]
    length = extended.shape[1] - (tap_count - 1)
    position = start_pos + jnp.arange(length, dtype=jnp.int32)
    current = position[None, :] >= offsets[:, None]
    total = jnp.zeros((extended.shape[0], length, extended.shape[2]), jnp.float32)
    for shift_by in range(tap_count):
        source = position - shift_by
        valid = (source[None, :] >= 0) & ((source[None, :] >= offsets[:, None]) == current)
        piece = extended[:, tap_count - 1 - shift_by:tap_count - 1 - shift_by + length, :]
        total = total + kernel[shift_by][None, None, :] * piece * valid[:, :, None].astype(jnp.float32)
    return total

def mlp_block(resid, gain, gate_w, up_w, down_w):
    normed = low(rms_norm(resid, gain))
    gate_val = low_back(matmul(normed, gate_w))
    up_val = low_back(matmul(normed, up_w))
    hidden = low(jax.nn.silu(gate_val) * up_val)
    return resid + low_back(matmul(hidden, down_w))

def forward(offsets, inputs, attn_query, attn_key, attn_value, attn_output, ffn1_gate, ffn1_up, ffn1_down, conv_input, conv_gate, conv_output, conv_kernel, ffn2_gate, ffn2_up, ffn2_down, norm_gains):
    row_count, length, model_width = inputs.shape
    normed_a = low(rms_norm(inputs, norm_gains[0]))
    query = low_back(low(matmul(normed_a, attn_query))).reshape(row_count, length, HEADS, QK)
    keys = low_back(low(matmul(normed_a, attn_key))).reshape(row_count, length, HEADS, QK)
    values = low_back(low(matmul(normed_a, attn_value))).reshape(row_count, length, HEADS, VH)
    attended = linear_attention(query, keys, values, offsets).reshape(row_count, length, model_width)
    resid_one = inputs + low_back(matmul(low(attended), attn_output))
    resid_two = mlp_block(resid_one, norm_gains[1], ffn1_gate, ffn1_up, ffn1_down)
    normed_c = low(rms_norm(resid_two, norm_gains[2]))
    inner_val = low_back(matmul(normed_c, conv_input))
    gate_c = low_back(matmul(normed_c, conv_gate))
    tap_count = conv_kernel.shape[0]
    extended = jnp.pad(inner_val, ((0, 0), (tap_count - 1, 0), (0, 0)))
    mixed_conv = conv_local(0, offsets, extended, conv_kernel)
    resid_three = resid_two + low_back(matmul(low(mixed_conv * gate_c), conv_output))
    return mlp_block(resid_three, norm_gains[3], ffn2_gate, ffn2_up, ffn2_down)

def reference(activations, offsets, cotangent, attn_query, attn_key, attn_value, attn_output, ffn1_gate, ffn1_up, ffn1_down, conv_input, conv_gate, conv_output, conv_kernel, ffn2_gate, ffn2_up, ffn2_down, norm_gains):
    weights = tuple((item.astype(jnp.float32) for item in (attn_query, attn_key, attn_value, attn_output, ffn1_gate, ffn1_up, ffn1_down, conv_input, conv_gate, conv_output, conv_kernel, ffn2_gate, ffn2_up, ffn2_down, norm_gains)))
    outputs = []
    input_grads = []
    totals = None
    for batch_index in range(MICRO):
        inputs = activations[batch_index].astype(jnp.float32)
        result, pullback = jax.vjp(partial(forward, offsets[batch_index]), inputs, *weights)
        grads = pullback(cotangent[batch_index].astype(jnp.float32))
        outputs.append(result.astype(jnp.bfloat16))
        input_grads.append(grads[0])
        if totals is None:
            totals = grads[1:]
        else:
            totals = tuple((left + right for left, right in zip(totals, grads[1:])))
    return (jnp.stack(outputs), jnp.stack(input_grads), totals[0], totals[1], totals[2], totals[3], totals[4], totals[5], totals[6], totals[7], totals[8], totals[9], totals[10], totals[11], totals[12], totals[13], totals[14])
```

```python
from functools import partial

import jax
import jax.numpy as jnp
from jax import lax
from jax.experimental import pallas as pl
from jax.experimental.pallas import tpu as pltpu
from jax.sharding import PartitionSpec as P

QK = 16
VH = 112
EPSILON = 1e-05
BF = jnp.bfloat16
F32 = jnp.float32


def ring_order(n):
    if n % 4:
        return list(range(n))
    inner = n // 4
    if inner == 2:
        return [0, 2, 4, 6, 7, 5, 3, 1]
    return list(range(n))


class Ring:
    def __init__(self, n):
        self.n = n
        self.hops = n <= 8
        self.order = ring_order(n)
        place = [0] * n
        for position, device in enumerate(self.order):
            place[device] = position
        self.place = place
        self.pos = jnp.asarray(place, jnp.int32)[lax.axis_index("seq")] if self.hops else jnp.int32(0)

    def hop(self, block, step):
        n = self.n
        route = [(self.order[i], self.order[(i + step) % n]) for i in range(n)]
        return lax.ppermute(block, "seq", route)

    def owners(self):
        return jnp.asarray(self.order, jnp.int32)[(self.pos + jnp.arange(self.n)) % self.n]

    def to_relative(self, x):
        if not self.hops:
            return x
        width = x.shape[-1] // self.n
        parts = [x[..., b * width : (b + 1) * width] for b in self.order]
        twice = jnp.concatenate(parts + parts, axis=-1)
        return lax.dynamic_slice_in_dim(twice, self.pos * width, x.shape[-1], axis=x.ndim - 1)

    def from_relative(self, x):
        if not self.hops:
            return x
        width = x.shape[-1] // self.n
        twice = jnp.concatenate([x, x], axis=-1)
        start = ((self.n - self.pos) % self.n) * width
        ring = lax.dynamic_slice_in_dim(twice, start, x.shape[-1], axis=x.ndim - 1)
        parts = [ring[..., p * width : (p + 1) * width] for p in self.place]
        return jnp.concatenate(parts, axis=-1)

    def gather(self, arrays, after=None):
        n = self.n
        if not self.hops:
            whole = [lax.all_gather(a, "seq") for a in arrays]
            return [[w[k] for k in range(n)] for w in whole], None
        right = list(arrays)
        left = list(arrays)
        if after is not None:
            ties_r, ties_l = after
            for j in range(len(arrays)):
                right[j], _ = lax.optimization_barrier((arrays[j], ties_r[j % len(ties_r)]))
                left[j], _ = lax.optimization_barrier((arrays[j], ties_l[j % len(ties_l)]))
        blocks = [{0: a} for a in arrays]
        both = (n - 1) // 2
        for k in range(1, both + 1):
            for j in range(len(arrays)):
                right[j] = self.hop(right[j], 1)
                left[j] = self.hop(left[j], -1)
                blocks[j][n - k] = right[j]
                blocks[j][k] = left[j]
        ties = (list(right), list(left))
        if n % 2 == 0:
            for j in range(len(arrays)):
                blocks[j][n // 2] = self.hop(right[j], 1) if j % 2 == 0 else self.hop(left[j], -1)
        return [[b[k] for k in range(n)] for b in blocks], ties

    def scatter(self, full, flip):
        n = self.n
        height = full.shape[0] // n
        if not self.hops:
            return lax.psum_scatter(full, "seq", scatter_dimension=0, tiled=True).astype(F32)

        def term(k):
            return full[k * height : (k + 1) * height]

        direction = -1 if flip else 1
        long_hops, short_hops = n // 2, (n - 1) // 2
        total = term(0).astype(F32)
        for d, hops in ((direction, long_hops), (-direction, short_hops)):
            if hops == 0:
                continue
            acc = term((d * hops) % n)
            for k in range(hops - 1, -1, -1):
                acc = self.hop(acc, d)
                if k:
                    acc = (acc.astype(F32) + term((d * k) % n).astype(F32)).astype(BF)
            total = total + acc.astype(F32)
        return total


def dot(a, b, ca, cb):
    return lax.dot_general(a, b, (((ca,), (cb,)), ((), ())), preferred_element_type=F32)


def head_masks(query_width, value_width):
    lane_q = lax.broadcasted_iota(jnp.int32, (1, query_width), 1)
    lane_v = lax.broadcasted_iota(jnp.int32, (1, value_width), 1)
    heads = query_width // QK
    return [
        (
            (lane_q >= h * QK) & (lane_q < (h + 1) * QK),
            (lane_v >= h * VH) & (lane_v < (h + 1) * VH),
        )
        for h in range(heads)
    ]


def query_mask(scal_ref, place_ref, tok):
    offset = scal_ref[1 + pl.program_id(0)]
    pos = scal_ref[0] + lax.broadcasted_iota(jnp.int32, (tok, 1), 0)
    low = jnp.where(pos >= offset, offset, 0)
    other = place_ref[...]
    return (other >= low) & (other <= pos)


def key_mask(scal_ref, place_ref, tok):
    offset = scal_ref[1 + pl.program_id(0)]
    pos = scal_ref[0] + lax.broadcasted_iota(jnp.int32, (tok, 1), 0)
    high = jnp.where(pos >= offset, jnp.int32(1 << 30), offset)
    other = place_ref[...]
    return (other >= pos) & (other < high)


def attend_kernel(scal_ref, place_ref, q_ref, k_ref, v_ref, out_ref):
    q, k, v = q_ref[0], k_ref[0], v_ref[0]
    mask = query_mask(scal_ref, place_ref, q.shape[0])
    total = jnp.zeros((q.shape[0], v.shape[1]), F32)
    for in_q, in_v in head_masks(q.shape[1], v.shape[1]):
        s = dot(jnp.where(in_q, q, jnp.zeros_like(q)), k, 1, 1) * (QK**-0.5)
        w = jnp.where(mask, 1.0 + s + 0.5 * s * s, 0.0)
        den = jnp.sum(w, axis=1, keepdims=True)
        total = total + jnp.where(in_v, dot(w.astype(BF), v, 1, 0) / den, 0.0)
    out_ref[0] = total.astype(BF)


def query_back_kernel(scal_ref, place_ref, q_ref, k_ref, v_ref, da_ref, dq_ref, dan_ref, extra_ref):
    q, k, v = q_ref[0], k_ref[0], v_ref[0]
    da = da_ref[0]
    tok = q.shape[0]
    mask = query_mask(scal_ref, place_ref, tok)
    lane = lax.broadcasted_iota(jnp.int32, (1, q.shape[1]), 1)
    heads = q.shape[1] // QK
    dq = jnp.zeros(q.shape, F32)
    dan_all = jnp.zeros(da.shape, F32)
    extra = jnp.zeros(q.shape, F32)
    for h, (in_q, in_v) in enumerate(head_masks(q.shape[1], v.shape[1])):
        s = dot(jnp.where(in_q, q, jnp.zeros_like(q)), k, 1, 1) * (QK**-0.5)
        w = jnp.where(mask, 1.0 + s + 0.5 * s * s, 0.0)
        den = jnp.sum(w, axis=1, keepdims=True)
        att = dot(w.astype(BF), v, 1, 0) / den
        dan = jnp.where(in_v, da / den, 0.0).astype(BF)
        dan_f = dan.astype(F32)
        delta = jnp.sum(dan_f * att, axis=1, keepdims=True)
        d_kernel = dot(dan, v, 1, 1) - delta
        ds = jnp.where(mask, d_kernel * (1.0 + s), 0.0).astype(BF)
        dq = dq + jnp.where(in_q, dot(ds, k, 1, 0) * (QK**-0.5), 0.0)
        dan_all = dan_all + dan_f
        high = delta.astype(BF).astype(F32)
        extra = extra + jnp.where(lane == h, high, 0.0)
        extra = extra + jnp.where(lane == heads + h, delta - high, 0.0)
    dq_ref[0] = dq.astype(BF)
    dan_ref[0] = dan_all.astype(BF)
    extra_ref[0] = extra.astype(BF)


def key_back_kernel(scal_ref, place_ref, k_ref, v_ref, q_ref, dan_ref, extra_ref, dk_ref, dv_ref):
    k, v = k_ref[0], v_ref[0]
    q, dan, extra = q_ref[0], dan_ref[0], extra_ref[0]
    tok = k.shape[0]
    mask = key_mask(scal_ref, place_ref, tok)
    lane = lax.broadcasted_iota(jnp.int32, (tok, k.shape[1]), 1)
    heads = k.shape[1] // QK
    dk = jnp.zeros(k.shape, F32)
    dv = jnp.zeros(v.shape, F32)
    for h, (in_q, in_v) in enumerate(head_masks(k.shape[1], v.shape[1])):
        s = dot(jnp.where(in_q, k, jnp.zeros_like(k)), q, 1, 1) * (QK**-0.5)
        w = jnp.where(mask, 1.0 + s + 0.5 * s * s, 0.0).astype(BF)
        dv = dv + jnp.where(in_v, dot(w, dan, 1, 0), 0.0)
        pick = jnp.where((lane == h) | (lane == heads + h), 1.0, 0.0).astype(BF)
        d_kernel = dot(jnp.where(in_v, v, jnp.zeros_like(v)), dan, 1, 1) - dot(pick, extra, 1, 1)
        ds = jnp.where(mask, d_kernel * (1.0 + s), 0.0).astype(BF)
        dk = dk + jnp.where(in_q, dot(ds, q, 1, 0) * (QK**-0.5), 0.0)
    dk_ref[0] = dk.astype(BF)
    dv_ref[0] = dv.astype(BF)


def by_rows(kernel, scal, place, operands, widths, kinds):
    rows = operands[0].shape[0]
    tok = operands[0].shape[1]
    specs = [
        pl.BlockSpec(memory_space=pltpu.SMEM),
        pl.BlockSpec(place.shape, lambda r: (0, 0)),
    ]
    specs += [pl.BlockSpec((1,) + a.shape[1:], lambda r: (r, 0, 0)) for a in operands]
    return pl.pallas_call(
        kernel,
        grid=(rows,),
        in_specs=specs,
        out_specs=[pl.BlockSpec((1, tok, w), lambda r: (r, 0, 0)) for w in widths],
        out_shape=[jax.ShapeDtypeStruct((rows, tok, w), t) for w, t in zip(widths, kinds)],
        compiler_params=pltpu.CompilerParams(vmem_limit_bytes=48 * 1024 * 1024),
    )(scal, place, *operands)


def rms_scale(x):
    return lax.rsqrt(jnp.mean(x * x, axis=-1, keepdims=True) + EPSILON)


def rms_norm(x, gain):
    return x * rms_scale(x) * gain


def rms_back(x, gain, dn):
    scale = rms_scale(x)
    unit = x * scale
    gain_grad = jnp.sum(dn * unit, axis=0)
    dg = dn * gain
    dx = scale * (dg - unit * jnp.mean(dg * unit, axis=-1, keepdims=True))
    return dx, gain_grad


def head_total(partial_sum):
    return lax.psum(partial_sum.astype(BF), "head").astype(F32)


def mlp_forward(resid, gain, weights):
    gate_w, up_w, down_t = weights
    normed = rms_norm(resid, gain).astype(BF)
    gate_val = dot(normed, gate_w, 1, 0)
    up_val = dot(normed, up_w, 1, 0)
    hidden = (gate_val * jax.nn.sigmoid(gate_val) * up_val).astype(BF)
    result = resid + head_total(dot(hidden, down_t, 1, 1))
    return result, (normed, gate_val, up_val, hidden)


def mlp_backward(resid, grad_out, gain, saved, weights):
    gate_w, up_w, down_t = weights
    normed, gate_val, up_val, hidden = saved
    grad_b = grad_out.astype(BF)
    down_grad = dot(grad_b, hidden, 0, 0).astype(BF)
    dh = dot(grad_b, down_t, 1, 0)
    sig = jax.nn.sigmoid(gate_val)
    silu = gate_val * sig
    d_gate = (dh * up_val * (sig * (1.0 + gate_val * (1.0 - sig)))).astype(BF)
    d_up = (dh * silu).astype(BF)
    gate_grad = dot(normed, d_gate, 0, 0).astype(BF)
    up_grad = dot(normed, d_up, 0, 0).astype(BF)
    dn = head_total(dot(d_gate, gate_w, 1, 1) + dot(d_up, up_w, 1, 1))
    dx, gain_grad = rms_back(resid, gain, dn)
    return grad_out + dx, gain_grad, (gate_grad, up_grad, down_grad)


def shifted(block, before, shift):
    if shift == 0:
        return block
    return jnp.concatenate([before[:, before.shape[1] - shift :], block[:, :-shift]], axis=1)


def advanced(block, after, shift):
    if shift == 0:
        return block
    return jnp.concatenate([block[:, shift:], after[:, :shift]], axis=1)


def per_device(
    activations,
    offsets,
    cotangent,
    attn_query,
    attn_key,
    attn_value,
    attn_output,
    ffn1_gate,
    ffn1_up,
    ffn1_down,
    conv_input,
    conv_gate,
    conv_output,
    conv_kernel,
    ffn2_gate,
    ffn2_up,
    ffn2_down,
    norm_gains,
):
    n = lax.axis_size("seq")
    ring = Ring(n)
    micro, row_count, tok, width = activations.shape
    rows = micro * row_count
    count = rows * tok
    qw, vw = attn_query.shape[1], attn_value.shape[1]
    cw = conv_input.shape[1]
    taps = conv_kernel.shape[0]
    here = lax.axis_index("seq")
    start = here * tok
    off = offsets.reshape(rows)

    qkv_s = jnp.concatenate([attn_query, attn_key, attn_value], axis=1)
    groups = (
        (qkv_s, attn_output.T),
        (ffn1_gate, ffn1_up, ffn1_down.T),
        (conv_input, conv_gate, conv_output.T),
        (ffn2_gate, ffn2_up, ffn2_down.T),
    )
    gathered = []
    ties = None
    for group in groups:
        blocks, ties = ring.gather(list(group), ties)
        gathered.append([jnp.concatenate(b, axis=0) for b in blocks])
    (qkv_w, out_t), ffn1, (inner_w, gate_w, conv_out_t), ffn2 = gathered

    gains = ring.to_relative(norm_gains).astype(F32)
    kernel_f = conv_kernel.astype(F32)
    inputs = ring.to_relative(activations.reshape(count, width)).astype(F32)
    grad_four = ring.to_relative(cotangent.reshape(count, width)).astype(F32)

    scal = jnp.concatenate([start[None].astype(jnp.int32), off])
    place = (ring.owners()[:, None] * tok + jnp.arange(tok, dtype=jnp.int32)[None]).reshape(1, n * tok)
    normed_a = rms_norm(inputs, gains[0]).astype(BF)
    qkv = dot(normed_a, qkv_w, 1, 0).astype(BF)
    (qkv_blocks,), _ = ring.gather([qkv])
    qkv_all = jnp.concatenate([b.reshape(rows, tok, -1) for b in qkv_blocks], axis=1)
    own = qkv.reshape(rows, tok, -1)
    q_own, k_own, v_own = own[..., :qw], own[..., qw : 2 * qw], own[..., 2 * qw :]
    q_all, k_all, v_all = qkv_all[..., :qw], qkv_all[..., qw : 2 * qw], qkv_all[..., 2 * qw :]
    (mixed,) = by_rows(attend_kernel, scal, place, (q_own, k_all, v_all), (vw,), (BF,))
    mixed = mixed.reshape(count, vw)
    resid_one = inputs + head_total(dot(mixed, out_t, 1, 1))

    resid_two, kept_one = mlp_forward(resid_one, gains[1], ffn1)

    normed_c = rms_norm(resid_two, gains[2]).astype(BF)
    inner = dot(normed_c, inner_w, 1, 0).reshape(rows, tok, cw)
    gate_c = dot(normed_c, gate_w, 1, 0).reshape(rows, tok, cw)
    pos = start + jnp.arange(tok + taps - 1, dtype=jnp.int32)
    current = pos[None, :] >= off[:, None]

    def valid(t, first, length):
        p = pos[None, first : first + length]
        source = p - t
        same = (source >= off[:, None]) == current[:, first : first + length]
        return ((source >= 0) & same).astype(F32)[:, :, None]

    edge = lax.ppermute(inner[:, tok - (taps - 1) :], "seq", [(i, i + 1) for i in range(n - 1)])
    moved = [shifted(inner, edge, t) * valid(t, 0, tok) for t in range(taps)]
    conv = sum(kernel_f[t][None, None, :] * moved[t] for t in range(taps))
    product = (conv * gate_c).astype(BF).reshape(count, cw)
    resid_three = resid_two + head_total(dot(product, conv_out_t, 1, 1))

    resid_four, kept_two = mlp_forward(resid_three, gains[3], ffn2)
    block_output = ring.from_relative(resid_four.astype(BF)).reshape(activations.shape)

    grad_three, gain_four, grads_two = mlp_backward(resid_three, grad_four, gains[3], kept_two, ffn2)
    sums_two = [ring.scatter(g, i % 2 == 1) for i, g in enumerate(grads_two)]

    grad_b = grad_three.astype(BF)
    conv_out_grad = dot(grad_b, product, 0, 0).astype(BF)
    d_product = dot(grad_b, conv_out_t, 1, 0).reshape(rows, tok, cw)
    d_gate_c = (d_product * conv).astype(BF).reshape(count, cw)
    d_conv = d_product * gate_c
    next_rows = lax.ppermute(d_conv[:, : taps - 1], "seq", [(i + 1, i) for i in range(n - 1)])
    d_inner = sum(
        kernel_f[t][None, None, :] * advanced(d_conv, next_rows, t) * valid(t, t, tok)
        for t in range(taps)
    )
    d_inner = d_inner.astype(BF).reshape(count, cw)
    kernel_grad = jnp.stack([jnp.sum(d_conv * moved[t], axis=(0, 1)) for t in range(taps)])
    conv_in_grad = dot(normed_c, d_inner, 0, 0).astype(BF)
    conv_gate_grad = dot(normed_c, d_gate_c, 0, 0).astype(BF)
    dn = head_total(dot(d_inner, inner_w, 1, 1) + dot(d_gate_c, gate_w, 1, 1))
    dx, gain_three = rms_back(resid_two, gains[2], dn)
    grad_two = grad_three + dx
    sums_conv = [
        ring.scatter(g, i % 2 == 0) for i, g in enumerate((conv_in_grad, conv_gate_grad, conv_out_grad))
    ]

    grad_one, gain_two, grads_one = mlp_backward(resid_one, grad_two, gains[1], kept_one, ffn1)
    sums_one = [ring.scatter(g, i % 2 == 1) for i, g in enumerate(grads_one)]

    grad_b = grad_one.astype(BF)
    output_grad = dot(grad_b, mixed, 0, 0).astype(BF)
    da = dot(grad_b, out_t, 1, 0).reshape(rows, tok, vw)
    dq, dan, extra = by_rows(
        query_back_kernel, scal, place, (q_own, k_all, v_all, da), (qw, vw, qw), (BF, BF, BF)
    )
    back = jnp.concatenate([dan, extra], axis=-1).reshape(count, vw + qw)
    (back_blocks,), _ = ring.gather([back])
    back_all = jnp.concatenate([b.reshape(rows, tok, -1) for b in back_blocks], axis=1)
    dk, dv = by_rows(
        key_back_kernel,
        scal,
        place,
        (k_own, v_own, q_all, back_all[..., :vw], back_all[..., vw:]),
        (qw, vw),
        (BF, BF),
    )
    d_qkv = jnp.concatenate([dq, dk, dv], axis=-1).reshape(count, 2 * qw + vw)
    qkv_grad = dot(normed_a, d_qkv, 0, 0).astype(BF)
    dn = head_total(dot(d_qkv, qkv_w, 1, 1))
    dx, gain_one = rms_back(inputs, gains[0], dn)
    input_grad = ring.from_relative(grad_one + dx).reshape(activations.shape)
    sums_attn = [ring.scatter(g, i % 2 == 0) for i, g in enumerate((qkv_grad, output_grad))]

    gains_grad = ring.from_relative(jnp.stack([gain_one, gain_two, gain_three, gain_four]))
    gains_grad = lax.psum(gains_grad.astype(BF), "seq").astype(F32)
    kernel_grad = lax.psum(kernel_grad.astype(BF), "seq").astype(F32)
    return (
        block_output,
        input_grad,
        sums_attn[0][:, :qw],
        sums_attn[0][:, qw : 2 * qw],
        sums_attn[0][:, 2 * qw :],
        sums_attn[1].T,
        sums_one[0],
        sums_one[1],
        sums_one[2].T,
        sums_conv[0],
        sums_conv[1],
        sums_conv[2].T,
        kernel_grad,
        sums_two[0],
        sums_two[1],
        sums_two[2].T,
        gains_grad,
    )


def solution(mesh):
    rows_in = P("seq", "head")
    rows_out = P("head", "seq")
    tokens = P(None, None, "seq", None)
    in_specs = (
        (tokens, P(), tokens)
        + (rows_in, rows_in, rows_in, rows_out)
        + (rows_in, rows_in, rows_out)
        + (rows_in, rows_in, rows_out)
        + (P(None, "head"),)
        + (rows_in, rows_in, rows_out)
        + (P(),)
    )
    out_specs = (
        (tokens, tokens)
        + (rows_in, rows_in, rows_in, rows_out)
        + (rows_in, rows_in, rows_out)
        + (rows_in, rows_in, rows_out)
        + (P(None, "head"),)
        + (rows_in, rows_in, rows_out)
        + (P(),)
    )
    return jax.shard_map(
        per_device, mesh=mesh, in_specs=in_specs, out_specs=out_specs, check_vma=False
    )
```

```python
from functools import partial

import jax
import jax.numpy as jnp
from jax import lax
from jax.experimental import pallas as pl
from jax.experimental.pallas import tpu as pltpu
from jax.sharding import PartitionSpec as P

QK = 16
VH = 112
EPSILON = 1e-05
BF = jnp.bfloat16
F32 = jnp.float32


MESH = pl.DeviceIdType.MESH
ANY = pl.BlockSpec(memory_space=pl.ANY)


def ring_device(p):
    return jnp.where(p < 4, 2 * p, 15 - 2 * p)


def ring_position(s):
    return jnp.where(lax.rem(s, 2) == 0, s // 2, 7 - s // 2)


def ring_size(n):
    return n == 8


def greet(n):
    pos = ring_position(lax.axis_index("seq"))
    right = ring_device(lax.rem(pos + 1, n))
    left = ring_device(lax.rem(pos + n - 1, n))
    barrier = pltpu.get_barrier_semaphore()
    for neighbour in (left, right):
        pl.semaphore_signal(barrier, inc=1, device_id={"seq": neighbour}, device_id_type=MESH)
    pl.semaphore_wait(barrier, 2)
    return pos, right, left


class GatherRing:
    def __init__(self, n, where, src, out, send, recv, flip):
        self.n, self.src, self.out, self.send, self.recv = n, src, out, send, recv
        self.pos, self.right, self.left = where
        self.height = src.shape[0]
        self.started = []
        self.flip = flip
        self.steps = n // 2
        self.done = 0

    def rows(self, r):
        owner = ring_device(lax.rem(self.pos + (r % self.n), self.n))
        return pl.ds(pl.multiple_of(owner * self.height, 32), self.height)

    def copy(self, k, d):
        rows = self.rows(-d * (k - 1))
        i = 0 if d == 1 else 1
        return pltpu.make_async_remote_copy(
            src_ref=self.src if k == 1 else self.out.at[rows],
            dst_ref=self.out.at[rows],
            send_sem=self.send.at[i, k - 1],
            recv_sem=self.recv.at[i, k - 1],
            device_id={"seq": self.right if d == 1 else self.left},
            device_id_type=MESH,
        )

    def begin(self, local):
        self.own = pltpu.make_async_copy(self.src, self.out.at[self.rows(0)], local)
        self.own.start()

    def ways(self, k):
        if k <= (self.n - 1) // 2:
            return (1, -1)
        return (-1,) if self.flip else (1,)

    def step(self):
        if self.done == self.steps:
            return
        self.done += 1
        k = self.done
        for d in self.ways(k):
            if k > 1:
                self.copy(k - 1, d).wait_recv()
            self.copy(k, d).start()

    def finish(self):
        while self.done < self.steps:
            self.step()
        self.own.wait()
        last = {d: max(k for k in range(1, self.steps + 1) if d in self.ways(k)) for d in (1, -1)}
        for d in (1, -1):
            self.copy(last[d], d).wait_recv()
        for k in range(1, self.steps + 1):
            for d in self.ways(k):
                self.copy(k, d).wait_send()


def gather_kernel(n, flips, *refs):
    count = len(flips)
    srcs, outs, sems = refs[:count], refs[count : 2 * count], refs[2 * count :]
    send, recv, local = sems
    where = greet(n)
    rings = [
        GatherRing(n, where, srcs[j], outs[j], send.at[j], recv.at[j], flips[j]) for j in range(count)
    ]
    for j, ring in enumerate(rings):
        ring.begin(local.at[j])
    for _ in range(n // 2):
        for ring in rings:
            ring.step()
    for ring in rings:
        ring.finish()


def gather_all(arrays, call_id, flip=0):
    n = lax.axis_size("seq")
    if not ring_size(n):
        return [lax.all_gather(a, "seq", axis=0, tiled=True) for a in arrays]
    count = len(arrays)
    return pl.pallas_call(
        partial(gather_kernel, n, [(j + flip) % 2 == 1 for j in range(count)]),
        in_specs=[ANY] * count,
        out_specs=[ANY] * count,
        out_shape=[jax.ShapeDtypeStruct((n * a.shape[0], a.shape[1]), a.dtype) for a in arrays],
        scratch_shapes=[
            pltpu.SemaphoreType.DMA((count, 2, n // 2)),
            pltpu.SemaphoreType.DMA((count, 2, n // 2)),
            pltpu.SemaphoreType.DMA((count,)),
        ],
        compiler_params=pltpu.CompilerParams(collective_id=call_id, has_side_effects=True),
    )(*arrays)


class ScatterRing:
    def __init__(self, n, where, full, out, terms, slots, send, recv, load, flip):
        self.n, self.full, self.out, self.terms, self.slots = n, full, out, terms, slots
        self.send, self.recv, self.load = send, recv, load
        self.pos, self.right, self.left = where
        self.height = out.shape[0]
        d = -1 if flip else 1
        self.hops = {d: n // 2, -d: (n - 1) // 2}
        self.order = (d, -d)
        self.done = 0
        self.steps = n // 2

    def source(self, r):
        owner = ring_device(lax.rem(self.pos + (r % self.n), self.n))
        return self.full.at[pl.ds(pl.multiple_of(owner * self.height, 32), self.height)]

    def term(self, d, h):
        r = d * (self.hops[d] - h)
        return pltpu.make_async_copy(self.source(r), self.terms.at[r % self.n], self.load.at[r % self.n])

    def copy(self, d, h):
        i = 0 if d == 1 else 1
        r = d * (self.hops[d] - h + 1)
        return pltpu.make_async_remote_copy(
            src_ref=self.source(r) if h == 1 else self.terms.at[r % self.n],
            dst_ref=self.slots.at[i, h - 1],
            send_sem=self.send.at[i, h - 1],
            recv_sem=self.recv.at[i, h - 1],
            device_id={"seq": self.right if d == 1 else self.left},
            device_id_type=MESH,
        )

    def step(self):
        if self.done == self.steps:
            return
        self.done += 1
        h = self.done
        for d in self.order:
            if h > self.hops[d]:
                continue
            if h > 1:
                self.copy(d, h - 1).wait_recv()
                self.term(d, h - 1).wait()
                i, r = (0 if d == 1 else 1), (d * (self.hops[d] - h + 1)) % self.n
                total = self.slots[i, h - 2].astype(F32) + self.terms[r].astype(F32)
                self.terms[r] = total.astype(BF)
            self.copy(d, h).start()
            if h < self.hops[d]:
                self.term(d, h).start()
        if h == 1:
            self.own = pltpu.make_async_copy(self.source(0), self.terms.at[0], self.load.at[0])
            self.own.start()

    def finish(self):
        while self.done < self.steps:
            self.step()
        self.own.wait()
        total = self.terms[0].astype(F32)
        for d in self.order:
            i, h = (0 if d == 1 else 1), self.hops[d]
            self.copy(d, h).wait_recv()
            total = total + self.slots[i, h - 1].astype(F32)
        self.out[...] = total
        for d in self.order:
            for h in range(1, self.hops[d] + 1):
                self.copy(d, h).wait_send()


def scatter_kernel(n, flips, *refs):
    count = len(flips)
    fulls, outs, rest = refs[:count], refs[count : 2 * count], refs[2 * count :]
    terms, slots, (send, recv, load) = rest[:count], rest[count : 2 * count], rest[2 * count :]
    where = greet(n)
    rings = [
        ScatterRing(
            n, where, fulls[j], outs[j], terms[j], slots[j], send.at[j], recv.at[j], load.at[j], flips[j]
        )
        for j in range(count)
    ]
    for _ in range(n // 2):
        for ring in rings:
            ring.step()
    for ring in rings:
        ring.finish()


def scatter_all(fulls, call_id, flip=0):
    n = lax.axis_size("seq")
    if not ring_size(n):
        return [
            lax.psum_scatter(g, "seq", scatter_dimension=0, tiled=True).astype(F32) for g in fulls
        ]
    count = len(fulls)
    blocks = [(g.shape[0] // n, g.shape[1]) for g in fulls]
    return pl.pallas_call(
        partial(scatter_kernel, n, [(j + flip) % 2 == 1 for j in range(count)]),
        in_specs=[ANY] * count,
        out_specs=[pl.BlockSpec(memory_space=pltpu.VMEM)] * count,
        out_shape=[jax.ShapeDtypeStruct(b, F32) for b in blocks],
        scratch_shapes=[pltpu.VMEM((n,) + b, BF) for b in blocks]
        + [pltpu.VMEM((2, n // 2) + b, BF) for b in blocks]
        + [
            pltpu.SemaphoreType.DMA((count, 2, n // 2)),
            pltpu.SemaphoreType.DMA((count, 2, n // 2)),
            pltpu.SemaphoreType.DMA((count, n)),
        ],
        compiler_params=pltpu.CompilerParams(
            collective_id=call_id, has_side_effects=True, vmem_limit_bytes=56 * 1024 * 1024
        ),
    )(*fulls)


def small_sum(x, axis):
    size = lax.axis_size(axis)
    if size > 8:
        return lax.psum(x.astype(BF), axis).astype(F32)
    sent = x.astype(BF)
    routes = [[(i, (i + k) % size) for i in range(size)] for k in range(1, size)]
    return x + sum(lax.ppermute(sent, axis, r).astype(F32) for r in routes)


def dot(a, b, ca, cb):
    return lax.dot_general(a, b, (((ca,), (cb,)), ((), ())), preferred_element_type=F32)


def head_masks(query_width, value_width):
    lane_q = lax.broadcasted_iota(jnp.int32, (1, query_width), 1)
    lane_v = lax.broadcasted_iota(jnp.int32, (1, value_width), 1)
    heads = query_width // QK
    return [
        (
            (lane_q >= h * QK) & (lane_q < (h + 1) * QK),
            (lane_v >= h * VH) & (lane_v < (h + 1) * VH),
        )
        for h in range(heads)
    ]


def query_mask(scal_ref, place_ref, tok):
    offset = scal_ref[1 + pl.program_id(0)]
    pos = scal_ref[0] + lax.broadcasted_iota(jnp.int32, (tok, 1), 0)
    low = jnp.where(pos >= offset, offset, 0)
    other = place_ref[...]
    return (other >= low) & (other <= pos)


def key_mask(scal_ref, place_ref, tok):
    offset = scal_ref[1 + pl.program_id(0)]
    pos = scal_ref[0] + lax.broadcasted_iota(jnp.int32, (tok, 1), 0)
    high = jnp.where(pos >= offset, jnp.int32(1 << 30), offset)
    other = place_ref[...]
    return (other >= pos) & (other < high)


def attend_kernel(scal_ref, place_ref, q_ref, k_ref, v_ref, out_ref):
    q, k, v = q_ref[0], k_ref[0], v_ref[0]
    mask = query_mask(scal_ref, place_ref, q.shape[0])
    total = jnp.zeros((q.shape[0], v.shape[1]), F32)
    for in_q, in_v in head_masks(q.shape[1], v.shape[1]):
        s = dot(jnp.where(in_q, q, jnp.zeros_like(q)), k, 1, 1) * (QK**-0.5)
        w = jnp.where(mask, 1.0 + s + 0.5 * s * s, 0.0)
        den = jnp.sum(w, axis=1, keepdims=True)
        total = total + jnp.where(in_v, dot(w.astype(BF), v, 1, 0) / den, 0.0)
    out_ref[0] = total.astype(BF)


def query_back_kernel(scal_ref, place_ref, q_ref, k_ref, v_ref, da_ref, dq_ref, dan_ref, extra_ref):
    q, k, v = q_ref[0], k_ref[0], v_ref[0]
    da = da_ref[0]
    tok = q.shape[0]
    mask = query_mask(scal_ref, place_ref, tok)
    lane = lax.broadcasted_iota(jnp.int32, (1, q.shape[1]), 1)
    heads = q.shape[1] // QK
    dq = jnp.zeros(q.shape, F32)
    dan_all = jnp.zeros(da.shape, F32)
    extra = jnp.zeros(q.shape, F32)
    for h, (in_q, in_v) in enumerate(head_masks(q.shape[1], v.shape[1])):
        s = dot(jnp.where(in_q, q, jnp.zeros_like(q)), k, 1, 1) * (QK**-0.5)
        w = jnp.where(mask, 1.0 + s + 0.5 * s * s, 0.0)
        den = jnp.sum(w, axis=1, keepdims=True)
        att = dot(w.astype(BF), v, 1, 0) / den
        dan = jnp.where(in_v, da / den, 0.0).astype(BF)
        dan_f = dan.astype(F32)
        delta = jnp.sum(dan_f * att, axis=1, keepdims=True)
        d_kernel = dot(dan, v, 1, 1) - delta
        ds = jnp.where(mask, d_kernel * (1.0 + s), 0.0).astype(BF)
        dq = dq + jnp.where(in_q, dot(ds, k, 1, 0) * (QK**-0.5), 0.0)
        dan_all = dan_all + dan_f
        high = delta.astype(BF).astype(F32)
        extra = extra + jnp.where(lane == h, high, 0.0)
        extra = extra + jnp.where(lane == heads + h, delta - high, 0.0)
    dq_ref[0] = dq.astype(BF)
    dan_ref[0] = dan_all.astype(BF)
    extra_ref[0] = extra.astype(BF)


def key_back_kernel(scal_ref, place_ref, k_ref, v_ref, q_ref, dan_ref, extra_ref, dk_ref, dv_ref):
    k, v = k_ref[0], v_ref[0]
    q, dan, extra = q_ref[0], dan_ref[0], extra_ref[0]
    tok = k.shape[0]
    mask = key_mask(scal_ref, place_ref, tok)
    lane = lax.broadcasted_iota(jnp.int32, (tok, k.shape[1]), 1)
    heads = k.shape[1] // QK
    dk = jnp.zeros(k.shape, F32)
    dv = jnp.zeros(v.shape, F32)
    for h, (in_q, in_v) in enumerate(head_masks(k.shape[1], v.shape[1])):
        s = dot(jnp.where(in_q, k, jnp.zeros_like(k)), q, 1, 1) * (QK**-0.5)
        w = jnp.where(mask, 1.0 + s + 0.5 * s * s, 0.0).astype(BF)
        dv = dv + jnp.where(in_v, dot(w, dan, 1, 0), 0.0)
        pick = jnp.where((lane == h) | (lane == heads + h), 1.0, 0.0).astype(BF)
        d_kernel = dot(jnp.where(in_v, v, jnp.zeros_like(v)), dan, 1, 1) - dot(pick, extra, 1, 1)
        ds = jnp.where(mask, d_kernel * (1.0 + s), 0.0).astype(BF)
        dk = dk + jnp.where(in_q, dot(ds, q, 1, 0) * (QK**-0.5), 0.0)
    dk_ref[0] = dk.astype(BF)
    dv_ref[0] = dv.astype(BF)


def by_rows(kernel, scal, place, operands, widths, kinds):
    rows = operands[0].shape[0]
    tok = operands[0].shape[1]
    specs = [
        pl.BlockSpec(memory_space=pltpu.SMEM),
        pl.BlockSpec(place.shape, lambda r: (0, 0)),
    ]
    specs += [pl.BlockSpec((1,) + a.shape[1:], lambda r: (r, 0, 0)) for a in operands]
    return pl.pallas_call(
        kernel,
        grid=(rows,),
        in_specs=specs,
        out_specs=[pl.BlockSpec((1, tok, w), lambda r: (r, 0, 0)) for w in widths],
        out_shape=[jax.ShapeDtypeStruct((rows, tok, w), t) for w, t in zip(widths, kinds)],
        compiler_params=pltpu.CompilerParams(vmem_limit_bytes=48 * 1024 * 1024),
    )(scal, place, *operands)


def rms_scale(x):
    return lax.rsqrt(jnp.mean(x * x, axis=-1, keepdims=True) + EPSILON)


def rms_norm(x, gain):
    return x * rms_scale(x) * gain


def rms_back(x, gain, dn):
    scale = rms_scale(x)
    unit = x * scale
    gain_grad = jnp.sum(dn * unit, axis=0)
    dg = dn * gain
    dx = scale * (dg - unit * jnp.mean(dg * unit, axis=-1, keepdims=True))
    return dx, gain_grad


def head_total(partial_sum):
    return lax.psum(partial_sum, "head").astype(F32)


def tie(xs, *others):
    return list(lax.optimization_barrier((tuple(xs), tuple(others)))[0])


def mlp_forward(resid, gain, weights):
    gate_w, up_w, down_t = weights
    normed = rms_norm(resid, gain).astype(BF)
    gate_val = dot(normed, gate_w, 1, 0)
    up_val = dot(normed, up_w, 1, 0)
    hidden = (gate_val * jax.nn.sigmoid(gate_val) * up_val).astype(BF)
    return dot(hidden, down_t, 1, 1).astype(BF), (normed, gate_val, up_val, hidden)


def mlp_backward(grad_b, saved, weights):
    gate_w, up_w, down_t = weights
    normed, gate_val, up_val, hidden = saved
    dh = dot(grad_b, down_t, 1, 0)
    sig = jax.nn.sigmoid(gate_val)
    silu = gate_val * sig
    d_gate = (dh * up_val * (sig * (1.0 + gate_val * (1.0 - sig)))).astype(BF)
    d_up = (dh * silu).astype(BF)
    dn_part = (dot(d_gate, gate_w, 1, 1) + dot(d_up, up_w, 1, 1)).astype(BF)
    gate_grad = dot(normed, d_gate, 0, 0).astype(BF)
    up_grad = dot(normed, d_up, 0, 0).astype(BF)
    down_grad = dot(grad_b, hidden, 0, 0).astype(BF)
    return dn_part, (gate_grad, up_grad, down_grad)


def shifted(block, before, shift):
    if shift == 0:
        return block
    return jnp.concatenate([before[:, before.shape[1] - shift :], block[:, :-shift]], axis=1)


def advanced(block, after, shift):
    if shift == 0:
        return block
    return jnp.concatenate([block[:, shift:], after[:, :shift]], axis=1)


def per_device(
    activations,
    offsets,
    cotangent,
    attn_query,
    attn_key,
    attn_value,
    attn_output,
    ffn1_gate,
    ffn1_up,
    ffn1_down,
    conv_input,
    conv_gate,
    conv_output,
    conv_kernel,
    ffn2_gate,
    ffn2_up,
    ffn2_down,
    norm_gains,
):
    n = lax.axis_size("seq")
    micro, row_count, tok, width = activations.shape
    rows = micro * row_count
    count = rows * tok
    qw, vw = attn_query.shape[1], attn_value.shape[1]
    cw = conv_input.shape[1]
    taps = conv_kernel.shape[0]
    here = lax.axis_index("seq")
    start = here * tok
    off = offsets.reshape(rows)

    qkv_s = jnp.concatenate([attn_query, attn_key, attn_value], axis=1)
    gains = norm_gains.astype(F32)
    kernel_f = conv_kernel.astype(F32)
    inputs = activations.reshape(count, width).astype(F32)
    grad_four = cotangent.reshape(count, width)
    qkv_w, out_t = gather_all([qkv_s, attn_output.T], 1)

    scal = jnp.concatenate([start[None].astype(jnp.int32), off])
    place = jnp.arange(n * tok, dtype=jnp.int32).reshape(1, n * tok)
    normed_a = rms_norm(inputs, gains[0]).astype(BF)
    qkv = dot(normed_a, qkv_w, 1, 0).astype(BF)

    def by_sequence(blocks):
        return jnp.swapaxes(blocks.reshape(n, rows, tok, -1), 0, 1).reshape(rows, n * tok, -1)

    qkv_all = by_sequence(gather_all([qkv], 2)[0])
    own = qkv.reshape(rows, tok, -1)
    q_own, k_own, v_own = own[..., :qw], own[..., qw : 2 * qw], own[..., 2 * qw :]
    q_all, k_all, v_all = qkv_all[..., :qw], qkv_all[..., qw : 2 * qw], qkv_all[..., 2 * qw :]
    (mixed,) = by_rows(attend_kernel, scal, place, (q_own, k_all, v_all), (vw,), (BF,))
    mixed = mixed.reshape(count, vw)
    attn_part = dot(mixed, out_t, 1, 1).astype(BF)
    attn_sum = head_total(attn_part)
    ffn1 = gather_all(tie((ffn1_gate, ffn1_up, ffn1_down.T), attn_part), 3)
    resid_one = inputs + attn_sum
    part, kept_one = mlp_forward(resid_one, gains[1], ffn1)
    ffn1_sum = head_total(part)
    inner_w, gate_w, conv_out_t = gather_all(
        tie((conv_input, conv_gate, conv_output.T), part), 4, 1
    )
    resid_two = resid_one + ffn1_sum

    normed_c = rms_norm(resid_two, gains[2]).astype(BF)
    inner = dot(normed_c, inner_w, 1, 0).reshape(rows, tok, cw)
    gate_c = dot(normed_c, gate_w, 1, 0).reshape(rows, tok, cw)
    pos = start + jnp.arange(tok + taps - 1, dtype=jnp.int32)
    current = pos[None, :] >= off[:, None]

    def valid(t, first, length):
        p = pos[None, first : first + length]
        source = p - t
        same = (source >= off[:, None]) == current[:, first : first + length]
        return ((source >= 0) & same).astype(F32)[:, :, None]

    edge = lax.ppermute(inner[:, tok - (taps - 1) :], "seq", [(i, i + 1) for i in range(n - 1)])
    moved = [shifted(inner, edge, t) * valid(t, 0, tok) for t in range(taps)]
    conv = sum(kernel_f[t][None, None, :] * moved[t] for t in range(taps))
    product = (conv * gate_c).astype(BF).reshape(count, cw)
    conv_part = dot(product, conv_out_t, 1, 1).astype(BF)
    conv_sum = head_total(conv_part)
    ffn2 = gather_all(tie((ffn2_gate, ffn2_up, ffn2_down.T), conv_part), 3)
    resid_three = resid_two + conv_sum
    out_part, kept_two = mlp_forward(resid_three, gains[3], ffn2)

    dn_part, grads_two = mlp_backward(grad_four, kept_two, ffn2)
    dn = head_total(dn_part)
    sums_two = scatter_all(tie(grads_two, dn_part), 5)
    (dn,) = tie((dn,), *sums_two)
    out_sum = head_total(tie((out_part,), *sums_two)[0])
    block_output = (resid_three + out_sum).astype(BF).reshape(activations.shape)
    dx, gain_four = rms_back(resid_three, gains[3], dn)
    grad_three = grad_four.astype(F32) + dx
    grad_b = grad_three.astype(BF)
    conv_out_grad = dot(grad_b, product, 0, 0).astype(BF)
    d_product = dot(grad_b, conv_out_t, 1, 0).reshape(rows, tok, cw)
    d_gate_c = (d_product * conv).astype(BF).reshape(count, cw)
    d_conv = d_product * gate_c
    next_rows = lax.ppermute(d_conv[:, : taps - 1], "seq", [(i + 1, i) for i in range(n - 1)])
    d_inner = sum(
        kernel_f[t][None, None, :] * advanced(d_conv, next_rows, t) * valid(t, t, tok)
        for t in range(taps)
    )
    d_inner = d_inner.astype(BF).reshape(count, cw)
    kernel_grad = jnp.stack([jnp.sum(d_conv * moved[t], axis=(0, 1)) for t in range(taps)])
    conv_in_grad = dot(normed_c, d_inner, 0, 0).astype(BF)
    conv_gate_grad = dot(normed_c, d_gate_c, 0, 0).astype(BF)
    dn_part = (dot(d_inner, inner_w, 1, 1) + dot(d_gate_c, gate_w, 1, 1)).astype(BF)
    dn = head_total(dn_part)
    sums_conv = scatter_all(tie((conv_in_grad, conv_gate_grad, conv_out_grad), dn_part), 6, 1)
    (dn,) = tie((dn,), *sums_conv)
    dx, gain_three = rms_back(resid_two, gains[2], dn)
    grad_two = grad_three + dx
    dn_part, grads_one = mlp_backward(grad_two.astype(BF), kept_one, ffn1)
    dn = head_total(dn_part)
    sums_one = scatter_all(tie(grads_one, dn_part), 5)
    (dn,) = tie((dn,), *sums_one)
    dx, gain_two = rms_back(resid_one, gains[1], dn)
    grad_one = grad_two + dx

    grad_b = grad_one.astype(BF)
    output_grad = dot(grad_b, mixed, 0, 0).astype(BF)
    da = dot(grad_b, out_t, 1, 0).reshape(rows, tok, vw)
    dq, dan, extra = by_rows(
        query_back_kernel, scal, place, (q_own, k_all, v_all, da), (qw, vw, qw), (BF, BF, BF)
    )
    back = jnp.concatenate([dan, extra], axis=-1).reshape(count, vw + qw)
    back_all = by_sequence(gather_all([back], 7, 1)[0])
    dk, dv = by_rows(
        key_back_kernel,
        scal,
        place,
        (k_own, v_own, q_all, back_all[..., :vw], back_all[..., vw:]),
        (qw, vw),
        (BF, BF),
    )
    d_qkv = jnp.concatenate([dq, dk, dv], axis=-1).reshape(count, 2 * qw + vw)
    qkv_grad = dot(normed_a, d_qkv, 0, 0).astype(BF)
    dn_part = dot(d_qkv, qkv_w, 1, 1).astype(BF)
    dn = head_total(dn_part)
    sums_attn = scatter_all(tie((qkv_grad, output_grad), dn_part), 8)
    (dn,) = tie((dn,), *sums_attn)
    unit = inputs * rms_scale(inputs)
    gain_one = jnp.sum(dn_part.astype(F32) * unit, axis=0)
    gain_one = small_sum(gain_one, "head")
    dx, _ = rms_back(inputs, gains[0], dn)
    input_grad = (grad_one + dx).reshape(activations.shape)

    gains_grad = small_sum(jnp.stack([gain_one, gain_two, gain_three, gain_four]), "seq")
    kernel_grad = small_sum(kernel_grad, "seq")
    return (
        block_output,
        input_grad,
        sums_attn[0][:, :qw],
        sums_attn[0][:, qw : 2 * qw],
        sums_attn[0][:, 2 * qw :],
        sums_attn[1].T,
        sums_one[0],
        sums_one[1],
        sums_one[2].T,
        sums_conv[0],
        sums_conv[1],
        sums_conv[2].T,
        kernel_grad,
        sums_two[0],
        sums_two[1],
        sums_two[2].T,
        gains_grad,
    )


def solution(mesh):
    rows_in = P("seq", "head")
    rows_out = P("head", "seq")
    tokens = P(None, None, "seq", None)
    in_specs = (
        (tokens, P(), tokens)
        + (rows_in, rows_in, rows_in, rows_out)
        + (rows_in, rows_in, rows_out)
        + (rows_in, rows_in, rows_out)
        + (P(None, "head"),)
        + (rows_in, rows_in, rows_out)
        + (P(),)
    )
    out_specs = (
        (tokens, tokens)
        + (rows_in, rows_in, rows_in, rows_out)
        + (rows_in, rows_in, rows_out)
        + (rows_in, rows_in, rows_out)
        + (P(None, "head"),)
        + (rows_in, rows_in, rows_out)
        + (P(),)
    )
    return jax.shard_map(
        per_device, mesh=mesh, in_specs=in_specs, out_specs=out_specs, check_vma=False
    )
```

```python
from functools import partial

import jax
import jax.numpy as jnp
from jax import lax
from jax.experimental import pallas as pl
from jax.experimental.pallas import tpu as pltpu
from jax.sharding import PartitionSpec as P

QK = 16
VH = 112
EPSILON = 1e-05
BF = jnp.bfloat16
F32 = jnp.float32


MESH = pl.DeviceIdType.MESH
ANY = pl.BlockSpec(memory_space=pl.ANY)


def ring_device(p):
    return jnp.where(p < 4, 2 * p, 15 - 2 * p)


def ring_position(s):
    return jnp.where(lax.rem(s, 2) == 0, s // 2, 7 - s // 2)


def ring_size(n):
    return n == 8


def greet(n):
    pos = ring_position(lax.axis_index("seq"))
    right = ring_device(lax.rem(pos + 1, n))
    left = ring_device(lax.rem(pos + n - 1, n))
    barrier = pltpu.get_barrier_semaphore()
    for neighbour in (left, right):
        pl.semaphore_signal(barrier, inc=1, device_id={"seq": neighbour}, device_id_type=MESH)
    pl.semaphore_wait(barrier, 2)
    return pos, right, left


class GatherRing:
    def __init__(self, n, where, src, out, place, send, recv, local, flip):
        self.n, self.src, self.out, self.place = n, src, out, place
        self.send, self.recv, self.local = send, recv, local
        self.pos, self.right, self.left = where
        self.flip = flip
        self.steps = n // 2
        self.done = 0

    def block(self, r):
        return self.place(self.out, ring_device(lax.rem(self.pos + (r % self.n), self.n)))

    def copy(self, k, d):
        block = self.block(-d * (k - 1))
        i = 0 if d == 1 else 1
        return pltpu.make_async_remote_copy(
            src_ref=self.src if k == 1 else block,
            dst_ref=block,
            send_sem=self.send.at[i, k - 1],
            recv_sem=self.recv.at[i, k - 1],
            device_id={"seq": self.right if d == 1 else self.left},
            device_id_type=MESH,
        )

    def ways(self, k):
        if k <= (self.n - 1) // 2:
            return (1, -1)
        return (-1,) if self.flip else (1,)

    def step(self):
        if self.done == self.steps:
            return
        if self.done == 0:
            pltpu.make_async_copy(self.src, self.block(0), self.local).start()
        self.done += 1
        k = self.done
        for d in self.ways(k):
            if k > 1:
                self.copy(k - 1, d).wait_recv()
            self.copy(k, d).start()

    def finish(self):
        while self.done < self.steps:
            self.step()
        pltpu.make_async_copy(self.src, self.block(0), self.local).wait()
        last = {d: max(k for k in range(1, self.steps + 1) if d in self.ways(k)) for d in (1, -1)}
        for d in (1, -1):
            self.copy(last[d], d).wait_recv()
        for k in range(1, self.steps + 1):
            for d in self.ways(k):
                self.copy(k, d).wait_send()


def by_block(height):
    return lambda ref, owner: ref.at[pl.ds(pl.multiple_of(owner * height, min(height, 32)), height)]


def by_position(tok):
    return lambda ref, owner: ref.at[:, pl.ds(pl.multiple_of(owner * tok, 16), tok)]


VMEM = pltpu.VMEM
MIB = 1024 * 1024


class Call:
    def __init__(self, call_id):
        self.n = lax.axis_size("seq")
        self.call_id = call_id
        self.ins, self.outs, self.scratch = {}, {}, {}
        self.gathers, self.scatters = {}, {}

    def take(self, name, array, space=VMEM):
        self.ins[name] = (array, pl.BlockSpec(memory_space=space))
        return name

    def give(self, name, shape, kind, space=VMEM):
        self.outs[name] = (jax.ShapeDtypeStruct(shape, kind), pl.BlockSpec(memory_space=space))
        return name

    def hold(self, name, shape, kind):
        self.scratch[name] = VMEM(shape, kind)
        return name

    def sems(self, name, *shape):
        self.scratch[name] = pltpu.SemaphoreType.DMA(shape)

    def gather(self, name, src, out, place, flip=False):
        half = self.n // 2
        self.sems(name + ".send", 2, half)
        self.sems(name + ".recv", 2, half)
        self.sems(name + ".local", 1)
        self.gathers[name] = (src, out, place, flip)

    def left(self, name, array):
        self.take(name, array)
        rows, width = array.shape
        self.hold(name + ".blocked", (self.n, rows, width // self.n), BF)

    def scatter(self, name, left, right, flip=False):
        n = self.n
        height = self.ins[left][0].shape[1] // n
        block = (height, right.shape[1])
        self.take(name + ".right", right)
        self.give(name, block, F32)
        self.hold(name + ".sums", (2, n // 2) + block, BF)
        self.hold(name + ".slots", (2, n // 2) + block, BF)
        self.sems(name + ".send", 2, n // 2)
        self.sems(name + ".recv", 2, n // 2)
        self.scatters[name] = (left, flip)

    def kernel(self, body, *refs):
        names = list(self.ins) + list(self.outs) + list(self.scratch)
        at = dict(zip(names, refs))
        where = greet(self.n)
        rings = {}
        for name, (src, out, place, flip) in self.gathers.items():
            rings[name] = GatherRing(
                self.n,
                where,
                at[src],
                at[out],
                place,
                at[name + ".send"],
                at[name + ".recv"],
                at[name + ".local"].at[0],
                flip,
            )
        ready = set()
        for name, (left, flip) in self.scatters.items():
            blocked = at[left + ".blocked"]
            if left not in ready:
                ready.add(left)
                width = blocked.shape[2]
                for b in range(self.n):
                    blocked[b] = at[left][:, b * width : (b + 1) * width]
            rings[name] = ScatterRing(
                self.n,
                where,
                blocked,
                at[name + ".right"],
                at[name],
                at[name + ".sums"],
                at[name + ".slots"],
                at[name + ".send"],
                at[name + ".recv"],
                flip,
            )
            rings[name].step()
        body(at, rings)
        for ring in rings.values():
            ring.finish()

    def run(self, body):
        outs = pl.pallas_call(
            partial(self.kernel, body),
            in_specs=[spec for _, spec in self.ins.values()],
            out_specs=[spec for _, spec in self.outs.values()],
            out_shape=[shape for shape, _ in self.outs.values()],
            scratch_shapes=list(self.scratch.values()),
            compiler_params=pltpu.CompilerParams(
                collective_id=self.call_id, has_side_effects=True, vmem_limit_bytes=58 * MIB
            ),
        )(*[array for array, _ in self.ins.values()])
        return dict(zip(self.outs, outs))


def in_turn(n):
    def body(at, rings):
        for _ in range(n // 2):
            for ring in rings.values():
                ring.step()

    return body


def gather_all(arrays, call_id, flip=0):
    n = lax.axis_size("seq")
    if not ring_size(n):
        return [lax.all_gather(a, "seq", axis=0, tiled=True) for a in arrays]
    call = Call(call_id)
    names = [str(j) for j in range(len(arrays))]
    for j, (name, a) in enumerate(zip(names, arrays)):
        call.take(name + ".src", a, pl.ANY)
        call.give(name, (n * a.shape[0],) + a.shape[1:], a.dtype, pl.ANY)
        call.gather(name, name + ".src", name, by_block(a.shape[0]), (j + flip) % 2 == 1)
    out = call.run(in_turn(n))
    return [out[name] for name in names]


class ScatterRing:
    def __init__(self, n, where, left, right, out, sums, slots, send, recv, flip):
        self.n, self.left_ref, self.right_ref, self.out = n, left, right, out
        self.sums, self.slots, self.send, self.recv = sums, slots, send, recv
        self.pos, self.right, self.left = where
        d = -1 if flip else 1
        self.hops = {d: n // 2, -d: (n - 1) // 2}
        self.order = (d, -d)
        self.done = 0
        self.steps = n // 2

    def term(self, r):
        owner = ring_device(lax.rem(self.pos + (r % self.n), self.n))
        return dot(self.left_ref[owner], self.right_ref[...], 0, 0)

    def copy(self, d, h):
        i = 0 if d == 1 else 1
        return pltpu.make_async_remote_copy(
            src_ref=self.sums.at[i, h - 1],
            dst_ref=self.slots.at[i, h - 1],
            send_sem=self.send.at[i, h - 1],
            recv_sem=self.recv.at[i, h - 1],
            device_id={"seq": self.right if d == 1 else self.left},
            device_id_type=MESH,
        )

    def step(self):
        if self.done == self.steps:
            return
        self.done += 1
        h = self.done
        for d in self.order:
            if h > self.hops[d]:
                continue
            i = 0 if d == 1 else 1
            total = self.term(d * (self.hops[d] - h + 1))
            if h > 1:
                self.copy(d, h - 1).wait_recv()
                total = total + self.slots[i, h - 2].astype(F32)
            self.sums[i, h - 1] = total.astype(BF)
            self.copy(d, h).start()

    def finish(self):
        while self.done < self.steps:
            self.step()
        total = self.term(0)
        for d in self.order:
            i, h = (0 if d == 1 else 1), self.hops[d]
            self.copy(d, h).wait_recv()
            total = total + self.slots[i, h - 1].astype(F32)
        self.out[...] = total
        for d in self.order:
            for h in range(1, self.hops[d] + 1):
                self.copy(d, h).wait_send()


def scatter_all(lefts, pairs, call_id, flip=0, small=None):
    n = lax.axis_size("seq")
    if not ring_size(n):
        sums = [
            lax.psum_scatter(
                dot(lefts[i], right, 0, 0).astype(BF), "seq", scatter_dimension=0, tiled=True
            ).astype(F32)
            for i, right in pairs
        ]
        return sums if small is None else sums + [lax.psum(small.astype(BF), "seq").astype(F32)]
    call = Call(call_id)
    names = [str(j) for j in range(len(pairs))]
    if small is not None:
        call.take("small.src", small)
        call.hold("small.all", (n * small.shape[0], small.shape[1]), F32)
        call.gather("small", "small.src", "small.all", by_block(small.shape[0]))
    for i, a in enumerate(lefts):
        call.left(f"left{i}", a)
    for j, (i, right) in enumerate(pairs):
        call.scatter(names[j], f"left{i}", right, (j + flip) % 2 == 1)
    if small is not None:
        names.append(call.give("small.sum", small.shape, F32))

    def body(at, rings):
        in_turn(n)(at, rings)
        if small is not None:
            rings["small"].finish()
            rows = small.shape[0]
            blocks = [at["small.all"][b * rows : (b + 1) * rows] for b in range(n)]
            at["small.sum"][...] = sum(blocks[1:], blocks[0])
            del rings["small"]

    out = call.run(body)
    return [out[name] for name in names]


def small_sum(x, axis):
    size = lax.axis_size(axis)
    if size > 8:
        return lax.psum(x.astype(BF), axis).astype(F32)
    sent = x.astype(BF)
    routes = [[(i, (i + k) % size) for i in range(size)] for k in range(1, size)]
    return x + sum(lax.ppermute(sent, axis, r).astype(F32) for r in routes)


def dot(a, b, ca, cb):
    return lax.dot_general(a, b, (((ca,), (cb,)), ((), ())), preferred_element_type=F32)


def head_masks(query_width, value_width):
    lane_q = lax.broadcasted_iota(jnp.int32, (1, query_width), 1)
    lane_v = lax.broadcasted_iota(jnp.int32, (1, value_width), 1)
    heads = query_width // QK
    return [
        (
            (lane_q >= h * QK) & (lane_q < (h + 1) * QK),
            (lane_v >= h * VH) & (lane_v < (h + 1) * VH),
        )
        for h in range(heads)
    ]


def query_mask(scal_ref, place_ref, tok, row):
    offset = scal_ref[1 + row]
    pos = scal_ref[0] + lax.broadcasted_iota(jnp.int32, (tok, 1), 0)
    low = jnp.where(pos >= offset, offset, 0)
    other = place_ref[...]
    return (other >= low) & (other <= pos)


def key_mask(scal_ref, place_ref, tok, row):
    offset = scal_ref[1 + row]
    pos = scal_ref[0] + lax.broadcasted_iota(jnp.int32, (tok, 1), 0)
    high = jnp.where(pos >= offset, jnp.int32(1 << 30), offset)
    other = place_ref[...]
    return (other >= pos) & (other < high)


def attend_kernel(scal_ref, place_ref, q_ref, k_ref, v_ref, out_ref):
    q, k, v = q_ref[0], k_ref[0], v_ref[0]
    mask = query_mask(scal_ref, place_ref, q.shape[0], pl.program_id(0))
    total = jnp.zeros((q.shape[0], v.shape[1]), F32)
    for in_q, in_v in head_masks(q.shape[1], v.shape[1]):
        s = dot(jnp.where(in_q, q, jnp.zeros_like(q)), k, 1, 1) * (QK**-0.5)
        w = jnp.where(mask, 1.0 + s + 0.5 * s * s, 0.0)
        den = jnp.sum(w, axis=1, keepdims=True)
        total = total + jnp.where(in_v, dot(w.astype(BF), v, 1, 0) / den, 0.0)
    out_ref[0] = total.astype(BF)


def query_back_kernel(scal_ref, place_ref, q_ref, k_ref, v_ref, da_ref, dq_ref, dan_ref, extra_ref):
    q, k, v = q_ref[0], k_ref[0], v_ref[0]
    da = da_ref[0]
    tok = q.shape[0]
    mask = query_mask(scal_ref, place_ref, tok, pl.program_id(0))
    lane = lax.broadcasted_iota(jnp.int32, (1, q.shape[1]), 1)
    heads = q.shape[1] // QK
    dq = jnp.zeros(q.shape, F32)
    dan_all = jnp.zeros(da.shape, F32)
    extra = jnp.zeros(q.shape, F32)
    for h, (in_q, in_v) in enumerate(head_masks(q.shape[1], v.shape[1])):
        s = dot(jnp.where(in_q, q, jnp.zeros_like(q)), k, 1, 1) * (QK**-0.5)
        w = jnp.where(mask, 1.0 + s + 0.5 * s * s, 0.0)
        den = jnp.sum(w, axis=1, keepdims=True)
        att = dot(w.astype(BF), v, 1, 0) / den
        dan = jnp.where(in_v, da / den, 0.0).astype(BF)
        dan_f = dan.astype(F32)
        delta = jnp.sum(dan_f * att, axis=1, keepdims=True)
        d_kernel = dot(dan, v, 1, 1) - delta
        ds = jnp.where(mask, d_kernel * (1.0 + s), 0.0).astype(BF)
        dq = dq + jnp.where(in_q, dot(ds, k, 1, 0) * (QK**-0.5), 0.0)
        dan_all = dan_all + dan_f
        high = delta.astype(BF).astype(F32)
        extra = extra + jnp.where(lane == h, high, 0.0)
        extra = extra + jnp.where(lane == heads + h, delta - high, 0.0)
    dq_ref[0] = dq.astype(BF)
    dan_ref[0] = dan_all.astype(BF)
    extra_ref[0] = extra.astype(BF)


def key_back_kernel(scal_ref, place_ref, k_ref, v_ref, q_ref, dan_ref, extra_ref, dk_ref, dv_ref):
    k, v = k_ref[0], v_ref[0]
    q, dan, extra = q_ref[0], dan_ref[0], extra_ref[0]
    tok = k.shape[0]
    mask = key_mask(scal_ref, place_ref, tok, pl.program_id(0))
    lane = lax.broadcasted_iota(jnp.int32, (tok, k.shape[1]), 1)
    heads = k.shape[1] // QK
    dk = jnp.zeros(k.shape, F32)
    dv = jnp.zeros(v.shape, F32)
    for h, (in_q, in_v) in enumerate(head_masks(k.shape[1], v.shape[1])):
        s = dot(jnp.where(in_q, k, jnp.zeros_like(k)), q, 1, 1) * (QK**-0.5)
        w = jnp.where(mask, 1.0 + s + 0.5 * s * s, 0.0).astype(BF)
        dv = dv + jnp.where(in_v, dot(w, dan, 1, 0), 0.0)
        pick = jnp.where((lane == h) | (lane == heads + h), 1.0, 0.0).astype(BF)
        d_kernel = dot(jnp.where(in_v, v, jnp.zeros_like(v)), dan, 1, 1) - dot(pick, extra, 1, 1)
        ds = jnp.where(mask, d_kernel * (1.0 + s), 0.0).astype(BF)
        dk = dk + jnp.where(in_q, dot(ds, q, 1, 0) * (QK**-0.5), 0.0)
    dk_ref[0] = dk.astype(BF)
    dv_ref[0] = dv.astype(BF)


def attend_back(scal, place, q, k, v, qkv_all, da, scatters, call_id):
    n = lax.axis_size("seq")
    rows, tok, vw = v.shape
    qkw = q.shape[-1]
    call = Call(call_id)
    call.take("scal", scal, pltpu.SMEM)
    for name, a in (("place", place), ("q", q), ("k", k), ("v", v), ("all", qkv_all), ("da", da)):
        call.take(name, a)
    lefts, pairs = scatters
    for i, a in enumerate(lefts):
        call.left(f"left{i}", a)
    for j, (i, right) in enumerate(pairs):
        call.scatter(f"s{j}", f"left{i}", right, j % 2 == 1)
    call.give("dqk", (rows, tok, qkw), BF)
    call.give("dv", (rows, tok, vw), BF)
    call.hold("dq", (rows, tok, qkw), F32)
    call.hold("back", (rows, tok, qkw + vw), BF)
    call.hold("back_all", (rows, n * tok, qkw + vw), BF)
    call.gather("g", "back", "back_all", by_position(tok), True)
    heads = qkw // 2 // QK

    def body(at, rings):
        lane = lax.broadcasted_iota(jnp.int32, (1, qkw), 1)
        masks = head_masks(qkw // 2, vw)
        far = [(lane >= qkw // 2 + h * QK) & (lane < qkw // 2 + (h + 1) * QK) for h in range(heads)]
        near = [(lane >= h * QK) & (lane < (h + 1) * QK) for h in range(heads)]

        def query_side(r, carry):
            q, da = at["q"][r], at["da"][r]
            qk, v = at["all"][r, :, :qkw], at["all"][r, :, qkw:]
            mask = query_mask(at["scal"], at["place"], tok, r)
            dq = jnp.zeros((tok, qkw), F32)
            dan_all = jnp.zeros((tok, vw), F32)
            extra = jnp.zeros((tok, qkw), F32)
            for h in range(heads):
                in_v = masks[h][1]
                s = dot(jnp.where(far[h], q, jnp.zeros_like(q)), qk, 1, 1) * (QK**-0.5)
                w = jnp.where(mask, 1.0 + s + 0.5 * s * s, 0.0)
                den = jnp.sum(w, axis=1, keepdims=True)
                att = dot(w.astype(BF), v, 1, 0) / den
                dan = jnp.where(in_v, da / den, 0.0).astype(BF)
                dan_f = dan.astype(F32)
                delta = jnp.sum(dan_f * att, axis=1, keepdims=True)
                ds = jnp.where(mask, (dot(dan, v, 1, 1) - delta) * (1.0 + s), 0.0).astype(BF)
                dq = dq + jnp.where(far[h], dot(ds, qk, 1, 0) * (QK**-0.5), 0.0)
                dan_all = dan_all + dan_f
                high = delta.astype(BF).astype(F32)
                extra = extra + jnp.where(lane == h, high, 0.0)
                extra = extra + jnp.where(lane == heads + h, delta - high, 0.0)
            at["dq"][r] = dq
            at["back"][r, :, :qkw] = extra.astype(BF)
            at["back"][r, :, qkw:] = dan_all.astype(BF)
            return carry

        def key_side(r, carry):
            k, v = at["k"][r], at["v"][r]
            qk = at["all"][r, :, :qkw]
            extra, dan = at["back_all"][r, :, :qkw], at["back_all"][r, :, qkw:]
            mask = key_mask(at["scal"], at["place"], tok, r)
            wide = lax.broadcasted_iota(jnp.int32, (tok, qkw), 1)
            dqk = at["dq"][r]
            dv = jnp.zeros((tok, vw), F32)
            for h in range(heads):
                in_v = masks[h][1]
                s = dot(jnp.where(near[h], k, jnp.zeros_like(k)), qk, 1, 1) * (QK**-0.5)
                w = jnp.where(mask, 1.0 + s + 0.5 * s * s, 0.0).astype(BF)
                dv = dv + jnp.where(in_v, dot(w, dan, 1, 0), 0.0)
                pick = jnp.where((wide == h) | (wide == heads + h), 1.0, 0.0).astype(BF)
                d_kernel = dot(jnp.where(in_v, v, jnp.zeros_like(v)), dan, 1, 1) - dot(pick, extra, 1, 1)
                ds = jnp.where(mask, d_kernel * (1.0 + s), 0.0).astype(BF)
                dqk = dqk + jnp.where(near[h], dot(ds, qk, 1, 0) * (QK**-0.5), 0.0)
            at["dqk"][r] = dqk.astype(BF)
            at["dv"][r] = dv.astype(BF)
            return carry

        lax.fori_loop(0, rows, query_side, 0)
        others = [ring for name, ring in rings.items() if name != "g"]
        for _ in range(n // 2):
            rings["g"].step()
            for ring in others:
                ring.step()
        rings["g"].finish()
        del rings["g"]
        lax.fori_loop(0, rows, key_side, 0)

    out = call.run(body)
    return out["dqk"], out["dv"], [out[f"s{j}"] for j in range(len(pairs))]


def by_rows(kernel, scal, place, operands, widths, kinds):
    rows = operands[0].shape[0]
    tok = operands[0].shape[1]
    specs = [
        pl.BlockSpec(memory_space=pltpu.SMEM),
        pl.BlockSpec(place.shape, lambda r: (0, 0)),
    ]
    specs += [pl.BlockSpec((1,) + a.shape[1:], lambda r: (r, 0, 0)) for a in operands]
    return pl.pallas_call(
        kernel,
        grid=(rows,),
        in_specs=specs,
        out_specs=[pl.BlockSpec((1, tok, w), lambda r: (r, 0, 0)) for w in widths],
        out_shape=[jax.ShapeDtypeStruct((rows, tok, w), t) for w, t in zip(widths, kinds)],
        compiler_params=pltpu.CompilerParams(vmem_limit_bytes=48 * 1024 * 1024),
    )(scal, place, *operands)


def rms_scale(x):
    return lax.rsqrt(jnp.mean(x * x, axis=-1, keepdims=True) + EPSILON)


def rms_norm(x, gain):
    return x * rms_scale(x) * gain


def rms_back(x, gain, dn):
    scale = rms_scale(x)
    unit = x * scale
    gain_grad = jnp.sum(dn * unit, axis=0)
    dg = dn * gain
    dx = scale * (dg - unit * jnp.mean(dg * unit, axis=-1, keepdims=True))
    return dx, gain_grad


def head_total(partial_sum):
    return lax.psum(partial_sum, "head").astype(F32)


def tie(xs, *others):
    return list(lax.optimization_barrier((tuple(xs), tuple(others)))[0])


def mlp_forward(resid, gain, weights):
    gate_w, up_w, down_t = weights
    normed = rms_norm(resid, gain).astype(BF)
    gate_val = dot(normed, gate_w, 1, 0)
    up_val = dot(normed, up_w, 1, 0)
    hidden = (gate_val * jax.nn.sigmoid(gate_val) * up_val).astype(BF)
    return dot(hidden, down_t, 1, 1).astype(BF), (normed, gate_val, up_val, hidden)


def mlp_scatter(kept, call_id, *others):
    (normed, grad_b), d_gate, d_up, hidden = kept
    normed, grad_b = tie((normed, grad_b), *others)
    return scatter_all((normed, grad_b), ((0, d_gate), (0, d_up), (1, hidden)), call_id)


def mlp_backward(grad_b, saved, weights):
    gate_w, up_w, down_t = weights
    normed, gate_val, up_val, hidden = saved
    dh = dot(grad_b, down_t, 1, 0)
    sig = jax.nn.sigmoid(gate_val)
    silu = gate_val * sig
    d_gate = (dh * up_val * (sig * (1.0 + gate_val * (1.0 - sig)))).astype(BF)
    d_up = (dh * silu).astype(BF)
    dn_part = (dot(d_gate, gate_w, 1, 1) + dot(d_up, up_w, 1, 1)).astype(BF)
    return dn_part, ((normed, grad_b), d_gate, d_up, hidden)


def shifted(block, before, shift):
    if shift == 0:
        return block
    return jnp.concatenate([before[:, before.shape[1] - shift :], block[:, :-shift]], axis=1)


def advanced(block, after, shift):
    if shift == 0:
        return block
    return jnp.concatenate([block[:, shift:], after[:, :shift]], axis=1)


def per_device(
    activations,
    offsets,
    cotangent,
    attn_query,
    attn_key,
    attn_value,
    attn_output,
    ffn1_gate,
    ffn1_up,
    ffn1_down,
    conv_input,
    conv_gate,
    conv_output,
    conv_kernel,
    ffn2_gate,
    ffn2_up,
    ffn2_down,
    norm_gains,
):
    n = lax.axis_size("seq")
    micro, row_count, tok, width = activations.shape
    rows = micro * row_count
    count = rows * tok
    qw, vw = attn_query.shape[1], attn_value.shape[1]
    cw = conv_input.shape[1]
    taps = conv_kernel.shape[0]
    here = lax.axis_index("seq")
    start = here * tok
    off = offsets.reshape(rows)

    qkv_s = jnp.concatenate([attn_query, attn_key, attn_value], axis=1)
    gains = norm_gains.astype(F32)
    kernel_f = conv_kernel.astype(F32)
    inputs = activations.reshape(count, width).astype(F32)
    grad_four = cotangent.reshape(count, width)
    qkv_w, out_t = gather_all([qkv_s, attn_output.T], 1)

    scal = jnp.concatenate([start[None].astype(jnp.int32), off])
    place = jnp.arange(n * tok, dtype=jnp.int32).reshape(1, n * tok)
    normed_a = rms_norm(inputs, gains[0]).astype(BF)
    qkv = dot(normed_a, qkv_w, 1, 0).astype(BF)

    def by_sequence(blocks):
        return jnp.swapaxes(blocks.reshape(n, rows, tok, -1), 0, 1).reshape(rows, n * tok, -1)

    qkv_all = by_sequence(gather_all([qkv], 2)[0])
    own = qkv.reshape(rows, tok, -1)
    q_own, k_own, v_own = own[..., :qw], own[..., qw : 2 * qw], own[..., 2 * qw :]
    q_all, k_all, v_all = qkv_all[..., :qw], qkv_all[..., qw : 2 * qw], qkv_all[..., 2 * qw :]
    (mixed,) = by_rows(attend_kernel, scal, place, (q_own, k_all, v_all), (vw,), (BF,))
    mixed = mixed.reshape(count, vw)
    attn_part = dot(mixed, out_t, 1, 1).astype(BF)
    attn_sum = head_total(attn_part)
    ffn1 = gather_all(tie((ffn1_gate, ffn1_up, ffn1_down.T), attn_part), 3)
    resid_one = inputs + attn_sum
    part, kept_one = mlp_forward(resid_one, gains[1], ffn1)
    ffn1_sum = head_total(part)
    inner_w, gate_w, conv_out_t = gather_all(
        tie((conv_input, conv_gate, conv_output.T), part), 4, 1
    )
    resid_two = resid_one + ffn1_sum

    normed_c = rms_norm(resid_two, gains[2]).astype(BF)
    inner = dot(normed_c, inner_w, 1, 0).reshape(rows, tok, cw)
    gate_c = dot(normed_c, gate_w, 1, 0).reshape(rows, tok, cw)
    pos = start + jnp.arange(tok + taps - 1, dtype=jnp.int32)
    current = pos[None, :] >= off[:, None]

    def valid(t, first, length):
        p = pos[None, first : first + length]
        source = p - t
        same = (source >= off[:, None]) == current[:, first : first + length]
        return ((source >= 0) & same).astype(F32)[:, :, None]

    edge = lax.ppermute(inner[:, tok - (taps - 1) :], "seq", [(i, i + 1) for i in range(n - 1)])
    moved = [shifted(inner, edge, t) * valid(t, 0, tok) for t in range(taps)]
    conv = sum(kernel_f[t][None, None, :] * moved[t] for t in range(taps))
    product = (conv * gate_c).astype(BF).reshape(count, cw)
    conv_part = dot(product, conv_out_t, 1, 1).astype(BF)
    conv_sum = head_total(conv_part)
    ffn2 = gather_all(tie((ffn2_gate, ffn2_up, ffn2_down.T), conv_part), 3)
    resid_three = resid_two + conv_sum
    out_part, kept_two = mlp_forward(resid_three, gains[3], ffn2)

    dn_part, grads_two = mlp_backward(grad_four, kept_two, ffn2)
    dn = head_total(dn_part)
    sums_two = mlp_scatter(grads_two, 5, dn_part)
    (dn,) = tie((dn,), *sums_two)
    out_sum = head_total(tie((out_part,), *sums_two)[0])
    block_output = (resid_three + out_sum).astype(BF).reshape(activations.shape)
    dx, gain_four = rms_back(resid_three, gains[3], dn)
    grad_three = grad_four.astype(F32) + dx
    grad_b = grad_three.astype(BF)
    d_product = dot(grad_b, conv_out_t, 1, 0).reshape(rows, tok, cw)
    d_gate_c = (d_product * conv).astype(BF).reshape(count, cw)
    d_conv = d_product * gate_c
    next_rows = lax.ppermute(d_conv[:, : taps - 1], "seq", [(i + 1, i) for i in range(n - 1)])
    d_inner = sum(
        kernel_f[t][None, None, :] * advanced(d_conv, next_rows, t) * valid(t, t, tok)
        for t in range(taps)
    )
    d_inner = d_inner.astype(BF).reshape(count, cw)
    kernel_grad = jnp.stack([jnp.sum(d_conv * moved[t], axis=(0, 1)) for t in range(taps)])
    dn_part = (dot(d_inner, inner_w, 1, 1) + dot(d_gate_c, gate_w, 1, 1)).astype(BF)
    dn = head_total(dn_part)
    sums_conv = scatter_all(
        tie((normed_c, grad_b), dn_part), ((0, d_inner), (0, d_gate_c), (1, product)), 6, 1
    )
    (dn,) = tie((dn,), *sums_conv)
    dx, gain_three = rms_back(resid_two, gains[2], dn)
    grad_two = grad_three + dx
    dn_part, grads_one = mlp_backward(grad_two.astype(BF), kept_one, ffn1)
    dn = head_total(dn_part)
    (normed_1, grad_b1), d_gate_1, d_up_1, hidden_1 = grads_one
    if ring_size(n):
        sums_one = scatter_all(tie((normed_1,), dn_part), ((0, d_gate_1),), 9)
        (dn,) = tie((dn,), *sums_one)
    dx, gain_two = rms_back(resid_one, gains[1], dn)
    grad_one = grad_two + dx

    grad_b = grad_one.astype(BF)
    da = dot(grad_b, out_t, 1, 0).reshape(rows, tok, vw)
    later = ((normed_1, grad_b1), ((0, d_up_1), (1, hidden_1)))
    if ring_size(n):
        blank = jnp.zeros_like(q_own)
        d_kq, d_v, more = attend_back(
            scal,
            place,
            jnp.concatenate([blank, q_own], axis=-1),
            jnp.concatenate([k_own, blank], axis=-1),
            v_own,
            qkv_all,
            da,
            later,
            7,
        )
        sums_one = sums_one + more
        d_kq = d_kq.reshape(count, 2 * qw)
    else:
        dq, dan, extra = by_rows(
            query_back_kernel, scal, place, (q_own, k_all, v_all, da), (qw, vw, qw), (BF, BF, BF)
        )
        back = jnp.concatenate([dan, extra], axis=-1).reshape(count, vw + qw)
        back_all = by_sequence(gather_all([back], 7, 1)[0])
        dk, d_v = by_rows(
            key_back_kernel,
            scal,
            place,
            (k_own, v_own, q_all, back_all[..., :vw], back_all[..., vw:]),
            (qw, vw),
            (BF, BF),
        )
        sums_one = scatter_all((normed_1,), ((0, d_gate_1),), 9) + scatter_all(*later, 10)
        d_kq = jnp.concatenate([dk, dq], axis=-1).reshape(count, 2 * qw)
    d_v = d_v.reshape(count, vw)
    d_all = jnp.concatenate([d_kq, d_v], axis=-1)
    kqv_w = jnp.concatenate([qkv_w[:, qw : 2 * qw], qkv_w[:, :qw], qkv_w[:, 2 * qw :]], axis=1)
    dn_part = dot(d_all, kqv_w, 1, 1).astype(BF)
    dn = head_total(dn_part)
    unit = inputs * rms_scale(inputs)
    gain_one = small_sum(jnp.sum(dn_part.astype(F32) * unit, axis=0), "head")
    small = jnp.concatenate(
        [
            jnp.stack([gain_one, gain_two, gain_three, gain_four]),
            jnp.pad(kernel_grad, ((0, 0), (0, width - cw))),
            jnp.zeros((8 - 4 - taps, width), F32),
        ]
    )
    sums_attn = scatter_all(
        tie((normed_a, grad_b), dn_part), ((0, d_kq), (0, d_v), (1, mixed)), 8, 0, small
    )
    gains_grad, kernel_grad = sums_attn[3][:4], sums_attn[3][4 : 4 + taps, :cw]
    (dn,) = tie((dn,), *sums_attn)
    dx, _ = rms_back(inputs, gains[0], dn)
    input_grad = (grad_one + dx).reshape(activations.shape)

    return (
        block_output,
        input_grad,
        sums_attn[0][:, qw:],
        sums_attn[0][:, :qw],
        sums_attn[1],
        sums_attn[2].T,
        sums_one[0],
        sums_one[1],
        sums_one[2].T,
        sums_conv[0],
        sums_conv[1],
        sums_conv[2].T,
        kernel_grad,
        sums_two[0],
        sums_two[1],
        sums_two[2].T,
        gains_grad,
    )


def solution(mesh):
    rows_in = P("seq", "head")
    rows_out = P("head", "seq")
    tokens = P(None, None, "seq", None)
    in_specs = (
        (tokens, P(), tokens)
        + (rows_in, rows_in, rows_in, rows_out)
        + (rows_in, rows_in, rows_out)
        + (rows_in, rows_in, rows_out)
        + (P(None, "head"),)
        + (rows_in, rows_in, rows_out)
        + (P(),)
    )
    out_specs = (
        (tokens, tokens)
        + (rows_in, rows_in, rows_in, rows_out)
        + (rows_in, rows_in, rows_out)
        + (rows_in, rows_in, rows_out)
        + (P(None, "head"),)
        + (rows_in, rows_in, rows_out)
        + (P(),)
    )
    return jax.shard_map(
        per_device, mesh=mesh, in_specs=in_specs, out_specs=out_specs, check_vma=False
    )
```

```python
from functools import partial

import jax
import jax.numpy as jnp
from jax import lax
from jax.experimental import pallas as pl
from jax.experimental.pallas import tpu as pltpu
from jax.sharding import PartitionSpec as P

QK = 16
VH = 112
EPSILON = 1e-05
BF = jnp.bfloat16
F32 = jnp.float32


MESH = pl.DeviceIdType.MESH
ANY = pl.BlockSpec(memory_space=pl.ANY)


def ring_device(p):
    return jnp.where(p < 4, 2 * p, 15 - 2 * p)


def ring_position(s):
    return jnp.where(lax.rem(s, 2) == 0, s // 2, 7 - s // 2)


def ring_size(n):
    return n == 8


def greet(n, everyone=False):
    me = lax.axis_index("seq")
    pos = ring_position(me)
    right = ring_device(lax.rem(pos + 1, n))
    left = ring_device(lax.rem(pos + n - 1, n))
    barrier = pltpu.get_barrier_semaphore()
    partners = [lax.rem(me + k, n) for k in range(1, n)] if everyone else [left, right]
    for partner in partners:
        pl.semaphore_signal(barrier, inc=1, device_id={"seq": partner}, device_id_type=MESH)
    pl.semaphore_wait(barrier, len(partners))
    return pos, right, left


class GatherRing:
    def __init__(self, n, where, src, out, place, send, recv, local, flip):
        self.n, self.src, self.out, self.place = n, src, out, place
        self.send, self.recv, self.local = send, recv, local
        self.pos, self.right, self.left = where
        self.flip = flip
        self.steps = n // 2
        self.done = 0

    def block(self, r):
        return self.place(self.out, ring_device(lax.rem(self.pos + (r % self.n), self.n)))

    def copy(self, k, d):
        block = self.block(-d * (k - 1))
        i = 0 if d == 1 else 1
        return pltpu.make_async_remote_copy(
            src_ref=self.src if k == 1 else block,
            dst_ref=block,
            send_sem=self.send.at[i, k - 1],
            recv_sem=self.recv.at[i, k - 1],
            device_id={"seq": self.right if d == 1 else self.left},
            device_id_type=MESH,
        )

    def ways(self, k):
        if k <= (self.n - 1) // 2:
            return (1, -1)
        return (-1,) if self.flip else (1,)

    def step(self):
        if self.done == self.steps:
            return
        if self.done == 0:
            pltpu.make_async_copy(self.src, self.block(0), self.local).start()
        self.done += 1
        k = self.done
        for d in self.ways(k):
            if k > 1:
                self.copy(k - 1, d).wait_recv()
            self.copy(k, d).start()

    def finish(self):
        while self.done < self.steps:
            self.step()
        pltpu.make_async_copy(self.src, self.block(0), self.local).wait()
        last = {d: max(k for k in range(1, self.steps + 1) if d in self.ways(k)) for d in (1, -1)}
        for d in (1, -1):
            self.copy(last[d], d).wait_recv()
        for k in range(1, self.steps + 1):
            for d in self.ways(k):
                self.copy(k, d).wait_send()


def by_block(height):
    return lambda ref, owner: ref.at[pl.ds(pl.multiple_of(owner * height, min(height, 32)), height)]


def by_position(tok):
    return lambda ref, owner: ref.at[:, pl.ds(pl.multiple_of(owner * tok, 16), tok)]


VMEM = pltpu.VMEM
MIB = 1024 * 1024


class Call:
    def __init__(self, call_id):
        self.n = lax.axis_size("seq")
        self.call_id = call_id
        self.ins, self.outs, self.scratch = {}, {}, {}
        self.gathers, self.scatters = {}, {}
        self.exchanges = []

    def exchange(self, name):
        self.sems(name + ".send", self.n)
        self.sems(name + ".recv", self.n)
        self.exchanges.append(name)

    def take(self, name, array, space=VMEM):
        self.ins[name] = (array, pl.BlockSpec(memory_space=space))
        return name

    def give(self, name, shape, kind, space=VMEM):
        self.outs[name] = (jax.ShapeDtypeStruct(shape, kind), pl.BlockSpec(memory_space=space))
        return name

    def hold(self, name, shape, kind):
        self.scratch[name] = VMEM(shape, kind)
        return name

    def sems(self, name, *shape):
        self.scratch[name] = pltpu.SemaphoreType.DMA(shape)

    def gather(self, name, src, out, place, flip=False):
        half = self.n // 2
        self.sems(name + ".send", 2, half)
        self.sems(name + ".recv", 2, half)
        self.sems(name + ".local", 1)
        self.gathers[name] = (src, out, place, flip)

    def left(self, name, array):
        self.take(name, array)
        rows, width = array.shape
        self.hold(name + ".blocked", (self.n, rows, width // self.n), BF)

    def scatter(self, name, left, right, flip=False, axis=0):
        n = self.n
        height = self.ins[left][0].shape[1] // n
        block = (height, right.shape[1 - axis])
        self.take(name + ".right", right)
        self.give(name, block, F32)
        self.hold(name + ".sums", (2, n // 2) + block, BF)
        self.hold(name + ".slots", (2, n // 2) + block, BF)
        self.sems(name + ".send", 2, n // 2)
        self.sems(name + ".recv", 2, n // 2)
        self.scatters[name] = (left, flip, axis)

    def kernel(self, body, *refs):
        names = list(self.ins) + list(self.outs) + list(self.scratch)
        at = dict(zip(names, refs))
        where = greet(self.n, bool(self.exchanges))
        rings = {}
        if self.early is not None:
            self.early(at)
        for name, (src, out, place, flip) in self.gathers.items():
            rings[name] = GatherRing(
                self.n,
                where,
                at[src],
                at[out],
                place,
                at[name + ".send"],
                at[name + ".recv"],
                at[name + ".local"].at[0],
                flip,
            )
        ready = set()
        for name, (left, flip, axis) in self.scatters.items():
            blocked = at[left + ".blocked"]
            if left not in ready:
                ready.add(left)
                width = blocked.shape[2]
                for b in range(self.n):
                    blocked[b] = at[left][:, b * width : (b + 1) * width]
            rings[name] = ScatterRing(
                self.n,
                where,
                blocked,
                at[name + ".right"],
                at[name],
                at[name + ".sums"],
                at[name + ".slots"],
                at[name + ".send"],
                at[name + ".recv"],
                flip,
                axis,
            )
            rings[name].step()
        body(at, rings)
        for ring in rings.values():
            ring.finish()

    early = None

    def run(self, body, early=None):
        self.early = early
        outs = pl.pallas_call(
            partial(self.kernel, body),
            in_specs=[spec for _, spec in self.ins.values()],
            out_specs=[spec for _, spec in self.outs.values()],
            out_shape=[shape for shape, _ in self.outs.values()],
            scratch_shapes=list(self.scratch.values()),
            compiler_params=pltpu.CompilerParams(
                collective_id=self.call_id, has_side_effects=True, vmem_limit_bytes=58 * MIB
            ),
        )(*[array for array, _ in self.ins.values()])
        return dict(zip(self.outs, outs))


def in_turn(n):
    def body(at, rings):
        for _ in range(n // 2):
            for ring in rings.values():
                ring.step()

    return body


def gather_all(arrays, call_id, flip=0):
    n = lax.axis_size("seq")
    if not ring_size(n):
        return [lax.all_gather(a, "seq", axis=0, tiled=True) for a in arrays]
    call = Call(call_id)
    names = [str(j) for j in range(len(arrays))]
    for j, (name, a) in enumerate(zip(names, arrays)):
        call.take(name + ".src", a, pl.ANY)
        call.give(name, (n * a.shape[0],) + a.shape[1:], a.dtype, pl.ANY)
        call.gather(name, name + ".src", name, by_block(a.shape[0]), (j + flip) % 2 == 1)
    out = call.run(in_turn(n))
    return [out[name] for name in names]


class ScatterRing:
    def __init__(self, n, where, left, right, out, sums, slots, send, recv, flip, axis):
        self.axis = axis
        self.n, self.left_ref, self.right_ref, self.out = n, left, right, out
        self.sums, self.slots, self.send, self.recv = sums, slots, send, recv
        self.pos, self.right, self.left = where
        d = -1 if flip else 1
        self.hops = {d: n // 2, -d: (n - 1) // 2}
        self.order = (d, -d)
        self.done = 0
        self.steps = n // 2

    def term(self, r):
        owner = ring_device(lax.rem(self.pos + (r % self.n), self.n))
        return dot(self.left_ref[owner], self.right_ref[...], 0, self.axis)

    def copy(self, d, h):
        i = 0 if d == 1 else 1
        return pltpu.make_async_remote_copy(
            src_ref=self.sums.at[i, h - 1],
            dst_ref=self.slots.at[i, h - 1],
            send_sem=self.send.at[i, h - 1],
            recv_sem=self.recv.at[i, h - 1],
            device_id={"seq": self.right if d == 1 else self.left},
            device_id_type=MESH,
        )

    def step(self):
        if self.done == self.steps:
            return
        self.done += 1
        h = self.done
        for d in self.order:
            if h > self.hops[d]:
                continue
            i = 0 if d == 1 else 1
            total = self.term(d * (self.hops[d] - h + 1))
            if h > 1:
                self.copy(d, h - 1).wait_recv()
                total = total + self.slots[i, h - 2].astype(F32)
            self.sums[i, h - 1] = total.astype(BF)
            self.copy(d, h).start()

    def finish(self):
        while self.done < self.steps:
            self.step()
        total = self.term(0)
        for d in self.order:
            i, h = (0 if d == 1 else 1), self.hops[d]
            self.copy(d, h).wait_recv()
            total = total + self.slots[i, h - 1].astype(F32)
        self.out[...] = total
        for d in self.order:
            for h in range(1, self.hops[d] + 1):
                self.copy(d, h).wait_send()


def scatter_all(lefts, pairs, call_id, flip=0, small=None):
    n = lax.axis_size("seq")
    pairs = [p if len(p) == 3 else p + (0,) for p in pairs]
    if not ring_size(n):
        sums = [
            lax.psum_scatter(
                dot(lefts[i], right, 0, axis).astype(BF), "seq", scatter_dimension=0, tiled=True
            ).astype(F32)
            for i, right, axis in pairs
        ]
        return sums if small is None else sums + [lax.psum(small.astype(BF), "seq").astype(F32)]
    call = Call(call_id)
    names = [str(j) for j in range(len(pairs))]
    if small is not None:
        call.take("small.src", small)
        call.hold("small.all", (n * small.shape[0], small.shape[1]), F32)
        call.gather("small", "small.src", "small.all", by_block(small.shape[0]))
    for i, a in enumerate(lefts):
        call.left(f"left{i}", a)
    for j, (i, right, axis) in enumerate(pairs):
        call.scatter(names[j], f"left{i}", right, (j + flip) % 2 == 1, axis)
    if small is not None:
        names.append(call.give("small.sum", small.shape, F32))

    def body(at, rings):
        in_turn(n)(at, rings)
        if small is not None:
            rings["small"].finish()
            rows = small.shape[0]
            blocks = [at["small.all"][b * rows : (b + 1) * rows] for b in range(n)]
            at["small.sum"][...] = sum(blocks[1:], blocks[0])
            del rings["small"]

    out = call.run(body)
    return [out[name] for name in names]


def small_sum(x, axis):
    size = lax.axis_size(axis)
    if size > 8:
        return lax.psum(x.astype(BF), axis).astype(F32)
    sent = x.astype(BF)
    routes = [[(i, (i + k) % size) for i in range(size)] for k in range(1, size)]
    return x + sum(lax.ppermute(sent, axis, r).astype(F32) for r in routes)


def dot(a, b, ca, cb):
    return lax.dot_general(a, b, (((ca,), (cb,)), ((), ())), preferred_element_type=F32)


def head_masks(query_width, value_width):
    lane_q = lax.broadcasted_iota(jnp.int32, (1, query_width), 1)
    lane_v = lax.broadcasted_iota(jnp.int32, (1, value_width), 1)
    heads = query_width // QK
    return [
        (
            (lane_q >= h * QK) & (lane_q < (h + 1) * QK),
            (lane_v >= h * VH) & (lane_v < (h + 1) * VH),
        )
        for h in range(heads)
    ]


def query_mask(scal_ref, place_ref, tok, row):
    offset = scal_ref[1 + row]
    pos = scal_ref[0] + lax.broadcasted_iota(jnp.int32, (tok, 1), 0)
    low = jnp.where(pos >= offset, offset, 0)
    other = place_ref[...]
    return (other >= low) & (other <= pos)


def key_mask(scal_ref, place_ref, tok, row):
    offset = scal_ref[1 + row]
    pos = scal_ref[0] + lax.broadcasted_iota(jnp.int32, (tok, 1), 0)
    high = jnp.where(pos >= offset, jnp.int32(1 << 30), offset)
    other = place_ref[...]
    return (other >= pos) & (other < high)


def attend_kernel(scal_ref, place_ref, q_ref, k_ref, v_ref, out_ref):
    q, k, v = q_ref[0], k_ref[0], v_ref[0]
    mask = query_mask(scal_ref, place_ref, q.shape[0], pl.program_id(0))
    total = jnp.zeros((q.shape[0], v.shape[1]), F32)
    for in_q, in_v in head_masks(q.shape[1], v.shape[1]):
        s = dot(jnp.where(in_q, q, jnp.zeros_like(q)), k, 1, 1) * (QK**-0.5)
        w = jnp.where(mask, 1.0 + s + 0.5 * s * s, 0.0)
        den = jnp.sum(w, axis=1, keepdims=True)
        total = total + jnp.where(in_v, dot(w.astype(BF), v, 1, 0) / den, 0.0)
    out_ref[0] = total.astype(BF)


def query_back_kernel(scal_ref, place_ref, q_ref, k_ref, v_ref, da_ref, dq_ref, dan_ref, extra_ref):
    q, k, v = q_ref[0], k_ref[0], v_ref[0]
    da = da_ref[0]
    tok = q.shape[0]
    mask = query_mask(scal_ref, place_ref, tok, pl.program_id(0))
    lane = lax.broadcasted_iota(jnp.int32, (1, q.shape[1]), 1)
    heads = q.shape[1] // QK
    dq = jnp.zeros(q.shape, F32)
    dan_all = jnp.zeros(da.shape, F32)
    extra = jnp.zeros(q.shape, F32)
    for h, (in_q, in_v) in enumerate(head_masks(q.shape[1], v.shape[1])):
        s = dot(jnp.where(in_q, q, jnp.zeros_like(q)), k, 1, 1) * (QK**-0.5)
        w = jnp.where(mask, 1.0 + s + 0.5 * s * s, 0.0)
        den = jnp.sum(w, axis=1, keepdims=True)
        att = dot(w.astype(BF), v, 1, 0) / den
        dan = jnp.where(in_v, da / den, 0.0).astype(BF)
        dan_f = dan.astype(F32)
        delta = jnp.sum(dan_f * att, axis=1, keepdims=True)
        d_kernel = dot(dan, v, 1, 1) - delta
        ds = jnp.where(mask, d_kernel * (1.0 + s), 0.0).astype(BF)
        dq = dq + jnp.where(in_q, dot(ds, k, 1, 0) * (QK**-0.5), 0.0)
        dan_all = dan_all + dan_f
        high = delta.astype(BF).astype(F32)
        extra = extra + jnp.where(lane == h, high, 0.0)
        extra = extra + jnp.where(lane == heads + h, delta - high, 0.0)
    dq_ref[0] = dq.astype(BF)
    dan_ref[0] = dan_all.astype(BF)
    extra_ref[0] = extra.astype(BF)


def key_back_kernel(scal_ref, place_ref, k_ref, v_ref, q_ref, dan_ref, extra_ref, dk_ref, dv_ref):
    k, v = k_ref[0], v_ref[0]
    q, dan, extra = q_ref[0], dan_ref[0], extra_ref[0]
    tok = k.shape[0]
    mask = key_mask(scal_ref, place_ref, tok, pl.program_id(0))
    lane = lax.broadcasted_iota(jnp.int32, (tok, k.shape[1]), 1)
    heads = k.shape[1] // QK
    dk = jnp.zeros(k.shape, F32)
    dv = jnp.zeros(v.shape, F32)
    for h, (in_q, in_v) in enumerate(head_masks(k.shape[1], v.shape[1])):
        s = dot(jnp.where(in_q, k, jnp.zeros_like(k)), q, 1, 1) * (QK**-0.5)
        w = jnp.where(mask, 1.0 + s + 0.5 * s * s, 0.0).astype(BF)
        dv = dv + jnp.where(in_v, dot(w, dan, 1, 0), 0.0)
        pick = jnp.where((lane == h) | (lane == heads + h), 1.0, 0.0).astype(BF)
        d_kernel = dot(jnp.where(in_v, v, jnp.zeros_like(v)), dan, 1, 1) - dot(pick, extra, 1, 1)
        ds = jnp.where(mask, d_kernel * (1.0 + s), 0.0).astype(BF)
        dk = dk + jnp.where(in_q, dot(ds, q, 1, 0) * (QK**-0.5), 0.0)
    dk_ref[0] = dk.astype(BF)
    dv_ref[0] = dv.astype(BF)


class Exchange:
    def __init__(self, n, at, name, block, place):
        self.n, self.block, self.place = n, block, place
        self.send, self.recv = at[name + ".send"], at[name + ".recv"]
        self.me = lax.axis_index("seq")

    def copy(self, k):
        partner = lax.rem(self.me + k, self.n)
        return pltpu.make_async_remote_copy(
            src_ref=self.block(partner),
            dst_ref=self.place(self.me),
            send_sem=self.send.at[k],
            recv_sem=self.recv.at[k],
            device_id={"seq": partner},
            device_id_type=MESH,
        )

    def own(self):
        return pltpu.make_async_copy(self.block(self.me), self.place(self.me), self.send.at[0])

    def start(self):
        for k in range(1, self.n):
            self.copy(k).start()
        self.own().start()

    def wait(self):
        self.own().wait()
        for k in range(1, self.n):
            self.copy(k).wait_recv()

    def wait_sent(self):
        for k in range(1, self.n):
            self.copy(k).wait_send()


def to_pair(ref, features, tok):
    def block(partner):
        rows = pl.ds(pl.multiple_of(lax.rem(partner, 2) * features, 16), features)
        return ref.at[rows, pl.ds(pl.multiple_of((partner // 2) * tok, 128), tok)]

    return block


def at_positions(ref, tok):
    return lambda device: ref.at[:, pl.ds(pl.multiple_of(device * tok, 128), tok)]


def causal(offset, i, tok):
    shape = ((i + 1) * tok, tok)
    earlier = lax.broadcasted_iota(jnp.int32, shape, 0)
    pos = i * tok + lax.broadcasted_iota(jnp.int32, shape, 1)
    return (earlier <= pos) & ((earlier >= offset) | (pos < offset))


def attend_pairs(off, qkv, carried, call_id):
    n = lax.axis_size("seq")
    tok = qkv.shape[1] * 2 // n
    features = qkv.shape[0] // 2
    vf = features - 4 * QK
    call = Call(call_id)
    call.take("off", off, pltpu.SMEM)
    call.take("qkv", qkv)
    for j, a in enumerate(carried):
        call.take(f"c{j}.src", a, pl.ANY)
        call.give(f"c{j}", (n * a.shape[0], a.shape[1]), a.dtype, pl.ANY)
        call.gather(f"c{j}", f"c{j}.src", f"c{j}", by_block(a.shape[0]), j % 2 == 1)
    call.give("mixed", (2 * vf, qkv.shape[1]), BF)
    call.give("all", (features, n * tok), BF)
    call.give("att", (vf, n * tok), F32)
    call.give("den", (8, n * tok), F32)
    call.hold("own", (vf, n * tok), BF)
    call.exchange("in")
    call.exchange("out")

    def incoming(at):
        return Exchange(n, at, "in", to_pair(at["qkv"], features, tok), at_positions(at["all"], tok))

    def body(at, rings):
        def turn():
            for ring in rings.values():
                ring.step()

        turn()
        arriving = incoming(at)
        arriving.wait()
        turn()
        me = lax.axis_index("seq")
        offset = at["off"][me // 2]
        whole = at["all"]
        at["den"][...] = jnp.ones_like(at["den"])
        for h in range(2):
            lines = slice(h * vf // 2, (h + 1) * vf // 2)
            for i in range(n):
                here, upto = slice(i * tok, (i + 1) * tok), slice(0, (i + 1) * tok)
                q = whole[h * QK : (h + 1) * QK, here]
                k = whole[(2 + h) * QK : (3 + h) * QK, upto]
                v = whole[4 * QK + h * vf // 2 : 4 * QK + (h + 1) * vf // 2, upto]
                s = dot(k, q, 0, 0) * (QK**-0.5)
                w = jnp.where(causal(offset, i, tok), 1.0 + s + 0.5 * s * s, 0.0)
                den = jnp.sum(w, axis=0, keepdims=True)
                att = dot(v, w.astype(BF), 1, 0) / den
                at["att"][lines, here] = att
                at["den"][h : h + 1, here] = den
                at["own"][lines, here] = att.astype(BF)
        leaving = Exchange(
            n, at, "out", at_positions(at["own"], tok), lambda me: to_pair(at["mixed"], vf, tok)(me)
        )
        leaving.start()
        turn()
        leaving.wait()
        arriving.wait_sent()
        leaving.wait_sent()

    out = call.run(body, lambda at: incoming(at).start())
    return out, [out[f"c{j}"] for j in range(len(carried))]


def attend_pairs_back(off, da, kept, scatters, call_id):
    n = lax.axis_size("seq")
    whole = kept["all"]
    features, tok = whole.shape[0], whole.shape[1] // n
    vf = features - 4 * QK
    call = Call(call_id)
    call.take("off", off, pltpu.SMEM)
    call.take("da", da)
    for name in ("all", "att", "den"):
        call.take(name, kept[name])
    lefts, pairs = scatters
    for i, a in enumerate(lefts):
        call.left(f"left{i}", a)
    for j, (i, right) in enumerate(pairs):
        call.scatter(f"s{j}", f"left{i}", right, j % 2 == 1)
    call.give("d", (2 * features, da.shape[1]), BF)
    call.hold("da_all", (vf, n * tok), BF)
    call.hold("sum", (2 * QK + vf, n * tok), F32)
    call.hold("own", (features, n * tok), BF)
    call.exchange("in")
    call.exchange("out")

    def incoming(at):
        return Exchange(n, at, "in", to_pair(at["da"], vf, tok), at_positions(at["da_all"], tok))

    def body(at, rings):
        arriving = incoming(at)
        arriving.wait()
        me = lax.axis_index("seq")
        offset = at["off"][me // 2]
        whole = at["all"]
        total = at["sum"]
        for h in range(2):
            lines = slice(h * vf // 2, (h + 1) * vf // 2)
            k_lines = slice(h * QK, (h + 1) * QK)
            v_lines = slice(2 * QK + h * vf // 2, 2 * QK + (h + 1) * vf // 2)
            for i in range(n - 1, -1, -1):
                here, upto = slice(i * tok, (i + 1) * tok), slice(0, (i + 1) * tok)
                q = whole[h * QK : (h + 1) * QK, here]
                k = whole[(2 + h) * QK : (3 + h) * QK, upto]
                v = whole[4 * QK + h * vf // 2 : 4 * QK + (h + 1) * vf // 2, upto]
                mask = causal(offset, i, tok)
                s = dot(k, q, 0, 0) * (QK**-0.5)
                w = jnp.where(mask, 1.0 + s + 0.5 * s * s, 0.0).astype(BF)
                dan = (at["da_all"][lines, here].astype(F32) / at["den"][h : h + 1, here]).astype(BF)
                delta = jnp.sum(dan.astype(F32) * at["att"][lines, here], axis=0, keepdims=True)
                ds = jnp.where(mask, (dot(v, dan, 0, 0) - delta) * (1.0 + s), 0.0).astype(BF)
                dq = dot(k, ds, 1, 0) * (QK**-0.5)
                at["own"][h * QK : (h + 1) * QK, here] = dq.astype(BF)
                dk = dot(q, ds, 1, 1) * (QK**-0.5)
                dv = dot(dan, w, 1, 1)
                if i == n - 1:
                    total[k_lines, upto] = dk
                    total[v_lines, upto] = dv
                else:
                    total[k_lines, upto] += dk
                    total[v_lines, upto] += dv
            if h == 0:
                for ring in rings.values():
                    ring.step()
        at["own"][2 * QK :, :] = total[...].astype(BF)
        leaving = Exchange(
            n, at, "out", at_positions(at["own"], tok), lambda me: to_pair(at["d"], features, tok)(me)
        )
        leaving.start()
        for ring in rings.values():
            ring.step()
        leaving.wait()
        arriving.wait_sent()
        leaving.wait_sent()

    out = call.run(body, lambda at: incoming(at).start())
    return out["d"], [out[f"s{j}"] for j in range(len(pairs))]


def by_rows(kernel, scal, place, operands, widths, kinds):
    rows = operands[0].shape[0]
    tok = operands[0].shape[1]
    specs = [
        pl.BlockSpec(memory_space=pltpu.SMEM),
        pl.BlockSpec(place.shape, lambda r: (0, 0)),
    ]
    specs += [pl.BlockSpec((1,) + a.shape[1:], lambda r: (r, 0, 0)) for a in operands]
    return pl.pallas_call(
        kernel,
        grid=(rows,),
        in_specs=specs,
        out_specs=[pl.BlockSpec((1, tok, w), lambda r: (r, 0, 0)) for w in widths],
        out_shape=[jax.ShapeDtypeStruct((rows, tok, w), t) for w, t in zip(widths, kinds)],
        compiler_params=pltpu.CompilerParams(vmem_limit_bytes=48 * 1024 * 1024),
    )(scal, place, *operands)


def rms_scale(x):
    return lax.rsqrt(jnp.mean(x * x, axis=-1, keepdims=True) + EPSILON)


def rms_norm(x, gain):
    return x * rms_scale(x) * gain


def rms_back(x, gain, dn):
    scale = rms_scale(x)
    unit = x * scale
    gain_grad = jnp.sum(dn * unit, axis=0)
    dg = dn * gain
    dx = scale * (dg - unit * jnp.mean(dg * unit, axis=-1, keepdims=True))
    return dx, gain_grad


def head_total(partial_sum):
    return lax.psum(partial_sum, "head").astype(F32)


def tie(xs, *others):
    return list(lax.optimization_barrier((tuple(xs), tuple(others)))[0])


def mlp_forward(resid, gain, weights):
    gate_w, up_w, down_t = weights
    normed = rms_norm(resid, gain).astype(BF)
    gate_val = dot(normed, gate_w, 1, 0)
    up_val = dot(normed, up_w, 1, 0)
    hidden = (gate_val * jax.nn.sigmoid(gate_val) * up_val).astype(BF)
    return dot(hidden, down_t, 1, 1).astype(BF), (normed, gate_val, up_val, hidden)


def mlp_scatter(kept, call_id, *others):
    (normed, grad_b), d_gate, d_up, hidden = kept
    normed, grad_b = tie((normed, grad_b), *others)
    return scatter_all((normed, grad_b), ((0, d_gate), (0, d_up), (1, hidden)), call_id)


def mlp_backward(grad_b, saved, weights):
    gate_w, up_w, down_t = weights
    normed, gate_val, up_val, hidden = saved
    dh = dot(grad_b, down_t, 1, 0)
    sig = jax.nn.sigmoid(gate_val)
    silu = gate_val * sig
    d_gate = (dh * up_val * (sig * (1.0 + gate_val * (1.0 - sig)))).astype(BF)
    d_up = (dh * silu).astype(BF)
    dn_part = (dot(d_gate, gate_w, 1, 1) + dot(d_up, up_w, 1, 1)).astype(BF)
    return dn_part, ((normed, grad_b), d_gate, d_up, hidden)


def shifted(block, before, shift):
    if shift == 0:
        return block
    return jnp.concatenate([before[:, before.shape[1] - shift :], block[:, :-shift]], axis=1)


def advanced(block, after, shift):
    if shift == 0:
        return block
    return jnp.concatenate([block[:, shift:], after[:, :shift]], axis=1)


def per_device(
    activations,
    offsets,
    cotangent,
    attn_query,
    attn_key,
    attn_value,
    attn_output,
    ffn1_gate,
    ffn1_up,
    ffn1_down,
    conv_input,
    conv_gate,
    conv_output,
    conv_kernel,
    ffn2_gate,
    ffn2_up,
    ffn2_down,
    norm_gains,
):
    n = lax.axis_size("seq")
    micro, row_count, tok, width = activations.shape
    rows = micro * row_count
    count = rows * tok
    qw, vw = attn_query.shape[1], attn_value.shape[1]
    cw = conv_input.shape[1]
    taps = conv_kernel.shape[0]
    here = lax.axis_index("seq")
    start = here * tok
    off = offsets.reshape(rows)

    paired = ring_size(n) and 2 * rows == n and qw == 4 * QK
    if paired:
        halves = [
            a[:, g * a.shape[1] // 2 : (g + 1) * a.shape[1] // 2]
            for g in range(2)
            for a in (attn_query, attn_key, attn_value)
        ]
        qkv_s = jnp.concatenate(halves, axis=1)
    else:
        qkv_s = jnp.concatenate([attn_query, attn_key, attn_value], axis=1)
    gains = norm_gains.astype(F32)
    kernel_f = conv_kernel.astype(F32)
    inputs = activations.reshape(count, width).astype(F32)
    grad_four = cotangent.reshape(count, width)
    outs_s = jnp.concatenate([attn_output.T, conv_output.T], axis=1)
    (qkv_w,) = gather_all([qkv_s], 1)

    scal = jnp.concatenate([start[None].astype(jnp.int32), off])
    place = jnp.arange(n * tok, dtype=jnp.int32).reshape(1, n * tok)
    normed_a = rms_norm(inputs, gains[0]).astype(BF)

    def by_sequence(blocks):
        return jnp.swapaxes(blocks.reshape(n, rows, tok, -1), 0, 1).reshape(rows, n * tok, -1)

    if paired:
        qkv = dot(qkv_w, normed_a, 0, 1).astype(BF)
        attention, (outs_t, gate_1) = attend_pairs(off, qkv, (outs_s, ffn1_gate), 2)
        mixed, mixed_axis = attention["mixed"], 1
    else:
        qkv = dot(normed_a, qkv_w, 1, 0).astype(BF)
        qkv_all = by_sequence(gather_all([qkv], 2)[0])
        own = qkv.reshape(rows, tok, -1)
        q_own, k_own, v_own = own[..., :qw], own[..., qw : 2 * qw], own[..., 2 * qw :]
        q_all, k_all, v_all = qkv_all[..., :qw], qkv_all[..., qw : 2 * qw], qkv_all[..., 2 * qw :]
        (mixed,) = by_rows(attend_kernel, scal, place, (q_own, k_all, v_all), (vw,), (BF,))
        mixed, mixed_axis = mixed.reshape(count, vw), 0
        outs_t, gate_1 = gather_all((outs_s, ffn1_gate), 11)
    out_t, conv_out_t = outs_t[:, :vw], outs_t[:, vw:]
    attn_part = dot(mixed, out_t, 1 - mixed_axis, 1).astype(BF)
    attn_sum = head_total(attn_part)
    ffn1 = [gate_1] + gather_all(tie((ffn1_up, ffn1_down.T), attn_part), 12)
    resid_one = inputs + attn_sum
    part, kept_one = mlp_forward(resid_one, gains[1], ffn1)
    ffn1_sum = head_total(part)
    inner_w, gate_w = gather_all(tie((conv_input, conv_gate), part), 4)
    resid_two = resid_one + ffn1_sum

    normed_c = rms_norm(resid_two, gains[2]).astype(BF)
    inner = dot(normed_c, inner_w, 1, 0).reshape(rows, tok, cw)
    gate_c = dot(normed_c, gate_w, 1, 0).reshape(rows, tok, cw)
    pos = start + jnp.arange(tok + taps - 1, dtype=jnp.int32)
    current = pos[None, :] >= off[:, None]

    def valid(t, first, length):
        p = pos[None, first : first + length]
        source = p - t
        same = (source >= off[:, None]) == current[:, first : first + length]
        return ((source >= 0) & same).astype(F32)[:, :, None]

    edge = lax.ppermute(inner[:, tok - (taps - 1) :], "seq", [(i, i + 1) for i in range(n - 1)])
    moved = [shifted(inner, edge, t) * valid(t, 0, tok) for t in range(taps)]
    conv = sum(kernel_f[t][None, None, :] * moved[t] for t in range(taps))
    product = (conv * gate_c).astype(BF).reshape(count, cw)
    conv_part = dot(product, conv_out_t, 1, 1).astype(BF)
    conv_sum = head_total(conv_part)
    ffn2 = gather_all(tie((ffn2_gate, ffn2_up, ffn2_down.T), conv_part), 3)
    resid_three = resid_two + conv_sum
    out_part, kept_two = mlp_forward(resid_three, gains[3], ffn2)

    dn_part, grads_two = mlp_backward(grad_four, kept_two, ffn2)
    dn = head_total(dn_part)
    sums_two = mlp_scatter(grads_two, 5, dn_part)
    (dn,) = tie((dn,), *sums_two)
    out_sum = head_total(tie((out_part,), *sums_two)[0])
    block_output = (resid_three + out_sum).astype(BF).reshape(activations.shape)
    dx, gain_four = rms_back(resid_three, gains[3], dn)
    grad_three = grad_four.astype(F32) + dx
    grad_b = grad_three.astype(BF)
    d_product = dot(grad_b, conv_out_t, 1, 0).reshape(rows, tok, cw)
    d_gate_c = (d_product * conv).astype(BF).reshape(count, cw)
    d_conv = d_product * gate_c
    next_rows = lax.ppermute(d_conv[:, : taps - 1], "seq", [(i + 1, i) for i in range(n - 1)])
    d_inner = sum(
        kernel_f[t][None, None, :] * advanced(d_conv, next_rows, t) * valid(t, t, tok)
        for t in range(taps)
    )
    d_inner = d_inner.astype(BF).reshape(count, cw)
    kernel_grad = jnp.stack([jnp.sum(d_conv * moved[t], axis=(0, 1)) for t in range(taps)])
    dn_part = (dot(d_inner, inner_w, 1, 1) + dot(d_gate_c, gate_w, 1, 1)).astype(BF)
    dn = head_total(dn_part)
    sums_conv = scatter_all(
        tie((normed_c, grad_b), dn_part), ((0, d_inner), (0, d_gate_c), (1, product)), 6, 1
    )
    (dn,) = tie((dn,), *sums_conv)
    dx, gain_three = rms_back(resid_two, gains[2], dn)
    grad_two = grad_three + dx
    dn_part, grads_one = mlp_backward(grad_two.astype(BF), kept_one, ffn1)
    dn = head_total(dn_part)
    (normed_1, grad_b1), d_gate_1, d_up_1, hidden_1 = grads_one
    if ring_size(n):
        sums_one = scatter_all(tie((normed_1,), dn_part), ((0, d_gate_1),), 9)
        (dn,) = tie((dn,), *sums_one)
    dx, gain_two = rms_back(resid_one, gains[1], dn)
    grad_one = grad_two + dx

    grad_b = grad_one.astype(BF)
    later = ((normed_1, grad_b1), ((0, d_up_1), (1, hidden_1)))
    if paired:
        da = dot(out_t, grad_b, 0, 1).astype(BF)
        d_qkv, more = attend_pairs_back(off, da, attention, later, 7)
        sums_one = sums_one + more
    else:
        da = dot(grad_b, out_t, 1, 0).reshape(rows, tok, vw)
        dq, dan, extra = by_rows(
            query_back_kernel, scal, place, (q_own, k_all, v_all, da), (qw, vw, qw), (BF, BF, BF)
        )
        back = jnp.concatenate([dan, extra], axis=-1).reshape(count, vw + qw)
        back_all = by_sequence(gather_all([back], 7, 1)[0])
        dk, dv = by_rows(
            key_back_kernel,
            scal,
            place,
            (k_own, v_own, q_all, back_all[..., :vw], back_all[..., vw:]),
            (qw, vw),
            (BF, BF),
        )
        sums_one = scatter_all((normed_1,), ((0, d_gate_1),), 9) + scatter_all(*later, 10)
        d_qkv = jnp.concatenate([dq, dk, dv], axis=-1).reshape(count, 2 * qw + vw)
    dn_part = dot(d_qkv, qkv_w, 1 - mixed_axis, 1).astype(BF)
    dn = head_total(dn_part)
    unit = inputs * rms_scale(inputs)
    gain_one = small_sum(jnp.sum(dn_part.astype(F32) * unit, axis=0), "head")
    small = jnp.concatenate(
        [
            jnp.stack([gain_one, gain_two, gain_three, gain_four]),
            jnp.pad(kernel_grad, ((0, 0), (0, width - cw))),
            jnp.zeros((8 - 4 - taps, width), F32),
        ]
    )
    sums_attn = scatter_all(
        tie((normed_a, grad_b), dn_part), ((0, d_qkv, mixed_axis), (1, mixed, mixed_axis)), 8, 0, small
    )
    gains_grad, kernel_grad = sums_attn[2][:4], sums_attn[2][4 : 4 + taps, :cw]
    qkv_sum = sums_attn[0]
    if paired:
        edges = (0, qw // 2, qw, qw + vw // 2)
        step = qw + vw // 2
        query_sum, key_sum, value_sum = (
            jnp.concatenate([qkv_sum[:, g * step + a : g * step + b] for g in range(2)], axis=1)
            for a, b in zip(edges[:-1], edges[1:])
        )
    else:
        query_sum, key_sum = qkv_sum[:, :qw], qkv_sum[:, qw : 2 * qw]
        value_sum = qkv_sum[:, 2 * qw :]
    (dn,) = tie((dn,), *sums_attn)
    dx, _ = rms_back(inputs, gains[0], dn)
    input_grad = (grad_one + dx).reshape(activations.shape)

    return (
        block_output,
        input_grad,
        query_sum,
        key_sum,
        value_sum,
        sums_attn[1].T,
        sums_one[0],
        sums_one[1],
        sums_one[2].T,
        sums_conv[0],
        sums_conv[1],
        sums_conv[2].T,
        kernel_grad,
        sums_two[0],
        sums_two[1],
        sums_two[2].T,
        gains_grad,
    )


def solution(mesh):
    rows_in = P("seq", "head")
    rows_out = P("head", "seq")
    tokens = P(None, None, "seq", None)
    in_specs = (
        (tokens, P(), tokens)
        + (rows_in, rows_in, rows_in, rows_out)
        + (rows_in, rows_in, rows_out)
        + (rows_in, rows_in, rows_out)
        + (P(None, "head"),)
        + (rows_in, rows_in, rows_out)
        + (P(),)
    )
    out_specs = (
        (tokens, tokens)
        + (rows_in, rows_in, rows_in, rows_out)
        + (rows_in, rows_in, rows_out)
        + (rows_in, rows_in, rows_out)
        + (P(None, "head"),)
        + (rows_in, rows_in, rows_out)
        + (P(),)
    )
    return jax.shard_map(
        per_device, mesh=mesh, in_specs=in_specs, out_specs=out_specs, check_vma=False
    )
```

```python
from functools import partial

import jax
import jax.numpy as jnp
from jax import lax
from jax.experimental import pallas as pl
from jax.experimental.pallas import tpu as pltpu
from jax.sharding import PartitionSpec as P

QK = 16
VH = 112
EPSILON = 1e-05
BF = jnp.bfloat16
F32 = jnp.float32


MESH = pl.DeviceIdType.MESH
ANY = pl.BlockSpec(memory_space=pl.ANY)


def ring_device(p):
    return jnp.where(p < 4, 2 * p, 15 - 2 * p)


def ring_position(s):
    return jnp.where(lax.rem(s, 2) == 0, s // 2, 7 - s // 2)


def ring_size(n):
    return n == 8


def greet(n, everyone=False):
    me = lax.axis_index("seq")
    pos = ring_position(me)
    right = ring_device(lax.rem(pos + 1, n))
    left = ring_device(lax.rem(pos + n - 1, n))
    barrier = pltpu.get_barrier_semaphore()
    partners = [lax.rem(me + k, n) for k in range(1, n)] if everyone else [left, right]
    for partner in partners:
        pl.semaphore_signal(barrier, inc=1, device_id={"seq": partner}, device_id_type=MESH)
    pl.semaphore_wait(barrier, len(partners))
    return pos, right, left


class GatherRing:
    def __init__(self, n, where, src, out, place, send, recv, local, flip):
        self.n, self.src, self.out, self.place = n, src, out, place
        self.send, self.recv, self.local = send, recv, local
        self.pos, self.right, self.left = where
        self.flip = flip
        self.steps = n // 2
        self.done = 0

    def block(self, r):
        return self.place(self.out, ring_device(lax.rem(self.pos + (r % self.n), self.n)))

    def copy(self, k, d):
        block = self.block(-d * (k - 1))
        i = 0 if d == 1 else 1
        return pltpu.make_async_remote_copy(
            src_ref=self.src if k == 1 else block,
            dst_ref=block,
            send_sem=self.send.at[i, k - 1],
            recv_sem=self.recv.at[i, k - 1],
            device_id={"seq": self.right if d == 1 else self.left},
            device_id_type=MESH,
        )

    def ways(self, k):
        if k <= (self.n - 1) // 2:
            return (1, -1)
        return (-1,) if self.flip else (1,)

    def step(self):
        if self.done == self.steps:
            return
        if self.done == 0:
            pltpu.make_async_copy(self.src, self.block(0), self.local).start()
        self.done += 1
        k = self.done
        for d in self.ways(k):
            if k > 1:
                self.copy(k - 1, d).wait_recv()
            self.copy(k, d).start()

    def finish(self):
        while self.done < self.steps:
            self.step()
        pltpu.make_async_copy(self.src, self.block(0), self.local).wait()
        last = {d: max(k for k in range(1, self.steps + 1) if d in self.ways(k)) for d in (1, -1)}
        for d in (1, -1):
            self.copy(last[d], d).wait_recv()
        for k in range(1, self.steps + 1):
            for d in self.ways(k):
                self.copy(k, d).wait_send()


def by_block(height, first=0, rows=None):
    rows = height if rows is None else rows
    unit = 8 if height % 16 else 16
    return lambda ref, owner: ref.at[pl.ds(pl.multiple_of(owner * height + first, unit), rows)]


def by_position(tok):
    return lambda ref, owner: ref.at[:, pl.ds(pl.multiple_of(owner * tok, 16), tok)]


VMEM = pltpu.VMEM
MIB = 1024 * 1024


class Call:
    def __init__(self, call_id):
        self.n = lax.axis_size("seq")
        self.call_id = call_id
        self.ins, self.outs, self.scratch = {}, {}, {}
        self.gathers, self.scatters = {}, {}
        self.exchanges = []

    def exchange(self, name):
        self.sems(name + ".send", self.n)
        self.sems(name + ".recv", self.n)
        self.exchanges.append(name)

    def take(self, name, array, space=VMEM):
        self.ins[name] = (array, pl.BlockSpec(memory_space=space))
        return name

    def give(self, name, shape, kind, space=VMEM):
        self.outs[name] = (jax.ShapeDtypeStruct(shape, kind), pl.BlockSpec(memory_space=space))
        return name

    def hold(self, name, shape, kind):
        self.scratch[name] = VMEM(shape, kind)
        return name

    def sems(self, name, *shape):
        self.scratch[name] = pltpu.SemaphoreType.DMA(shape)

    def gather_blocks(self, name, array, flip=False):
        height = array.shape[0]
        self.take(name + ".src", array, pl.ANY)
        self.give(name, (self.n * height,) + array.shape[1:], array.dtype, pl.ANY)
        half = height // 2
        for p in range(2):
            self.gather(
                f"{name}.{p}",
                name + ".src",
                name,
                by_block(height, p * half, half),
                bool(p) != flip,
                (p * half, half),
            )

    def gather(self, name, src, out, place, flip=False, rows=None):
        half = self.n // 2
        self.sems(name + ".send", 2, half)
        self.sems(name + ".recv", 2, half)
        self.sems(name + ".local", 1)
        self.gathers[name] = (src, out, place, flip, rows)

    def left(self, name, array):
        self.take(name, array)
        rows, width = array.shape
        self.hold(name + ".blocked", (self.n, rows, width // self.n), BF)

    def scatter(self, name, left, right, flip=False, axis=0):
        n = self.n
        height = self.ins[left][0].shape[1] // n
        width = right.shape[1 - axis]
        self.take(name + ".right", right)
        self.give(name, (height, width), F32)
        cut = -(-width // 256) * 128
        for p, span in enumerate(((0, cut), (cut, width))):
            part = f"{name}.{p}"
            block = (height, span[1] - span[0])
            self.hold(part + ".sums", (2, n // 2) + block, BF)
            self.hold(part + ".slots", (2, n // 2) + block, BF)
            self.sems(part + ".send", 2, n // 2)
            self.sems(part + ".recv", 2, n // 2)
            self.scatters[part] = (name, left, bool(p) != flip, axis, span)

    def kernel(self, body, *refs):
        names = list(self.ins) + list(self.outs) + list(self.scratch)
        at = dict(zip(names, refs))
        where = greet(self.n, bool(self.exchanges))
        rings = {}
        if self.early is not None:
            self.early(at)
        for name, (src, out, place, flip, rows) in self.gathers.items():
            rings[name] = GatherRing(
                self.n,
                where,
                at[src] if rows is None else at[src].at[pl.ds(*rows)],
                at[out],
                place,
                at[name + ".send"],
                at[name + ".recv"],
                at[name + ".local"].at[0],
                flip,
            )
        ready = set()
        for name, (whole, left, flip, axis, span) in self.scatters.items():
            blocked = at[left + ".blocked"]
            if left not in ready:
                ready.add(left)
                width = blocked.shape[2]
                for b in range(self.n):
                    blocked[b] = at[left][:, b * width : (b + 1) * width]
            rings[name] = ScatterRing(
                self.n,
                where,
                blocked,
                at[whole + ".right"],
                at[whole],
                at[name + ".sums"],
                at[name + ".slots"],
                at[name + ".send"],
                at[name + ".recv"],
                flip,
                axis,
                span,
            )
            rings[name].step()
        body(at, rings)
        for ring in rings.values():
            ring.finish()

    early = None

    def run(self, body, early=None):
        self.early = early
        outs = pl.pallas_call(
            partial(self.kernel, body),
            in_specs=[spec for _, spec in self.ins.values()],
            out_specs=[spec for _, spec in self.outs.values()],
            out_shape=[shape for shape, _ in self.outs.values()],
            scratch_shapes=list(self.scratch.values()),
            compiler_params=pltpu.CompilerParams(
                collective_id=self.call_id, has_side_effects=True, vmem_limit_bytes=58 * MIB
            ),
        )(*[array for array, _ in self.ins.values()])
        return dict(zip(self.outs, outs))


def in_turn(n):
    def body(at, rings):
        for _ in range(n // 2):
            for ring in rings.values():
                ring.step()

    return body


def gather_all(arrays, call_id, flip=0):
    n = lax.axis_size("seq")
    if not ring_size(n):
        return [lax.all_gather(a, "seq", axis=0, tiled=True) for a in arrays]
    call = Call(call_id)
    names = [str(j) for j in range(len(arrays))]
    for j, (name, a) in enumerate(zip(names, arrays)):
        call.gather_blocks(name, a, (j + flip) % 2 == 1)
    out = call.run(in_turn(n))
    return [out[name] for name in names]


class ScatterRing:
    def __init__(self, n, where, left, right, out, sums, slots, send, recv, flip, axis, span):
        self.axis, self.span = axis, slice(*span)
        self.n, self.left_ref, self.right_ref, self.out = n, left, right, out
        self.sums, self.slots, self.send, self.recv = sums, slots, send, recv
        self.pos, self.right, self.left = where
        d = -1 if flip else 1
        self.hops = {d: n // 2, -d: (n - 1) // 2}
        self.order = (d, -d)
        self.done = 0
        self.steps = n // 2

    def term(self, r):
        owner = ring_device(lax.rem(self.pos + (r % self.n), self.n))
        right = self.right_ref[:, self.span] if self.axis == 0 else self.right_ref[self.span]
        return dot(self.left_ref[owner], right, 0, self.axis)

    def copy(self, d, h):
        i = 0 if d == 1 else 1
        return pltpu.make_async_remote_copy(
            src_ref=self.sums.at[i, h - 1],
            dst_ref=self.slots.at[i, h - 1],
            send_sem=self.send.at[i, h - 1],
            recv_sem=self.recv.at[i, h - 1],
            device_id={"seq": self.right if d == 1 else self.left},
            device_id_type=MESH,
        )

    def step(self):
        if self.done == self.steps:
            return
        self.done += 1
        h = self.done
        for d in self.order:
            if h > self.hops[d]:
                continue
            i = 0 if d == 1 else 1
            total = self.term(d * (self.hops[d] - h + 1))
            if h > 1:
                self.copy(d, h - 1).wait_recv()
                total = total + self.slots[i, h - 2].astype(F32)
            self.sums[i, h - 1] = total.astype(BF)
            self.copy(d, h).start()

    def finish(self):
        while self.done < self.steps:
            self.step()
        total = self.term(0)
        for d in self.order:
            i, h = (0 if d == 1 else 1), self.hops[d]
            self.copy(d, h).wait_recv()
            total = total + self.slots[i, h - 1].astype(F32)
        self.out[:, self.span] = total
        for d in self.order:
            for h in range(1, self.hops[d] + 1):
                self.copy(d, h).wait_send()


def scatter_all(lefts, pairs, call_id, flip=0, small=None, after=()):
    n = lax.axis_size("seq")
    pairs = [p if len(p) == 3 else p + (0,) for p in pairs]
    if not ring_size(n):
        sums = [
            lax.psum_scatter(
                dot(lefts[i], right, 0, axis).astype(BF), "seq", scatter_dimension=0, tiled=True
            ).astype(F32)
            for i, right, axis in pairs
        ]
        return sums if small is None else sums + [lax.psum(small.astype(BF), "seq").astype(F32)]
    call = Call(call_id)
    names = [str(j) for j in range(len(pairs))]
    for j, a in enumerate(after):
        call.take(f"after{j}", a, pl.ANY)
    if small is not None:
        call.take("small.src", small)
        call.hold("small.all", (n * small.shape[0], small.shape[1]), F32)
        call.gather("small", "small.src", "small.all", by_block(small.shape[0]))
    for i, a in enumerate(lefts):
        call.left(f"left{i}", a)
    for j, (i, right, axis) in enumerate(pairs):
        call.scatter(names[j], f"left{i}", right, (j + flip) % 2 == 1, axis)
    if small is not None:
        names.append(call.give("small.sum", small.shape, F32))

    def body(at, rings):
        in_turn(n)(at, rings)
        if small is not None:
            rings["small"].finish()
            rows = small.shape[0]
            blocks = [at["small.all"][b * rows : (b + 1) * rows] for b in range(n)]
            at["small.sum"][...] = sum(blocks[1:], blocks[0])
            del rings["small"]

    out = call.run(body)
    return [out[name] for name in names]


def small_sum(x, axis):
    size = lax.axis_size(axis)
    if size > 8:
        return lax.psum(x.astype(BF), axis).astype(F32)
    sent = x.astype(BF)
    routes = [[(i, (i + k) % size) for i in range(size)] for k in range(1, size)]
    return x + sum(lax.ppermute(sent, axis, r).astype(F32) for r in routes)


def dot(a, b, ca, cb):
    return lax.dot_general(a, b, (((ca,), (cb,)), ((), ())), preferred_element_type=F32)


def head_masks(query_width, value_width):
    lane_q = lax.broadcasted_iota(jnp.int32, (1, query_width), 1)
    lane_v = lax.broadcasted_iota(jnp.int32, (1, value_width), 1)
    heads = query_width // QK
    return [
        (
            (lane_q >= h * QK) & (lane_q < (h + 1) * QK),
            (lane_v >= h * VH) & (lane_v < (h + 1) * VH),
        )
        for h in range(heads)
    ]


def query_mask(scal_ref, place_ref, tok, row):
    offset = scal_ref[1 + row]
    pos = scal_ref[0] + lax.broadcasted_iota(jnp.int32, (tok, 1), 0)
    low = jnp.where(pos >= offset, offset, 0)
    other = place_ref[...]
    return (other >= low) & (other <= pos)


def key_mask(scal_ref, place_ref, tok, row):
    offset = scal_ref[1 + row]
    pos = scal_ref[0] + lax.broadcasted_iota(jnp.int32, (tok, 1), 0)
    high = jnp.where(pos >= offset, jnp.int32(1 << 30), offset)
    other = place_ref[...]
    return (other >= pos) & (other < high)


def attend_kernel(scal_ref, place_ref, q_ref, k_ref, v_ref, out_ref):
    q, k, v = q_ref[0], k_ref[0], v_ref[0]
    mask = query_mask(scal_ref, place_ref, q.shape[0], pl.program_id(0))
    total = jnp.zeros((q.shape[0], v.shape[1]), F32)
    for in_q, in_v in head_masks(q.shape[1], v.shape[1]):
        s = dot(jnp.where(in_q, q, jnp.zeros_like(q)), k, 1, 1) * (QK**-0.5)
        w = jnp.where(mask, 1.0 + s + 0.5 * s * s, 0.0)
        den = jnp.sum(w, axis=1, keepdims=True)
        total = total + jnp.where(in_v, dot(w.astype(BF), v, 1, 0) / den, 0.0)
    out_ref[0] = total.astype(BF)


def query_back_kernel(scal_ref, place_ref, q_ref, k_ref, v_ref, da_ref, dq_ref, dan_ref, extra_ref):
    q, k, v = q_ref[0], k_ref[0], v_ref[0]
    da = da_ref[0]
    tok = q.shape[0]
    mask = query_mask(scal_ref, place_ref, tok, pl.program_id(0))
    lane = lax.broadcasted_iota(jnp.int32, (1, q.shape[1]), 1)
    heads = q.shape[1] // QK
    dq = jnp.zeros(q.shape, F32)
    dan_all = jnp.zeros(da.shape, F32)
    extra = jnp.zeros(q.shape, F32)
    for h, (in_q, in_v) in enumerate(head_masks(q.shape[1], v.shape[1])):
        s = dot(jnp.where(in_q, q, jnp.zeros_like(q)), k, 1, 1) * (QK**-0.5)
        w = jnp.where(mask, 1.0 + s + 0.5 * s * s, 0.0)
        den = jnp.sum(w, axis=1, keepdims=True)
        att = dot(w.astype(BF), v, 1, 0) / den
        dan = jnp.where(in_v, da / den, 0.0).astype(BF)
        dan_f = dan.astype(F32)
        delta = jnp.sum(dan_f * att, axis=1, keepdims=True)
        d_kernel = dot(dan, v, 1, 1) - delta
        ds = jnp.where(mask, d_kernel * (1.0 + s), 0.0).astype(BF)
        dq = dq + jnp.where(in_q, dot(ds, k, 1, 0) * (QK**-0.5), 0.0)
        dan_all = dan_all + dan_f
        high = delta.astype(BF).astype(F32)
        extra = extra + jnp.where(lane == h, high, 0.0)
        extra = extra + jnp.where(lane == heads + h, delta - high, 0.0)
    dq_ref[0] = dq.astype(BF)
    dan_ref[0] = dan_all.astype(BF)
    extra_ref[0] = extra.astype(BF)


def key_back_kernel(scal_ref, place_ref, k_ref, v_ref, q_ref, dan_ref, extra_ref, dk_ref, dv_ref):
    k, v = k_ref[0], v_ref[0]
    q, dan, extra = q_ref[0], dan_ref[0], extra_ref[0]
    tok = k.shape[0]
    mask = key_mask(scal_ref, place_ref, tok, pl.program_id(0))
    lane = lax.broadcasted_iota(jnp.int32, (tok, k.shape[1]), 1)
    heads = k.shape[1] // QK
    dk = jnp.zeros(k.shape, F32)
    dv = jnp.zeros(v.shape, F32)
    for h, (in_q, in_v) in enumerate(head_masks(k.shape[1], v.shape[1])):
        s = dot(jnp.where(in_q, k, jnp.zeros_like(k)), q, 1, 1) * (QK**-0.5)
        w = jnp.where(mask, 1.0 + s + 0.5 * s * s, 0.0).astype(BF)
        dv = dv + jnp.where(in_v, dot(w, dan, 1, 0), 0.0)
        pick = jnp.where((lane == h) | (lane == heads + h), 1.0, 0.0).astype(BF)
        d_kernel = dot(jnp.where(in_v, v, jnp.zeros_like(v)), dan, 1, 1) - dot(pick, extra, 1, 1)
        ds = jnp.where(mask, d_kernel * (1.0 + s), 0.0).astype(BF)
        dk = dk + jnp.where(in_q, dot(ds, q, 1, 0) * (QK**-0.5), 0.0)
    dk_ref[0] = dk.astype(BF)
    dv_ref[0] = dv.astype(BF)


class Exchange:
    def __init__(self, n, at, name, block, place):
        self.n, self.block, self.place = n, block, place
        self.send, self.recv = at[name + ".send"], at[name + ".recv"]
        self.me = lax.axis_index("seq")

    def copy(self, k):
        partner = lax.rem(self.me + k, self.n)
        return pltpu.make_async_remote_copy(
            src_ref=self.block(partner),
            dst_ref=self.place(self.me),
            send_sem=self.send.at[k],
            recv_sem=self.recv.at[k],
            device_id={"seq": partner},
            device_id_type=MESH,
        )

    def own(self):
        return pltpu.make_async_copy(self.block(self.me), self.place(self.me), self.send.at[0])

    def start(self):
        for k in range(1, self.n):
            self.copy(k).start()
        self.own().start()

    def wait(self):
        self.own().wait()
        for k in range(1, self.n):
            self.copy(k).wait_recv()

    def wait_sent(self):
        for k in range(1, self.n):
            self.copy(k).wait_send()


def to_pair(ref, features, tok):
    def block(partner):
        rows = pl.ds(pl.multiple_of(lax.rem(partner, 2) * features, 16), features)
        return ref.at[rows, pl.ds(pl.multiple_of((partner // 2) * tok, 128), tok)]

    return block


def at_positions(ref, tok):
    return lambda device: ref.at[:, pl.ds(pl.multiple_of(device * tok, 128), tok)]


def causal(offset, i, tok):
    shape = ((i + 1) * tok, tok)
    earlier = lax.broadcasted_iota(jnp.int32, shape, 0)
    pos = i * tok + lax.broadcasted_iota(jnp.int32, shape, 1)
    return (earlier <= pos) & ((earlier >= offset) | (pos < offset))


def attend_pairs(off, qkv, carried, call_id):
    n = lax.axis_size("seq")
    tok = qkv.shape[1] * 2 // n
    features = qkv.shape[0] // 2
    vf = features - 4 * QK
    call = Call(call_id)
    call.take("off", off, pltpu.SMEM)
    call.take("qkv", qkv)
    for j, a in enumerate(carried):
        call.gather_blocks(f"c{j}", a, j % 2 == 1)
    call.give("mixed", (2 * vf, qkv.shape[1]), BF)
    call.give("all", (features, n * tok), BF)
    call.give("att", (vf, n * tok), F32)
    call.give("den", (8, n * tok), F32)
    call.hold("own", (vf, n * tok), BF)
    call.exchange("in")
    call.exchange("out")

    def incoming(at):
        return Exchange(n, at, "in", to_pair(at["qkv"], features, tok), at_positions(at["all"], tok))

    def body(at, rings):
        def turn():
            for ring in rings.values():
                ring.step()

        turn()
        arriving = incoming(at)
        arriving.wait()
        turn()
        me = lax.axis_index("seq")
        offset = at["off"][me // 2]
        whole = at["all"]
        at["den"][...] = jnp.ones_like(at["den"])
        for h in range(2):
            lines = slice(h * vf // 2, (h + 1) * vf // 2)
            for i in range(n):
                here, upto = slice(i * tok, (i + 1) * tok), slice(0, (i + 1) * tok)
                q = whole[h * QK : (h + 1) * QK, here]
                k = whole[(2 + h) * QK : (3 + h) * QK, upto]
                v = whole[4 * QK + h * vf // 2 : 4 * QK + (h + 1) * vf // 2, upto]
                s = dot(k, q, 0, 0) * (QK**-0.5)
                w = jnp.where(causal(offset, i, tok), 1.0 + s + 0.5 * s * s, 0.0)
                den = jnp.sum(w, axis=0, keepdims=True)
                att = dot(v, w.astype(BF), 1, 0) / den
                at["att"][lines, here] = att
                at["den"][h : h + 1, here] = den
                at["own"][lines, here] = att.astype(BF)
        leaving = Exchange(
            n, at, "out", at_positions(at["own"], tok), lambda me: to_pair(at["mixed"], vf, tok)(me)
        )
        leaving.start()
        for _ in range(n // 2):
            turn()
        arriving.wait_sent()
        leaving.wait()
        leaving.wait_sent()

    out = call.run(body, lambda at: incoming(at).start())
    return out, [out[f"c{j}"] for j in range(len(carried))]


def attend_pairs_back(off, da, kept, scatters, call_id):
    n = lax.axis_size("seq")
    whole = kept["all"]
    features, tok = whole.shape[0], whole.shape[1] // n
    vf = features - 4 * QK
    call = Call(call_id)
    call.take("off", off, pltpu.SMEM)
    call.take("da", da)
    for name in ("all", "att", "den"):
        call.take(name, kept[name])
    lefts, pairs = scatters
    for i, a in enumerate(lefts):
        call.left(f"left{i}", a)
    for j, (i, right) in enumerate(pairs):
        call.scatter(f"s{j}", f"left{i}", right, j % 2 == 1)
    call.give("d", (2 * features, da.shape[1]), BF)
    call.hold("da_all", (vf, n * tok), BF)
    call.hold("sum", (2 * QK + vf, n * tok), F32)
    call.hold("own", (features, n * tok), BF)
    call.exchange("in")
    call.exchange("out")

    def incoming(at):
        return Exchange(n, at, "in", to_pair(at["da"], vf, tok), at_positions(at["da_all"], tok))

    def body(at, rings):
        arriving = incoming(at)
        arriving.wait()
        me = lax.axis_index("seq")
        offset = at["off"][me // 2]
        whole = at["all"]
        total = at["sum"]
        for h in range(2):
            lines = slice(h * vf // 2, (h + 1) * vf // 2)
            k_lines = slice(h * QK, (h + 1) * QK)
            v_lines = slice(2 * QK + h * vf // 2, 2 * QK + (h + 1) * vf // 2)
            for i in range(n - 1, -1, -1):
                here, upto = slice(i * tok, (i + 1) * tok), slice(0, (i + 1) * tok)
                q = whole[h * QK : (h + 1) * QK, here]
                k = whole[(2 + h) * QK : (3 + h) * QK, upto]
                v = whole[4 * QK + h * vf // 2 : 4 * QK + (h + 1) * vf // 2, upto]
                mask = causal(offset, i, tok)
                s = dot(k, q, 0, 0) * (QK**-0.5)
                w = jnp.where(mask, 1.0 + s + 0.5 * s * s, 0.0).astype(BF)
                dan = (at["da_all"][lines, here].astype(F32) / at["den"][h : h + 1, here]).astype(BF)
                delta = jnp.sum(dan.astype(F32) * at["att"][lines, here], axis=0, keepdims=True)
                ds = jnp.where(mask, (dot(v, dan, 0, 0) - delta) * (1.0 + s), 0.0).astype(BF)
                dq = dot(k, ds, 1, 0) * (QK**-0.5)
                at["own"][h * QK : (h + 1) * QK, here] = dq.astype(BF)
                dk = dot(q, ds, 1, 1) * (QK**-0.5)
                dv = dot(dan, w, 1, 1)
                if i == n - 1:
                    total[k_lines, upto] = dk
                    total[v_lines, upto] = dv
                else:
                    total[k_lines, upto] += dk
                    total[v_lines, upto] += dv
            if h == 0:
                for ring in rings.values():
                    ring.step()
        at["own"][2 * QK :, :] = total[...].astype(BF)
        leaving = Exchange(
            n, at, "out", at_positions(at["own"], tok), lambda me: to_pair(at["d"], features, tok)(me)
        )
        leaving.start()
        for _ in range(n // 2):
            for ring in rings.values():
                ring.step()
        arriving.wait_sent()
        leaving.wait()
        leaving.wait_sent()

    out = call.run(body, lambda at: incoming(at).start())
    return out["d"], [out[f"s{j}"] for j in range(len(pairs))]


def by_rows(kernel, scal, place, operands, widths, kinds):
    rows = operands[0].shape[0]
    tok = operands[0].shape[1]
    specs = [
        pl.BlockSpec(memory_space=pltpu.SMEM),
        pl.BlockSpec(place.shape, lambda r: (0, 0)),
    ]
    specs += [pl.BlockSpec((1,) + a.shape[1:], lambda r: (r, 0, 0)) for a in operands]
    return pl.pallas_call(
        kernel,
        grid=(rows,),
        in_specs=specs,
        out_specs=[pl.BlockSpec((1, tok, w), lambda r: (r, 0, 0)) for w in widths],
        out_shape=[jax.ShapeDtypeStruct((rows, tok, w), t) for w, t in zip(widths, kinds)],
        compiler_params=pltpu.CompilerParams(vmem_limit_bytes=48 * 1024 * 1024),
    )(scal, place, *operands)


def rms_scale(x):
    return lax.rsqrt(jnp.mean(x * x, axis=-1, keepdims=True) + EPSILON)


def rms_norm(x, gain):
    return x * rms_scale(x) * gain


def rms_back(x, gain, dn):
    scale = rms_scale(x)
    unit = x * scale
    gain_grad = jnp.sum(dn * unit, axis=0)
    dg = dn * gain
    dx = scale * (dg - unit * jnp.mean(dg * unit, axis=-1, keepdims=True))
    return dx, gain_grad


def head_total(partial_sum):
    return lax.psum(partial_sum, "head").astype(F32)


def tie(xs, *others):
    return list(lax.optimization_barrier((tuple(xs), tuple(others)))[0])


def mlp_forward(resid, gain, weights):
    gate_w, up_w, down_t = weights
    normed = rms_norm(resid, gain).astype(BF)
    gate_val = dot(normed, gate_w, 1, 0)
    up_val = dot(normed, up_w, 1, 0)
    hidden = (gate_val * jax.nn.sigmoid(gate_val) * up_val).astype(BF)
    return dot(hidden, down_t, 1, 1).astype(BF), (normed, gate_val, up_val, hidden)


def mlp_scatter(kept, call_id, *others):
    (normed, grad_b), d_gate, d_up, hidden = kept
    normed, grad_b = tie((normed, grad_b), *others)
    return scatter_all((normed, grad_b), ((0, d_gate), (0, d_up), (1, hidden)), call_id)


def mlp_backward(grad_b, saved, weights):
    gate_w, up_w, down_t = weights
    normed, gate_val, up_val, hidden = saved
    dh = dot(grad_b, down_t, 1, 0)
    sig = jax.nn.sigmoid(gate_val)
    silu = gate_val * sig
    d_gate = (dh * up_val * (sig * (1.0 + gate_val * (1.0 - sig)))).astype(BF)
    d_up = (dh * silu).astype(BF)
    dn_part = (dot(d_gate, gate_w, 1, 1) + dot(d_up, up_w, 1, 1)).astype(BF)
    return dn_part, ((normed, grad_b), d_gate, d_up, hidden)


def shifted(block, before, shift):
    if shift == 0:
        return block
    return jnp.concatenate([before[:, before.shape[1] - shift :], block[:, :-shift]], axis=1)


def advanced(block, after, shift):
    if shift == 0:
        return block
    return jnp.concatenate([block[:, shift:], after[:, :shift]], axis=1)


def per_device(
    activations,
    offsets,
    cotangent,
    attn_query,
    attn_key,
    attn_value,
    attn_output,
    ffn1_gate,
    ffn1_up,
    ffn1_down,
    conv_input,
    conv_gate,
    conv_output,
    conv_kernel,
    ffn2_gate,
    ffn2_up,
    ffn2_down,
    norm_gains,
):
    n = lax.axis_size("seq")
    micro, row_count, tok, width = activations.shape
    rows = micro * row_count
    count = rows * tok
    qw, vw = attn_query.shape[1], attn_value.shape[1]
    cw = conv_input.shape[1]
    taps = conv_kernel.shape[0]
    here = lax.axis_index("seq")
    start = here * tok
    off = offsets.reshape(rows)

    paired = ring_size(n) and 2 * rows == n and qw == 4 * QK
    if paired:
        halves = [
            a[:, g * a.shape[1] // 2 : (g + 1) * a.shape[1] // 2]
            for g in range(2)
            for a in (attn_query, attn_key, attn_value)
        ]
        qkv_s = jnp.concatenate(halves, axis=1)
    else:
        qkv_s = jnp.concatenate([attn_query, attn_key, attn_value], axis=1)
    gains = norm_gains.astype(F32)
    kernel_f = conv_kernel.astype(F32)
    inputs = activations.reshape(count, width).astype(F32)
    grad_four = cotangent.reshape(count, width)
    outs_s = jnp.concatenate([attn_output.T, conv_output.T], axis=1)
    (qkv_w,) = gather_all([qkv_s], 1)

    scal = jnp.concatenate([start[None].astype(jnp.int32), off])
    place = jnp.arange(n * tok, dtype=jnp.int32).reshape(1, n * tok)
    normed_a = rms_norm(inputs, gains[0]).astype(BF)

    def by_sequence(blocks):
        return jnp.swapaxes(blocks.reshape(n, rows, tok, -1), 0, 1).reshape(rows, n * tok, -1)

    if paired:
        qkv = dot(qkv_w, normed_a, 0, 1).astype(BF)
        attention, (outs_t, gate_1) = attend_pairs(off, qkv, (outs_s, ffn1_gate), 2)
        mixed, mixed_axis = attention["mixed"], 1
    else:
        qkv = dot(normed_a, qkv_w, 1, 0).astype(BF)
        qkv_all = by_sequence(gather_all([qkv], 2)[0])
        own = qkv.reshape(rows, tok, -1)
        q_own, k_own, v_own = own[..., :qw], own[..., qw : 2 * qw], own[..., 2 * qw :]
        q_all, k_all, v_all = qkv_all[..., :qw], qkv_all[..., qw : 2 * qw], qkv_all[..., 2 * qw :]
        (mixed,) = by_rows(attend_kernel, scal, place, (q_own, k_all, v_all), (vw,), (BF,))
        mixed, mixed_axis = mixed.reshape(count, vw), 0
        outs_t, gate_1 = gather_all((outs_s, ffn1_gate), 11)
    out_t, conv_out_t = outs_t[:, :vw], outs_t[:, vw:]
    attn_part = dot(mixed, out_t, 1 - mixed_axis, 1).astype(BF)
    attn_sum = head_total(attn_part)
    ffn1 = [gate_1] + gather_all(tie((ffn1_up, ffn1_down.T), attn_part), 12)
    resid_one = inputs + attn_sum
    part, kept_one = mlp_forward(resid_one, gains[1], ffn1)
    ffn1_sum = head_total(part)
    inner_w, gate_w, gate_2 = gather_all(tie((conv_input, conv_gate, ffn2_gate), part), 4)
    resid_two = resid_one + ffn1_sum

    normed_c = rms_norm(resid_two, gains[2]).astype(BF)
    inner = dot(normed_c, inner_w, 1, 0).reshape(rows, tok, cw)
    gate_c = dot(normed_c, gate_w, 1, 0).reshape(rows, tok, cw)
    pos = start + jnp.arange(tok + taps - 1, dtype=jnp.int32)
    current = pos[None, :] >= off[:, None]

    def valid(t, first, length):
        p = pos[None, first : first + length]
        source = p - t
        same = (source >= off[:, None]) == current[:, first : first + length]
        return ((source >= 0) & same).astype(F32)[:, :, None]

    edge = lax.ppermute(inner[:, tok - (taps - 1) :], "seq", [(i, i + 1) for i in range(n - 1)])
    moved = [shifted(inner, edge, t) * valid(t, 0, tok) for t in range(taps)]
    conv = sum(kernel_f[t][None, None, :] * moved[t] for t in range(taps))
    product = (conv * gate_c).astype(BF).reshape(count, cw)
    conv_part = dot(product, conv_out_t, 1, 1).astype(BF)
    conv_sum = head_total(conv_part)
    ffn2 = [gate_2] + gather_all(tie((ffn2_up, ffn2_down.T), conv_part), 12)
    resid_three = resid_two + conv_sum
    out_part, kept_two = mlp_forward(resid_three, gains[3], ffn2)

    dn_part, grads_two = mlp_backward(grad_four, kept_two, ffn2)
    both = lax.psum(jnp.concatenate([dn_part, out_part]), "head")
    dn, out_sum = both[:count].astype(F32), both[count:]
    sums_two = mlp_scatter(grads_two, 5, dn_part, out_part)
    (dn,) = tie((dn,), *sums_two)
    block_output = (resid_three + out_sum.astype(F32)).astype(BF).reshape(activations.shape)
    dx, gain_four = rms_back(resid_three, gains[3], dn)
    grad_three = grad_four.astype(F32) + dx
    grad_b = grad_three.astype(BF)
    d_product = dot(grad_b, conv_out_t, 1, 0).reshape(rows, tok, cw)
    d_gate_c = (d_product * conv).astype(BF).reshape(count, cw)
    d_conv = d_product * gate_c
    next_rows = lax.ppermute(d_conv[:, : taps - 1], "seq", [(i + 1, i) for i in range(n - 1)])
    d_inner = sum(
        kernel_f[t][None, None, :] * advanced(d_conv, next_rows, t) * valid(t, t, tok)
        for t in range(taps)
    )
    d_inner = d_inner.astype(BF).reshape(count, cw)
    kernel_grad = jnp.stack([jnp.sum(d_conv * moved[t], axis=(0, 1)) for t in range(taps)])
    dn_part = (dot(d_inner, inner_w, 1, 1) + dot(d_gate_c, gate_w, 1, 1)).astype(BF)
    dn = head_total(dn_part)
    sums_conv = scatter_all(
        tie((normed_c, grad_b), dn_part),
        ((0, d_inner), (0, d_gate_c), (1, product)),
        6,
        1,
    )
    (dn,) = tie((dn,), *sums_conv)
    dx, gain_three = rms_back(resid_two, gains[2], dn)
    grad_two = grad_three + dx
    dn_part, grads_one = mlp_backward(grad_two.astype(BF), kept_one, ffn1)
    dn = head_total(dn_part)
    (normed_1, grad_b1), d_gate_1, d_up_1, hidden_1 = grads_one
    if ring_size(n):
        sums_one = scatter_all(tie((normed_1,), dn_part), ((0, d_gate_1),), 9)
        (dn,) = tie((dn,), *sums_one)
    dx, gain_two = rms_back(resid_one, gains[1], dn)
    grad_one = grad_two + dx

    grad_b = grad_one.astype(BF)
    later = ((normed_1, grad_b1), ((0, d_up_1), (1, hidden_1)))
    if paired:
        da = dot(out_t, grad_b, 0, 1).astype(BF)
        d_qkv, more = attend_pairs_back(off, da, attention, later, 7)
        sums_one = sums_one + more
    else:
        da = dot(grad_b, out_t, 1, 0).reshape(rows, tok, vw)
        dq, dan, extra = by_rows(
            query_back_kernel, scal, place, (q_own, k_all, v_all, da), (qw, vw, qw), (BF, BF, BF)
        )
        back = jnp.concatenate([dan, extra], axis=-1).reshape(count, vw + qw)
        back_all = by_sequence(gather_all([back], 7, 1)[0])
        dk, dv = by_rows(
            key_back_kernel,
            scal,
            place,
            (k_own, v_own, q_all, back_all[..., :vw], back_all[..., vw:]),
            (qw, vw),
            (BF, BF),
        )
        sums_one = scatter_all((normed_1,), ((0, d_gate_1),), 9) + scatter_all(*later, 10)
        d_qkv = jnp.concatenate([dq, dk, dv], axis=-1).reshape(count, 2 * qw + vw)
    dn_part = dot(d_qkv, qkv_w, 1 - mixed_axis, 1).astype(BF)
    dn = head_total(dn_part)
    unit = inputs * rms_scale(inputs)
    gain_one = small_sum(jnp.sum(dn_part.astype(F32) * unit, axis=0), "head")
    small = jnp.concatenate(
        [
            jnp.stack([gain_one, gain_two, gain_three, gain_four]),
            jnp.pad(kernel_grad, ((0, 0), (0, width - cw))),
            jnp.zeros((8 - 4 - taps, width), F32),
        ]
    )
    if paired:
        d_qkv, mixed = d_qkv.T, mixed.T
    sums_attn = scatter_all(
        tie((normed_a, grad_b), dn_part), ((0, d_qkv), (1, mixed)), 8, 0, small
    )
    gains_grad, kernel_grad = sums_attn[2][:4], sums_attn[2][4 : 4 + taps, :cw]
    qkv_sum = sums_attn[0]
    if paired:
        edges = (0, qw // 2, qw, qw + vw // 2)
        step = qw + vw // 2
        query_sum, key_sum, value_sum = (
            jnp.concatenate([qkv_sum[:, g * step + a : g * step + b] for g in range(2)], axis=1)
            for a, b in zip(edges[:-1], edges[1:])
        )
    else:
        query_sum, key_sum = qkv_sum[:, :qw], qkv_sum[:, qw : 2 * qw]
        value_sum = qkv_sum[:, 2 * qw :]
    (dn,) = tie((dn,), *sums_attn)
    dx, _ = rms_back(inputs, gains[0], dn)
    input_grad = (grad_one + dx).reshape(activations.shape)

    return (
        block_output,
        input_grad,
        query_sum,
        key_sum,
        value_sum,
        sums_attn[1].T,
        sums_one[0],
        sums_one[1],
        sums_one[2].T,
        sums_conv[0],
        sums_conv[1],
        sums_conv[2].T,
        kernel_grad,
        sums_two[0],
        sums_two[1],
        sums_two[2].T,
        gains_grad,
    )


def solution(mesh):
    rows_in = P("seq", "head")
    rows_out = P("head", "seq")
    tokens = P(None, None, "seq", None)
    in_specs = (
        (tokens, P(), tokens)
        + (rows_in, rows_in, rows_in, rows_out)
        + (rows_in, rows_in, rows_out)
        + (rows_in, rows_in, rows_out)
        + (P(None, "head"),)
        + (rows_in, rows_in, rows_out)
        + (P(),)
    )
    out_specs = (
        (tokens, tokens)
        + (rows_in, rows_in, rows_in, rows_out)
        + (rows_in, rows_in, rows_out)
        + (rows_in, rows_in, rows_out)
        + (P(None, "head"),)
        + (rows_in, rows_in, rows_out)
        + (P(),)
    )
    return jax.shard_map(
        per_device, mesh=mesh, in_specs=in_specs, out_specs=out_specs, check_vma=False
    )
```

```python
from functools import partial

import jax
import jax.numpy as jnp
from jax import lax
from jax.experimental import pallas as pl
from jax.experimental.pallas import tpu as pltpu
from jax.sharding import PartitionSpec as P

QK = 16
VH = 112
EPSILON = 1e-05
BF = jnp.bfloat16
F32 = jnp.float32


MESH = pl.DeviceIdType.MESH
ANY = pl.BlockSpec(memory_space=pl.ANY)


def ring_device(p):
    return jnp.where(p < 4, 2 * p, 15 - 2 * p)


def ring_position(s):
    return jnp.where(lax.rem(s, 2) == 0, s // 2, 7 - s // 2)


def ring_size(n):
    return n == 8


def greet(n, everyone=False):
    me = lax.axis_index("seq")
    pos = ring_position(me)
    right = ring_device(lax.rem(pos + 1, n))
    left = ring_device(lax.rem(pos + n - 1, n))
    barrier = pltpu.get_barrier_semaphore()
    partners = [lax.rem(me + k, n) for k in range(1, n)] if everyone else [left, right]
    for partner in partners:
        pl.semaphore_signal(barrier, inc=1, device_id={"seq": partner}, device_id_type=MESH)
    pl.semaphore_wait(barrier, len(partners))
    return pos, right, left


class GatherRing:
    def __init__(self, n, where, src, out, place, send, recv, local, flip):
        self.n, self.src, self.out, self.place = n, src, out, place
        self.send, self.recv, self.local = send, recv, local
        self.pos, self.right, self.left = where
        self.flip = flip
        self.steps = n // 2
        self.done = 0

    def block(self, r):
        return self.place(self.out, ring_device(lax.rem(self.pos + (r % self.n), self.n)))

    def copy(self, k, d):
        block = self.block(-d * (k - 1))
        i = 0 if d == 1 else 1
        return pltpu.make_async_remote_copy(
            src_ref=self.src if k == 1 else block,
            dst_ref=block,
            send_sem=self.send.at[i, k - 1],
            recv_sem=self.recv.at[i, k - 1],
            device_id={"seq": self.right if d == 1 else self.left},
            device_id_type=MESH,
        )

    def ways(self, k):
        if k <= (self.n - 1) // 2:
            return (1, -1)
        return (-1,) if self.flip else (1,)

    def step(self):
        if self.done == self.steps:
            return
        if self.done == 0:
            pltpu.make_async_copy(self.src, self.block(0), self.local).start()
        self.done += 1
        k = self.done
        for d in self.ways(k):
            if k > 1:
                self.copy(k - 1, d).wait_recv()
            self.copy(k, d).start()

    def finish(self):
        while self.done < self.steps:
            self.step()
        pltpu.make_async_copy(self.src, self.block(0), self.local).wait()
        last = {d: max(k for k in range(1, self.steps + 1) if d in self.ways(k)) for d in (1, -1)}
        for d in (1, -1):
            self.copy(last[d], d).wait_recv()
        for k in range(1, self.steps + 1):
            for d in self.ways(k):
                self.copy(k, d).wait_send()


def by_block(height, first=0, rows=None):
    rows = height if rows is None else rows
    unit = 8 if height % 16 else 16
    return lambda ref, owner: ref.at[pl.ds(pl.multiple_of(owner * height + first, unit), rows)]


def by_position(tok):
    return lambda ref, owner: ref.at[:, pl.ds(pl.multiple_of(owner * tok, 16), tok)]


VMEM = pltpu.VMEM
MIB = 1024 * 1024


class Call:
    def __init__(self, call_id):
        self.n = lax.axis_size("seq")
        self.call_id = call_id
        self.ins, self.outs, self.scratch = {}, {}, {}
        self.gathers, self.scatters = {}, {}
        self.exchanges = []

    def exchange(self, name):
        self.sems(name + ".send", self.n)
        self.sems(name + ".recv", self.n)
        self.exchanges.append(name)

    def take(self, name, array, space=VMEM):
        self.ins[name] = (array, pl.BlockSpec(memory_space=space))
        return name

    def give(self, name, shape, kind, space=VMEM):
        self.outs[name] = (jax.ShapeDtypeStruct(shape, kind), pl.BlockSpec(memory_space=space))
        return name

    def hold(self, name, shape, kind):
        self.scratch[name] = VMEM(shape, kind)
        return name

    def sems(self, name, *shape):
        self.scratch[name] = pltpu.SemaphoreType.DMA(shape)

    def gather_blocks(self, name, array, flip=False):
        height = array.shape[0]
        self.take(name + ".src", array, pl.ANY)
        self.give(name, (self.n * height,) + array.shape[1:], array.dtype, pl.ANY)
        half = height // 2
        for p in range(2):
            self.gather(
                f"{name}.{p}",
                name + ".src",
                name,
                by_block(height, p * half, half),
                bool(p) != flip,
                (p * half, half),
            )

    def gather(self, name, src, out, place, flip=False, rows=None):
        half = self.n // 2
        self.sems(name + ".send", 2, half)
        self.sems(name + ".recv", 2, half)
        self.sems(name + ".local", 1)
        self.gathers[name] = (src, out, place, flip, rows)

    def left(self, name, array):
        self.take(name, array)
        rows, width = array.shape
        self.hold(name + ".blocked", (self.n, rows, width // self.n), BF)

    def scatter(self, name, left, right, flip=False, axis=0):
        n = self.n
        height = self.ins[left][0].shape[1] // n
        width = right.shape[1 - axis]
        self.take(name + ".right", right)
        self.give(name, (height, width), F32)
        cut = -(-width // 256) * 128
        for p, span in enumerate(((0, cut), (cut, width))):
            part = f"{name}.{p}"
            block = (height, span[1] - span[0])
            self.hold(part + ".sums", (2, n // 2) + block, BF)
            self.hold(part + ".slots", (2, n // 2) + block, BF)
            self.sems(part + ".send", 2, n // 2)
            self.sems(part + ".recv", 2, n // 2)
            self.scatters[part] = (name, left, bool(p) != flip, axis, span)

    def kernel(self, body, *refs):
        names = list(self.ins) + list(self.outs) + list(self.scratch)
        at = dict(zip(names, refs))
        where = greet(self.n, bool(self.exchanges))
        rings = {}
        for name, (src, out, place, flip, rows) in self.gathers.items():
            rings[name] = GatherRing(
                self.n,
                where,
                at[src] if rows is None else at[src].at[pl.ds(*rows)],
                at[out],
                place,
                at[name + ".send"],
                at[name + ".recv"],
                at[name + ".local"].at[0],
                flip,
            )
        ready = set()
        for name, (whole, left, flip, axis, span) in self.scatters.items():
            blocked = at[left + ".blocked"]
            if left not in ready:
                ready.add(left)
                width = blocked.shape[2]
                for b in range(self.n):
                    blocked[b] = at[left][:, b * width : (b + 1) * width]
            rings[name] = ScatterRing(
                self.n,
                where,
                blocked,
                at[whole + ".right"],
                at[whole],
                at[name + ".sums"],
                at[name + ".slots"],
                at[name + ".send"],
                at[name + ".recv"],
                flip,
                axis,
                span,
            )
            rings[name].step()
        body(at, rings)
        for ring in rings.values():
            ring.finish()

    def run(self, body):
        outs = pl.pallas_call(
            partial(self.kernel, body),
            in_specs=[spec for _, spec in self.ins.values()],
            out_specs=[spec for _, spec in self.outs.values()],
            out_shape=[shape for shape, _ in self.outs.values()],
            scratch_shapes=list(self.scratch.values()),
            compiler_params=pltpu.CompilerParams(
                collective_id=self.call_id, has_side_effects=True, vmem_limit_bytes=58 * MIB
            ),
        )(*[array for array, _ in self.ins.values()])
        return dict(zip(self.outs, outs))


def in_turn(n):
    def body(at, rings):
        for _ in range(n // 2):
            for ring in rings.values():
                ring.step()

    return body


def gather_all(arrays, call_id, flip=0):
    n = lax.axis_size("seq")
    if not ring_size(n):
        return [lax.all_gather(a, "seq", axis=0, tiled=True) for a in arrays]
    call = Call(call_id)
    names = [str(j) for j in range(len(arrays))]
    for j, (name, a) in enumerate(zip(names, arrays)):
        call.gather_blocks(name, a, (j + flip) % 2 == 1)
    out = call.run(in_turn(n))
    return [out[name] for name in names]


def gather_beside_norm(x, gain, array, call_id):
    n = lax.axis_size("seq")
    if not ring_size(n):
        normed = rms_norm(x.astype(F32), gain[0]).astype(BF)
        return normed, lax.all_gather(array, "seq", axis=0, tiled=True)
    call = Call(call_id)
    call.take("x", x)
    call.take("gain", gain)
    call.give("normed", x.shape, BF)
    call.gather_blocks("w", array)
    rows = x.shape[0] // n

    def body(at, rings):
        for k in range(n):
            if k % 2 == 0:
                for ring in rings.values():
                    ring.step()
            lines = slice(k * rows, (k + 1) * rows)
            at["normed"][lines] = rms_norm(at["x"][lines].astype(F32), at["gain"][...]).astype(BF)

    out = call.run(body)
    return out["normed"], out["w"]


class ScatterRing:
    def __init__(self, n, where, left, right, out, sums, slots, send, recv, flip, axis, span):
        self.axis, self.span = axis, slice(*span)
        self.n, self.left_ref, self.right_ref, self.out = n, left, right, out
        self.sums, self.slots, self.send, self.recv = sums, slots, send, recv
        self.pos, self.right, self.left = where
        d = -1 if flip else 1
        self.hops = {d: n // 2, -d: (n - 1) // 2}
        self.order = (d, -d)
        self.done = 0
        self.steps = n // 2

    def term(self, r):
        owner = ring_device(lax.rem(self.pos + (r % self.n), self.n))
        right = self.right_ref[:, self.span] if self.axis == 0 else self.right_ref[self.span]
        return dot(self.left_ref[owner], right, 0, self.axis)

    def copy(self, d, h):
        i = 0 if d == 1 else 1
        return pltpu.make_async_remote_copy(
            src_ref=self.sums.at[i, h - 1],
            dst_ref=self.slots.at[i, h - 1],
            send_sem=self.send.at[i, h - 1],
            recv_sem=self.recv.at[i, h - 1],
            device_id={"seq": self.right if d == 1 else self.left},
            device_id_type=MESH,
        )

    def step(self):
        if self.done == self.steps:
            return
        self.done += 1
        h = self.done
        for d in self.order:
            if h > self.hops[d]:
                continue
            i = 0 if d == 1 else 1
            total = self.term(d * (self.hops[d] - h + 1))
            if h > 1:
                self.copy(d, h - 1).wait_recv()
                total = total + self.slots[i, h - 2].astype(F32)
            self.sums[i, h - 1] = total.astype(BF)
            self.copy(d, h).start()

    def finish(self):
        while self.done < self.steps:
            self.step()
        total = self.term(0)
        for d in self.order:
            i, h = (0 if d == 1 else 1), self.hops[d]
            self.copy(d, h).wait_recv()
            total = total + self.slots[i, h - 1].astype(F32)
        self.out[:, self.span] = total
        for d in self.order:
            for h in range(1, self.hops[d] + 1):
                self.copy(d, h).wait_send()


def scatter_all(lefts, pairs, call_id, flip=0, small=None, after=()):
    n = lax.axis_size("seq")
    pairs = [p if len(p) == 3 else p + (0,) for p in pairs]
    if not ring_size(n):
        sums = [
            lax.psum_scatter(
                dot(lefts[i], right, 0, axis).astype(BF), "seq", scatter_dimension=0, tiled=True
            ).astype(F32)
            for i, right, axis in pairs
        ]
        return sums if small is None else sums + [lax.psum(small.astype(BF), "seq").astype(F32)]
    call = Call(call_id)
    names = [str(j) for j in range(len(pairs))]
    for j, a in enumerate(after):
        call.take(f"after{j}", a, pl.ANY)
    if small is not None:
        call.take("small.src", small)
        call.hold("small.all", (n * small.shape[0], small.shape[1]), F32)
        call.gather("small", "small.src", "small.all", by_block(small.shape[0]))
    for i, a in enumerate(lefts):
        call.left(f"left{i}", a)
    for j, (i, right, axis) in enumerate(pairs):
        call.scatter(names[j], f"left{i}", right, (j + flip) % 2 == 1, axis)
    if small is not None:
        names.append(call.give("small.sum", small.shape, F32))

    def body(at, rings):
        in_turn(n)(at, rings)
        if small is not None:
            rings["small"].finish()
            rows = small.shape[0]
            blocks = [at["small.all"][b * rows : (b + 1) * rows] for b in range(n)]
            at["small.sum"][...] = sum(blocks[1:], blocks[0])
            del rings["small"]

    out = call.run(body)
    return [out[name] for name in names]


def small_sum(x, axis):
    size = lax.axis_size(axis)
    if size > 8:
        return lax.psum(x.astype(BF), axis).astype(F32)
    sent = x.astype(BF)
    routes = [[(i, (i + k) % size) for i in range(size)] for k in range(1, size)]
    return x + sum(lax.ppermute(sent, axis, r).astype(F32) for r in routes)


def dot(a, b, ca, cb):
    return lax.dot_general(a, b, (((ca,), (cb,)), ((), ())), preferred_element_type=F32)


def head_masks(query_width, value_width):
    lane_q = lax.broadcasted_iota(jnp.int32, (1, query_width), 1)
    lane_v = lax.broadcasted_iota(jnp.int32, (1, value_width), 1)
    heads = query_width // QK
    return [
        (
            (lane_q >= h * QK) & (lane_q < (h + 1) * QK),
            (lane_v >= h * VH) & (lane_v < (h + 1) * VH),
        )
        for h in range(heads)
    ]


def query_mask(scal_ref, place_ref, tok, row):
    offset = scal_ref[1 + row]
    pos = scal_ref[0] + lax.broadcasted_iota(jnp.int32, (tok, 1), 0)
    low = jnp.where(pos >= offset, offset, 0)
    other = place_ref[...]
    return (other >= low) & (other <= pos)


def key_mask(scal_ref, place_ref, tok, row):
    offset = scal_ref[1 + row]
    pos = scal_ref[0] + lax.broadcasted_iota(jnp.int32, (tok, 1), 0)
    high = jnp.where(pos >= offset, jnp.int32(1 << 30), offset)
    other = place_ref[...]
    return (other >= pos) & (other < high)


def attend_kernel(scal_ref, place_ref, q_ref, k_ref, v_ref, out_ref):
    q, k, v = q_ref[0], k_ref[0], v_ref[0]
    mask = query_mask(scal_ref, place_ref, q.shape[0], pl.program_id(0))
    total = jnp.zeros((q.shape[0], v.shape[1]), F32)
    for in_q, in_v in head_masks(q.shape[1], v.shape[1]):
        s = dot(jnp.where(in_q, q, jnp.zeros_like(q)), k, 1, 1) * (QK**-0.5)
        w = jnp.where(mask, 1.0 + s + 0.5 * s * s, 0.0)
        den = jnp.sum(w, axis=1, keepdims=True)
        total = total + jnp.where(in_v, dot(w.astype(BF), v, 1, 0) / den, 0.0)
    out_ref[0] = total.astype(BF)


def query_back_kernel(scal_ref, place_ref, q_ref, k_ref, v_ref, da_ref, dq_ref, dan_ref, extra_ref):
    q, k, v = q_ref[0], k_ref[0], v_ref[0]
    da = da_ref[0]
    tok = q.shape[0]
    mask = query_mask(scal_ref, place_ref, tok, pl.program_id(0))
    lane = lax.broadcasted_iota(jnp.int32, (1, q.shape[1]), 1)
    heads = q.shape[1] // QK
    dq = jnp.zeros(q.shape, F32)
    dan_all = jnp.zeros(da.shape, F32)
    extra = jnp.zeros(q.shape, F32)
    for h, (in_q, in_v) in enumerate(head_masks(q.shape[1], v.shape[1])):
        s = dot(jnp.where(in_q, q, jnp.zeros_like(q)), k, 1, 1) * (QK**-0.5)
        w = jnp.where(mask, 1.0 + s + 0.5 * s * s, 0.0)
        den = jnp.sum(w, axis=1, keepdims=True)
        att = dot(w.astype(BF), v, 1, 0) / den
        dan = jnp.where(in_v, da / den, 0.0).astype(BF)
        dan_f = dan.astype(F32)
        delta = jnp.sum(dan_f * att, axis=1, keepdims=True)
        d_kernel = dot(dan, v, 1, 1) - delta
        ds = jnp.where(mask, d_kernel * (1.0 + s), 0.0).astype(BF)
        dq = dq + jnp.where(in_q, dot(ds, k, 1, 0) * (QK**-0.5), 0.0)
        dan_all = dan_all + dan_f
        high = delta.astype(BF).astype(F32)
        extra = extra + jnp.where(lane == h, high, 0.0)
        extra = extra + jnp.where(lane == heads + h, delta - high, 0.0)
    dq_ref[0] = dq.astype(BF)
    dan_ref[0] = dan_all.astype(BF)
    extra_ref[0] = extra.astype(BF)


def key_back_kernel(scal_ref, place_ref, k_ref, v_ref, q_ref, dan_ref, extra_ref, dk_ref, dv_ref):
    k, v = k_ref[0], v_ref[0]
    q, dan, extra = q_ref[0], dan_ref[0], extra_ref[0]
    tok = k.shape[0]
    mask = key_mask(scal_ref, place_ref, tok, pl.program_id(0))
    lane = lax.broadcasted_iota(jnp.int32, (tok, k.shape[1]), 1)
    heads = k.shape[1] // QK
    dk = jnp.zeros(k.shape, F32)
    dv = jnp.zeros(v.shape, F32)
    for h, (in_q, in_v) in enumerate(head_masks(k.shape[1], v.shape[1])):
        s = dot(jnp.where(in_q, k, jnp.zeros_like(k)), q, 1, 1) * (QK**-0.5)
        w = jnp.where(mask, 1.0 + s + 0.5 * s * s, 0.0).astype(BF)
        dv = dv + jnp.where(in_v, dot(w, dan, 1, 0), 0.0)
        pick = jnp.where((lane == h) | (lane == heads + h), 1.0, 0.0).astype(BF)
        d_kernel = dot(jnp.where(in_v, v, jnp.zeros_like(v)), dan, 1, 1) - dot(pick, extra, 1, 1)
        ds = jnp.where(mask, d_kernel * (1.0 + s), 0.0).astype(BF)
        dk = dk + jnp.where(in_q, dot(ds, q, 1, 0) * (QK**-0.5), 0.0)
    dk_ref[0] = dk.astype(BF)
    dv_ref[0] = dv.astype(BF)


class Exchange:
    def __init__(self, n, at, name, block, place):
        self.n, self.block, self.place = n, block, place
        self.send, self.recv = at[name + ".send"], at[name + ".recv"]
        self.me = lax.axis_index("seq")

    def copy(self, k):
        partner = lax.rem(self.me + k, self.n)
        return pltpu.make_async_remote_copy(
            src_ref=self.block(partner),
            dst_ref=self.place(self.me),
            send_sem=self.send.at[k],
            recv_sem=self.recv.at[k],
            device_id={"seq": partner},
            device_id_type=MESH,
        )

    def own(self):
        return pltpu.make_async_copy(self.block(self.me), self.place(self.me), self.send.at[0])

    def start(self):
        for k in range(1, self.n):
            self.copy(k).start()
        self.own().start()

    def wait(self):
        self.own().wait()
        for k in range(1, self.n):
            self.copy(k).wait_recv()

    def wait_sent(self):
        for k in range(1, self.n):
            self.copy(k).wait_send()


def to_pair(ref, features, tok):
    def block(partner):
        rows = pl.ds(pl.multiple_of(lax.rem(partner, 2) * features, 16), features)
        return ref.at[rows, pl.ds(pl.multiple_of((partner // 2) * tok, 128), tok)]

    return block


def at_positions(ref, tok):
    return lambda device: ref.at[:, pl.ds(pl.multiple_of(device * tok, 128), tok)]


def causal(offset, i, tok):
    shape = ((i + 1) * tok, tok)
    earlier = lax.broadcasted_iota(jnp.int32, shape, 0)
    pos = i * tok + lax.broadcasted_iota(jnp.int32, shape, 1)
    return (earlier <= pos) & ((earlier >= offset) | (pos < offset))


def attend_pairs(off, weight, normed, carried, call_id):
    n = lax.axis_size("seq")
    count = normed.shape[0]
    tok = count * 2 // n
    features = weight.shape[1] // 2
    vf = features - 4 * QK
    call = Call(call_id)
    call.take("off", off, pltpu.SMEM)
    call.take("weight", weight)
    call.take("normed", normed)
    call.hold("qkv", (2 * features, count), BF)
    call.hold("mixed_t", (2 * vf, count), BF)
    for j, a in enumerate(carried):
        call.gather_blocks(f"c{j}", a, j % 2 == 1)
    call.give("mixed", (count, 2 * vf), BF)
    call.give("all", (features, n * tok), BF)
    call.give("att", (vf, n * tok), F32)
    call.give("den", (8, n * tok), F32)
    call.hold("own", (vf, n * tok), BF)
    call.exchange("in")
    call.exchange("out")

    def incoming(at):
        return Exchange(n, at, "in", to_pair(at["qkv"], features, tok), at_positions(at["all"], tok))

    def body(at, rings):
        def turn():
            for ring in rings.values():
                ring.step()

        turn()
        half = count // 2
        for p in range(2):
            part = dot(at["normed"][p * half : (p + 1) * half], at["weight"][...], 1, 0)
            at["qkv"][:, p * half : (p + 1) * half] = part.T.astype(BF)
        arriving = incoming(at)
        arriving.start()
        arriving.wait()
        turn()
        me = lax.axis_index("seq")
        offset = at["off"][me // 2]
        whole = at["all"]
        at["den"][...] = jnp.ones_like(at["den"])
        for h in range(2):
            lines = slice(h * vf // 2, (h + 1) * vf // 2)
            for i in range(n):
                here, upto = slice(i * tok, (i + 1) * tok), slice(0, (i + 1) * tok)
                q = whole[h * QK : (h + 1) * QK, here]
                k = whole[(2 + h) * QK : (3 + h) * QK, upto]
                v = whole[4 * QK + h * vf // 2 : 4 * QK + (h + 1) * vf // 2, upto]
                s = dot(k, q, 0, 0) * (QK**-0.5)
                w = jnp.where(causal(offset, i, tok), 1.0 + s + 0.5 * s * s, 0.0)
                den = jnp.sum(w, axis=0, keepdims=True)
                att = dot(v, w.astype(BF), 1, 0) / den
                at["att"][lines, here] = att
                at["den"][h : h + 1, here] = den
                at["own"][lines, here] = att.astype(BF)
        leaving = Exchange(
            n, at, "out", at_positions(at["own"], tok), lambda me: to_pair(at["mixed_t"], vf, tok)(me)
        )
        leaving.start()
        for _ in range(n // 2):
            turn()
        arriving.wait_sent()
        leaving.wait()
        at["mixed"][...] = at["mixed_t"][...].astype(F32).T.astype(BF)
        leaving.wait_sent()

    out = call.run(body)
    return out, [out[f"c{j}"] for j in range(len(carried))]


def attend_pairs_back(off, grad, out_t, weight, kept, scatters, call_id):
    n = lax.axis_size("seq")
    whole = kept["all"]
    features, tok = whole.shape[0], whole.shape[1] // n
    vf = features - 4 * QK
    call = Call(call_id)
    call.take("off", off, pltpu.SMEM)
    call.take("grad", grad)
    call.take("out_t", out_t)
    call.take("weight", weight)
    count, width = grad.shape
    call.hold("da", (2 * vf, count), BF)
    for name in ("all", "att", "den"):
        call.take(name, kept[name])
    lefts, pairs = scatters
    for i, a in enumerate(lefts):
        call.left(f"left{i}", a)
    for j, (i, right) in enumerate(pairs):
        call.scatter(f"s{j}", f"left{i}", right, j % 2 == 1)
    call.give("d", (count, 2 * features), BF)
    call.give("part", (count, width), BF)
    call.hold("d_t", (2 * features, count), BF)
    call.hold("da_all", (vf, n * tok), BF)
    call.hold("sum", (2 * QK + vf, n * tok), F32)
    call.hold("own", (features, n * tok), BF)
    call.exchange("in")
    call.exchange("out")

    def incoming(at):
        return Exchange(n, at, "in", to_pair(at["da"], vf, tok), at_positions(at["da_all"], tok))

    def body(at, rings):
        half = count // 2
        for p in range(2):
            part = dot(at["grad"][p * half : (p + 1) * half], at["out_t"][:, : 2 * vf], 1, 0)
            at["da"][:, p * half : (p + 1) * half] = part.T.astype(BF)
        arriving = incoming(at)
        arriving.start()
        arriving.wait()
        for ring in rings.values():
            ring.step()
        me = lax.axis_index("seq")
        offset = at["off"][me // 2]
        whole = at["all"]
        total = at["sum"]
        for h in range(2):
            lines = slice(h * vf // 2, (h + 1) * vf // 2)
            k_lines = slice(h * QK, (h + 1) * QK)
            v_lines = slice(2 * QK + h * vf // 2, 2 * QK + (h + 1) * vf // 2)
            for i in range(n - 1, -1, -1):
                here, upto = slice(i * tok, (i + 1) * tok), slice(0, (i + 1) * tok)
                q = whole[h * QK : (h + 1) * QK, here]
                k = whole[(2 + h) * QK : (3 + h) * QK, upto]
                v = whole[4 * QK + h * vf // 2 : 4 * QK + (h + 1) * vf // 2, upto]
                mask = causal(offset, i, tok)
                s = dot(k, q, 0, 0) * (QK**-0.5)
                w = jnp.where(mask, 1.0 + s + 0.5 * s * s, 0.0).astype(BF)
                dan = (at["da_all"][lines, here].astype(F32) / at["den"][h : h + 1, here]).astype(BF)
                delta = jnp.sum(dan.astype(F32) * at["att"][lines, here], axis=0, keepdims=True)
                ds = jnp.where(mask, (dot(v, dan, 0, 0) - delta) * (1.0 + s), 0.0).astype(BF)
                dq = dot(k, ds, 1, 0) * (QK**-0.5)
                at["own"][h * QK : (h + 1) * QK, here] = dq.astype(BF)
                dk = dot(q, ds, 1, 1) * (QK**-0.5)
                dv = dot(dan, w, 1, 1)
                if i == n - 1:
                    total[k_lines, upto] = dk
                    total[v_lines, upto] = dv
                else:
                    total[k_lines, upto] += dk
                    total[v_lines, upto] += dv
        at["own"][2 * QK :, :] = total[...].astype(BF)
        leaving = Exchange(
            n, at, "out", at_positions(at["own"], tok), lambda me: to_pair(at["d_t"], features, tok)(me)
        )
        leaving.start()
        for ring in rings.values():
            ring.step()
        leaving.wait()
        at["d"][...] = at["d_t"][...].astype(F32).T.astype(BF)
        for j in range(width // 256):
            lines = slice(j * 256, (j + 1) * 256)
            at["part"][:, lines] = dot(at["d"][...], at["weight"][lines, :], 1, 1).astype(BF)
        for _ in range(n // 2):
            for ring in rings.values():
                ring.step()
        arriving.wait_sent()
        leaving.wait_sent()

    out = call.run(body)
    return out["d"], out["part"], [out[f"s{j}"] for j in range(len(pairs))]


def by_rows(kernel, scal, place, operands, widths, kinds):
    rows = operands[0].shape[0]
    tok = operands[0].shape[1]
    specs = [
        pl.BlockSpec(memory_space=pltpu.SMEM),
        pl.BlockSpec(place.shape, lambda r: (0, 0)),
    ]
    specs += [pl.BlockSpec((1,) + a.shape[1:], lambda r: (r, 0, 0)) for a in operands]
    return pl.pallas_call(
        kernel,
        grid=(rows,),
        in_specs=specs,
        out_specs=[pl.BlockSpec((1, tok, w), lambda r: (r, 0, 0)) for w in widths],
        out_shape=[jax.ShapeDtypeStruct((rows, tok, w), t) for w, t in zip(widths, kinds)],
        compiler_params=pltpu.CompilerParams(vmem_limit_bytes=48 * 1024 * 1024),
    )(scal, place, *operands)


def rms_scale(x):
    return lax.rsqrt(jnp.mean(x * x, axis=-1, keepdims=True) + EPSILON)


def rms_norm(x, gain):
    return x * rms_scale(x) * gain


def rms_back(x, gain, dn):
    scale = rms_scale(x)
    unit = x * scale
    gain_grad = jnp.sum(dn * unit, axis=0)
    dg = dn * gain
    dx = scale * (dg - unit * jnp.mean(dg * unit, axis=-1, keepdims=True))
    return dx, gain_grad


def closing_kernel(count, *refs):
    x_ref, dn_ref, grad_ref, gain_ref = refs[:4]
    srcs, out_ref, dsts = refs[4 : 4 + count], refs[4 + count], refs[5 + count :]
    dx, _ = rms_back(x_ref[...].astype(F32), gain_ref[...], dn_ref[...].astype(F32))
    out_ref[...] = grad_ref[...] + dx
    for src, dst in zip(srcs, dsts):
        dst[...] = src[...]


def closing(x, dn, grad, gain, results):
    steps = 4

    def rows(a):
        return pl.BlockSpec((a.shape[0] // steps, a.shape[1]), lambda i: (i, 0))

    whole = pl.BlockSpec(gain.shape, lambda i: (0, 0))
    shapes = [jax.ShapeDtypeStruct(x.shape, F32)]
    shapes += [jax.ShapeDtypeStruct(r.shape, r.dtype) for r in results]
    out = pl.pallas_call(
        partial(closing_kernel, len(results)),
        grid=(steps,),
        in_specs=[rows(x), rows(dn), rows(grad), whole] + [rows(r) for r in results],
        out_specs=[rows(a) for a in shapes],
        out_shape=shapes,
        compiler_params=pltpu.CompilerParams(vmem_limit_bytes=58 * MIB),
    )(x, dn, grad, gain, *results)
    return out[0], out[1:]


def head_total(partial_sum):
    return lax.psum(partial_sum, "head").astype(F32)


def tie(xs, *others):
    return list(lax.optimization_barrier((tuple(xs), tuple(others)))[0])


def mlp_forward(resid, gain, weights):
    gate_w, up_w, down_t = weights
    normed = rms_norm(resid, gain).astype(BF)
    gate_val = dot(normed, gate_w, 1, 0)
    up_val = dot(normed, up_w, 1, 0)
    hidden = (gate_val * jax.nn.sigmoid(gate_val) * up_val).astype(BF)
    return dot(hidden, down_t, 1, 1).astype(BF), (normed, gate_val, up_val, hidden)


def mlp_scatter(kept, call_id, *others):
    (normed, grad_b), d_gate, d_up, hidden = kept
    normed, grad_b = tie((normed, grad_b), *others)
    return scatter_all((normed, grad_b), ((0, d_gate), (0, d_up), (1, hidden)), call_id)


def mlp_backward(grad_b, saved, weights):
    gate_w, up_w, down_t = weights
    normed, gate_val, up_val, hidden = saved
    dh = dot(grad_b, down_t, 1, 0)
    sig = jax.nn.sigmoid(gate_val)
    silu = gate_val * sig
    d_gate = (dh * up_val * (sig * (1.0 + gate_val * (1.0 - sig)))).astype(BF)
    d_up = (dh * silu).astype(BF)
    dn_part = (dot(d_gate, gate_w, 1, 1) + dot(d_up, up_w, 1, 1)).astype(BF)
    return dn_part, ((normed, grad_b), d_gate, d_up, hidden)


def shifted(block, before, shift):
    if shift == 0:
        return block
    return jnp.concatenate([before[:, before.shape[1] - shift :], block[:, :-shift]], axis=1)


def advanced(block, after, shift):
    if shift == 0:
        return block
    return jnp.concatenate([block[:, shift:], after[:, :shift]], axis=1)


def per_device(
    activations,
    offsets,
    cotangent,
    attn_query,
    attn_key,
    attn_value,
    attn_output,
    ffn1_gate,
    ffn1_up,
    ffn1_down,
    conv_input,
    conv_gate,
    conv_output,
    conv_kernel,
    ffn2_gate,
    ffn2_up,
    ffn2_down,
    norm_gains,
):
    n = lax.axis_size("seq")
    micro, row_count, tok, width = activations.shape
    rows = micro * row_count
    count = rows * tok
    qw, vw = attn_query.shape[1], attn_value.shape[1]
    cw = conv_input.shape[1]
    taps = conv_kernel.shape[0]
    here = lax.axis_index("seq")
    start = here * tok
    off = offsets.reshape(rows)

    paired = ring_size(n) and 2 * rows == n and qw == 4 * QK
    if paired:
        halves = [
            a[:, g * a.shape[1] // 2 : (g + 1) * a.shape[1] // 2]
            for g in range(2)
            for a in (attn_query, attn_key, attn_value)
        ]
        qkv_s = jnp.concatenate(halves, axis=1)
    else:
        qkv_s = jnp.concatenate([attn_query, attn_key, attn_value], axis=1)
    gains = norm_gains.astype(F32)
    kernel_f = conv_kernel.astype(F32)
    acts_flat = activations.reshape(count, width)
    inputs = acts_flat.astype(F32)
    grad_four = cotangent.reshape(count, width)
    outs_s = jnp.concatenate([attn_output.T, conv_output.T], axis=1)
    normed_a, qkv_w = gather_beside_norm(acts_flat, gains[:1], qkv_s, 1)

    scal = jnp.concatenate([start[None].astype(jnp.int32), off])
    place = jnp.arange(n * tok, dtype=jnp.int32).reshape(1, n * tok)

    def by_sequence(blocks):
        return jnp.swapaxes(blocks.reshape(n, rows, tok, -1), 0, 1).reshape(rows, n * tok, -1)

    if paired:
        attention, (outs_t, gate_1) = attend_pairs(off, qkv_w, normed_a, (outs_s, ffn1_gate), 2)
        mixed = attention["mixed"]
    else:
        qkv = dot(normed_a, qkv_w, 1, 0).astype(BF)
        qkv_all = by_sequence(gather_all([qkv], 2)[0])
        own = qkv.reshape(rows, tok, -1)
        q_own, k_own, v_own = own[..., :qw], own[..., qw : 2 * qw], own[..., 2 * qw :]
        q_all, k_all, v_all = qkv_all[..., :qw], qkv_all[..., qw : 2 * qw], qkv_all[..., 2 * qw :]
        (mixed,) = by_rows(attend_kernel, scal, place, (q_own, k_all, v_all), (vw,), (BF,))
        mixed = mixed.reshape(count, vw)
        outs_t, gate_1 = gather_all((outs_s, ffn1_gate), 11)
    out_t, conv_out_t = outs_t[:, :vw], outs_t[:, vw:]
    attn_part = dot(mixed, out_t, 1, 1).astype(BF)
    attn_sum = head_total(attn_part)
    ffn1 = [gate_1] + gather_all(tie((ffn1_up, ffn1_down.T), attn_part), 12)
    resid_one = inputs + attn_sum
    part, kept_one = mlp_forward(resid_one, gains[1], ffn1)
    ffn1_sum = head_total(part)
    inner_w, gate_w, gate_2 = gather_all(tie((conv_input, conv_gate, ffn2_gate), part), 4)
    resid_two = resid_one + ffn1_sum

    normed_c = rms_norm(resid_two, gains[2]).astype(BF)
    inner = dot(normed_c, inner_w, 1, 0).reshape(rows, tok, cw)
    gate_c = dot(normed_c, gate_w, 1, 0).reshape(rows, tok, cw)
    pos = start + jnp.arange(tok + taps - 1, dtype=jnp.int32)
    current = pos[None, :] >= off[:, None]

    def valid(t, first, length):
        p = pos[None, first : first + length]
        source = p - t
        same = (source >= off[:, None]) == current[:, first : first + length]
        return ((source >= 0) & same).astype(F32)[:, :, None]

    edge = lax.ppermute(inner[:, tok - (taps - 1) :], "seq", [(i, i + 1) for i in range(n - 1)])
    moved = [shifted(inner, edge, t) * valid(t, 0, tok) for t in range(taps)]
    conv = sum(kernel_f[t][None, None, :] * moved[t] for t in range(taps))
    product = (conv * gate_c).astype(BF).reshape(count, cw)
    conv_part = dot(product, conv_out_t, 1, 1).astype(BF)
    conv_sum = head_total(conv_part)
    ffn2 = [gate_2] + gather_all(tie((ffn2_up, ffn2_down.T), conv_part), 12)
    resid_three = resid_two + conv_sum
    out_part, kept_two = mlp_forward(resid_three, gains[3], ffn2)

    dn_part, grads_two = mlp_backward(grad_four, kept_two, ffn2)
    both = lax.psum(jnp.concatenate([dn_part, out_part]), "head")
    dn, out_sum = both[:count].astype(F32), both[count:]
    sums_two = mlp_scatter(grads_two, 5, dn_part, out_part)
    (dn,) = tie((dn,), *sums_two)
    block_output = (resid_three + out_sum.astype(F32)).astype(BF).reshape(activations.shape)
    dx, gain_four = rms_back(resid_three, gains[3], dn)
    grad_three = grad_four.astype(F32) + dx
    grad_b = grad_three.astype(BF)
    d_product = dot(grad_b, conv_out_t, 1, 0).reshape(rows, tok, cw)
    d_gate_c = (d_product * conv).astype(BF).reshape(count, cw)
    d_conv = d_product * gate_c
    next_rows = lax.ppermute(d_conv[:, : taps - 1], "seq", [(i + 1, i) for i in range(n - 1)])
    d_inner = sum(
        kernel_f[t][None, None, :] * advanced(d_conv, next_rows, t) * valid(t, t, tok)
        for t in range(taps)
    )
    d_inner = d_inner.astype(BF).reshape(count, cw)
    kernel_grad = jnp.stack([jnp.sum(d_conv * moved[t], axis=(0, 1)) for t in range(taps)])
    dn_part = (dot(d_inner, inner_w, 1, 1) + dot(d_gate_c, gate_w, 1, 1)).astype(BF)
    dn = head_total(dn_part)
    sums_conv = scatter_all(
        tie((normed_c, grad_b), dn_part),
        ((0, d_inner), (0, d_gate_c), (1, product)),
        6,
        1,
    )
    (dn,) = tie((dn,), *sums_conv)
    dx, gain_three = rms_back(resid_two, gains[2], dn)
    grad_two = grad_three + dx
    dn_part, grads_one = mlp_backward(grad_two.astype(BF), kept_one, ffn1)
    dn = head_total(dn_part)
    (normed_1, grad_b1), d_gate_1, d_up_1, hidden_1 = grads_one
    if ring_size(n):
        sums_one = scatter_all(tie((normed_1,), dn_part), ((0, d_gate_1),), 9)
        (dn,) = tie((dn,), *sums_one)
    dx, gain_two = rms_back(resid_one, gains[1], dn)
    grad_one = grad_two + dx

    grad_b = grad_one.astype(BF)
    later = ((normed_1, grad_b1), ((0, d_up_1), (1, hidden_1)))
    if paired:
        d_qkv, dn_part, more = attend_pairs_back(off, grad_b, outs_t, qkv_w, attention, later, 7)
        sums_one = sums_one + more
    else:
        da = dot(grad_b, out_t, 1, 0).reshape(rows, tok, vw)
        dq, dan, extra = by_rows(
            query_back_kernel, scal, place, (q_own, k_all, v_all, da), (qw, vw, qw), (BF, BF, BF)
        )
        back = jnp.concatenate([dan, extra], axis=-1).reshape(count, vw + qw)
        back_all = by_sequence(gather_all([back], 7, 1)[0])
        dk, dv = by_rows(
            key_back_kernel,
            scal,
            place,
            (k_own, v_own, q_all, back_all[..., :vw], back_all[..., vw:]),
            (qw, vw),
            (BF, BF),
        )
        sums_one = scatter_all((normed_1,), ((0, d_gate_1),), 9) + scatter_all(*later, 10)
        d_qkv = jnp.concatenate([dq, dk, dv], axis=-1).reshape(count, 2 * qw + vw)
        dn_part = dot(d_qkv, qkv_w, 1, 1).astype(BF)
    dn = lax.psum(dn_part, "head")
    unit = inputs * rms_scale(inputs)
    gain_one = small_sum(jnp.sum(dn_part.astype(F32) * unit, axis=0), "head")
    small = jnp.concatenate(
        [
            jnp.stack([gain_one, gain_two, gain_three, gain_four]),
            jnp.pad(kernel_grad, ((0, 0), (0, width - cw))),
            jnp.zeros((8 - 4 - taps, width), F32),
        ]
    )
    sums_attn = scatter_all(
        tie((normed_a, grad_b), dn_part), ((0, d_qkv), (1, mixed)), 8, 0, small
    )
    gains_grad, kernel_grad = sums_attn[2][:4], sums_attn[2][4 : 4 + taps, :cw]
    qkv_sum = sums_attn[0]
    if paired:
        edges = (0, qw // 2, qw, qw + vw // 2)
        step = qw + vw // 2
        query_sum, key_sum, value_sum = (
            jnp.concatenate([qkv_sum[:, g * step + a : g * step + b] for g in range(2)], axis=1)
            for a, b in zip(edges[:-1], edges[1:])
        )
    else:
        query_sum, key_sum = qkv_sum[:, :qw], qkv_sum[:, qw : 2 * qw]
        value_sum = qkv_sum[:, 2 * qw :]
    straight = (sums_one[0], sums_one[1], sums_conv[0], sums_conv[1], sums_two[0], sums_two[1])
    if ring_size(n):
        input_grad, straight = closing(acts_flat, dn, grad_one, gains[:1], straight)
    else:
        input_grad = grad_one + rms_back(inputs, gains[0], dn.astype(F32))[0]
    input_grad = input_grad.reshape(activations.shape)
    return (
        block_output,
        input_grad,
        query_sum,
        key_sum,
        value_sum,
        sums_attn[1].T,
        straight[0],
        straight[1],
        sums_one[2].T,
        straight[2],
        straight[3],
        sums_conv[2].T,
        kernel_grad,
        straight[4],
        straight[5],
        sums_two[2].T,
        gains_grad,
    )


def solution(mesh):
    rows_in = P("seq", "head")
    rows_out = P("head", "seq")
    tokens = P(None, None, "seq", None)
    in_specs = (
        (tokens, P(), tokens)
        + (rows_in, rows_in, rows_in, rows_out)
        + (rows_in, rows_in, rows_out)
        + (rows_in, rows_in, rows_out)
        + (P(None, "head"),)
        + (rows_in, rows_in, rows_out)
        + (P(),)
    )
    out_specs = (
        (tokens, tokens)
        + (rows_in, rows_in, rows_in, rows_out)
        + (rows_in, rows_in, rows_out)
        + (rows_in, rows_in, rows_out)
        + (P(None, "head"),)
        + (rows_in, rows_in, rows_out)
        + (P(),)
    )
    return jax.shard_map(
        per_device, mesh=mesh, in_specs=in_specs, out_specs=out_specs, check_vma=False
    )
```

```python
from functools import partial

import jax
import jax.numpy as jnp
from jax import lax
from jax.experimental import pallas as pl
from jax.experimental.pallas import tpu as pltpu
from jax.sharding import PartitionSpec as P

QK = 16
VH = 112
EPSILON = 1e-05
BF = jnp.bfloat16
F32 = jnp.float32


MESH = pl.DeviceIdType.MESH
ANY = pl.BlockSpec(memory_space=pl.ANY)


def ring_device(p):
    return jnp.where(p < 4, 2 * p, 15 - 2 * p)


def ring_position(s):
    return jnp.where(lax.rem(s, 2) == 0, s // 2, 7 - s // 2)


def ring_size(n):
    return n == 8


def greet(n, everyone=False):
    me = lax.axis_index("seq")
    pos = ring_position(me)
    right = ring_device(lax.rem(pos + 1, n))
    left = ring_device(lax.rem(pos + n - 1, n))
    barrier = pltpu.get_barrier_semaphore()
    partners = [lax.rem(me + k, n) for k in range(1, n)] if everyone else [left, right]
    for partner in partners:
        pl.semaphore_signal(barrier, inc=1, device_id={"seq": partner}, device_id_type=MESH)
    pl.semaphore_wait(barrier, len(partners))
    return pos, right, left


class GatherRing:
    def __init__(self, n, where, src, out, place, send, recv, local, flip):
        self.n, self.src, self.out, self.place = n, src, out, place
        self.send, self.recv, self.local = send, recv, local
        self.pos, self.right, self.left = where
        self.flip = flip
        self.steps = n // 2
        self.done = 0

    def block(self, r):
        return self.place(self.out, ring_device(lax.rem(self.pos + (r % self.n), self.n)))

    def copy(self, k, d):
        block = self.block(-d * (k - 1))
        i = 0 if d == 1 else 1
        return pltpu.make_async_remote_copy(
            src_ref=self.src if k == 1 else block,
            dst_ref=block,
            send_sem=self.send.at[i, k - 1],
            recv_sem=self.recv.at[i, k - 1],
            device_id={"seq": self.right if d == 1 else self.left},
            device_id_type=MESH,
        )

    def ways(self, k):
        if k <= (self.n - 1) // 2:
            return (1, -1)
        return (-1,) if self.flip else (1,)

    def step(self):
        if self.done == self.steps:
            return
        if self.done == 0:
            pltpu.make_async_copy(self.src, self.block(0), self.local).start()
        self.done += 1
        k = self.done
        for d in self.ways(k):
            if k > 1:
                self.copy(k - 1, d).wait_recv()
            self.copy(k, d).start()

    def finish(self):
        while self.done < self.steps:
            self.step()
        pltpu.make_async_copy(self.src, self.block(0), self.local).wait()
        last = {d: max(k for k in range(1, self.steps + 1) if d in self.ways(k)) for d in (1, -1)}
        for d in (1, -1):
            self.copy(last[d], d).wait_recv()
        for k in range(1, self.steps + 1):
            for d in self.ways(k):
                self.copy(k, d).wait_send()


def by_block(height, first=0, rows=None):
    rows = height if rows is None else rows
    unit = 8 if height % 16 else 16
    return lambda ref, owner: ref.at[pl.ds(pl.multiple_of(owner * height + first, unit), rows)]


def by_position(tok):
    return lambda ref, owner: ref.at[:, pl.ds(pl.multiple_of(owner * tok, 16), tok)]


VMEM = pltpu.VMEM
MIB = 1024 * 1024


class Call:
    def __init__(self, call_id):
        self.n = lax.axis_size("seq")
        self.call_id = call_id
        self.ins, self.outs, self.scratch = {}, {}, {}
        self.gathers, self.scatters = {}, {}
        self.exchanges = []

    def exchange(self, name):
        self.sems(name + ".send", self.n)
        self.sems(name + ".recv", self.n)
        self.exchanges.append(name)

    def take(self, name, array, space=VMEM):
        self.ins[name] = (array, pl.BlockSpec(memory_space=space))
        return name

    def give(self, name, shape, kind, space=VMEM):
        self.outs[name] = (jax.ShapeDtypeStruct(shape, kind), pl.BlockSpec(memory_space=space))
        return name

    def hold(self, name, shape, kind):
        self.scratch[name] = VMEM(shape, kind)
        return name

    def sems(self, name, *shape):
        self.scratch[name] = pltpu.SemaphoreType.DMA(shape)

    def gather_blocks(self, name, array, flip=False):
        height = array.shape[0]
        self.take(name + ".src", array, pl.ANY)
        self.give(name, (self.n * height,) + array.shape[1:], array.dtype, pl.ANY)
        half = height // 2
        for p in range(2):
            self.gather(
                f"{name}.{p}",
                name + ".src",
                name,
                by_block(height, p * half, half),
                bool(p) != flip,
                (p * half, half),
            )

    def gather(self, name, src, out, place, flip=False, rows=None):
        half = self.n // 2
        self.sems(name + ".send", 2, half)
        self.sems(name + ".recv", 2, half)
        self.sems(name + ".local", 1)
        self.gathers[name] = (src, out, place, flip, rows)

    def left(self, name, array):
        self.take(name, array)
        rows, width = array.shape
        self.hold(name + ".blocked", (self.n, rows, width // self.n), BF)

    def scatter(self, name, left, right, flip=False, axis=0):
        n = self.n
        height = self.ins[left][0].shape[1] // n
        width = right.shape[1 - axis]
        self.take(name + ".right", right)
        self.give(name, (height, width), F32)
        cut = -(-width // 256) * 128
        for p, span in enumerate(((0, cut), (cut, width))):
            part = f"{name}.{p}"
            block = (height, span[1] - span[0])
            self.hold(part + ".sums", (2, n // 2) + block, BF)
            self.hold(part + ".slots", (2, n // 2) + block, BF)
            self.sems(part + ".send", 2, n // 2)
            self.sems(part + ".recv", 2, n // 2)
            self.scatters[part] = (name, left, bool(p) != flip, axis, span)

    def kernel(self, body, *refs):
        names = list(self.ins) + list(self.outs) + list(self.scratch)
        at = dict(zip(names, refs))
        where = greet(self.n, bool(self.exchanges))
        rings = {}
        for name, (src, out, place, flip, rows) in self.gathers.items():
            rings[name] = GatherRing(
                self.n,
                where,
                at[src] if rows is None else at[src].at[pl.ds(*rows)],
                at[out],
                place,
                at[name + ".send"],
                at[name + ".recv"],
                at[name + ".local"].at[0],
                flip,
            )
        ready = set()
        for name, (whole, left, flip, axis, span) in self.scatters.items():
            blocked = at[left + ".blocked"]
            if left not in ready:
                ready.add(left)
                width = blocked.shape[2]
                for b in range(self.n):
                    blocked[b] = at[left][:, b * width : (b + 1) * width]
            rings[name] = ScatterRing(
                self.n,
                where,
                blocked,
                at[whole + ".right"],
                at[whole],
                at[name + ".sums"],
                at[name + ".slots"],
                at[name + ".send"],
                at[name + ".recv"],
                flip,
                axis,
                span,
            )
            rings[name].step()
        body(at, rings)
        for ring in rings.values():
            ring.finish()

    def run(self, body):
        outs = pl.pallas_call(
            partial(self.kernel, body),
            in_specs=[spec for _, spec in self.ins.values()],
            out_specs=[spec for _, spec in self.outs.values()],
            out_shape=[shape for shape, _ in self.outs.values()],
            scratch_shapes=list(self.scratch.values()),
            compiler_params=pltpu.CompilerParams(
                collective_id=self.call_id, has_side_effects=True, vmem_limit_bytes=58 * MIB
            ),
        )(*[array for array, _ in self.ins.values()])
        return dict(zip(self.outs, outs))


def in_turn(n):
    def body(at, rings):
        for _ in range(n // 2):
            for ring in rings.values():
                ring.step()

    return body


def gather_all(arrays, call_id, flip=0):
    n = lax.axis_size("seq")
    if not ring_size(n):
        return [lax.all_gather(a, "seq", axis=0, tiled=True) for a in arrays]
    call = Call(call_id)
    names = [str(j) for j in range(len(arrays))]
    for j, (name, a) in enumerate(zip(names, arrays)):
        call.gather_blocks(name, a, (j + flip) % 2 == 1)
    out = call.run(in_turn(n))
    return [out[name] for name in names]


def first_gather(x, gain, parts, paired_outs, call_id):
    n = lax.axis_size("seq")
    call = Call(call_id)
    call.take("x", x)
    call.take("gain", gain)
    height = parts[2].shape[0]
    for name, a in zip("qkv", parts):
        call.take(name, a)
    for i, a in enumerate(paired_outs):
        call.take(f"o{i}", a)
    call.give("normed", x.shape, BF)
    call.give("outs", (height, sum(a.shape[0] for a in paired_outs)), BF)
    width = parts[0].shape[0] + parts[1].shape[0] + parts[2].shape[1]
    call.hold("src", (height, width), BF)
    call.give("w", (n * height, width), BF, pl.ANY)
    half = height // 2
    for p in range(2):
        call.gather(f"w.{p}", "src", "w", by_block(height, p * half, half), p == 1, (p * half, half))
    rows = x.shape[0] // n

    def body(at, rings):
        first = at["gain"][:1].astype(F32)
        kinds = [at["q"][...].astype(F32).T, at["k"][...].astype(F32).T, at["v"][...].astype(F32)]
        pieces = []
        for g in range(2):
            for a in kinds:
                size = a.shape[1] // 2
                pieces.append(a[:, g * size : (g + 1) * size])
        at["src"][...] = jnp.concatenate(pieces, axis=1).astype(BF)
        for k in range(n):
            if k % 2 == 0:
                for ring in rings.values():
                    ring.step()
            lines = slice(k * rows, (k + 1) * rows)
            at["normed"][lines] = rms_norm(at["x"][lines].astype(F32), first).astype(BF)
            if k == 1:
                both = [at[f"o{i}"][...].astype(F32) for i in range(len(paired_outs))]
                at["outs"][...] = jnp.concatenate(both, axis=0).T.astype(BF)

    out = call.run(body)
    return out["normed"], out["w"], out["outs"]


class ScatterRing:
    def __init__(self, n, where, left, right, out, sums, slots, send, recv, flip, axis, span):
        self.axis, self.span = axis, slice(*span)
        self.n, self.left_ref, self.right_ref, self.out = n, left, right, out
        self.sums, self.slots, self.send, self.recv = sums, slots, send, recv
        self.pos, self.right, self.left = where
        d = -1 if flip else 1
        self.hops = {d: n // 2, -d: (n - 1) // 2}
        self.order = (d, -d)
        self.done = 0
        self.steps = n // 2

    def term(self, r):
        owner = ring_device(lax.rem(self.pos + (r % self.n), self.n))
        right = self.right_ref[:, self.span] if self.axis == 0 else self.right_ref[self.span]
        return dot(self.left_ref[owner], right, 0, self.axis)

    def copy(self, d, h):
        i = 0 if d == 1 else 1
        return pltpu.make_async_remote_copy(
            src_ref=self.sums.at[i, h - 1],
            dst_ref=self.slots.at[i, h - 1],
            send_sem=self.send.at[i, h - 1],
            recv_sem=self.recv.at[i, h - 1],
            device_id={"seq": self.right if d == 1 else self.left},
            device_id_type=MESH,
        )

    def step(self):
        if self.done == self.steps:
            return
        self.done += 1
        h = self.done
        for d in self.order:
            if h > self.hops[d]:
                continue
            i = 0 if d == 1 else 1
            total = self.term(d * (self.hops[d] - h + 1))
            if h > 1:
                self.copy(d, h - 1).wait_recv()
                total = total + self.slots[i, h - 2].astype(F32)
            self.sums[i, h - 1] = total.astype(BF)
            self.copy(d, h).start()

    def finish(self):
        while self.done < self.steps:
            self.step()
        total = self.term(0)
        for d in self.order:
            i, h = (0 if d == 1 else 1), self.hops[d]
            self.copy(d, h).wait_recv()
            total = total + self.slots[i, h - 1].astype(F32)
        self.out[:, self.span] = total
        for d in self.order:
            for h in range(1, self.hops[d] + 1):
                self.copy(d, h).wait_send()


def scatter_all(lefts, pairs, call_id, flip=0, small=None, after=()):
    n = lax.axis_size("seq")
    pairs = [p if len(p) == 3 else p + (0,) for p in pairs]
    if not ring_size(n):
        sums = [
            lax.psum_scatter(
                dot(lefts[i], right, 0, axis).astype(BF), "seq", scatter_dimension=0, tiled=True
            ).astype(F32)
            for i, right, axis in pairs
        ]
        return sums if small is None else sums + [lax.psum(small.astype(BF), "seq").astype(F32)]
    call = Call(call_id)
    names = [str(j) for j in range(len(pairs))]
    for j, a in enumerate(after):
        call.take(f"after{j}", a, pl.ANY)
    if small is not None:
        call.take("small.src", small)
        call.hold("small.all", (n * small.shape[0], small.shape[1]), F32)
        call.gather("small", "small.src", "small.all", by_block(small.shape[0]))
    for i, a in enumerate(lefts):
        call.left(f"left{i}", a)
    for j, (i, right, axis) in enumerate(pairs):
        call.scatter(names[j], f"left{i}", right, (j + flip) % 2 == 1, axis)
    if small is not None:
        names.append(call.give("small.sum", small.shape, F32))

    def body(at, rings):
        in_turn(n)(at, rings)
        if small is not None:
            rings["small"].finish()
            rows = small.shape[0]
            blocks = [at["small.all"][b * rows : (b + 1) * rows] for b in range(n)]
            at["small.sum"][...] = sum(blocks[1:], blocks[0])
            del rings["small"]

    out = call.run(body)
    return [out[name] for name in names]


def small_sum(x, axis):
    size = lax.axis_size(axis)
    if size > 8:
        return lax.psum(x.astype(BF), axis).astype(F32)
    sent = x.astype(BF)
    routes = [[(i, (i + k) % size) for i in range(size)] for k in range(1, size)]
    return x + sum(lax.ppermute(sent, axis, r).astype(F32) for r in routes)


def dot(a, b, ca, cb):
    return lax.dot_general(a, b, (((ca,), (cb,)), ((), ())), preferred_element_type=F32)


def head_masks(query_width, value_width):
    lane_q = lax.broadcasted_iota(jnp.int32, (1, query_width), 1)
    lane_v = lax.broadcasted_iota(jnp.int32, (1, value_width), 1)
    heads = query_width // QK
    return [
        (
            (lane_q >= h * QK) & (lane_q < (h + 1) * QK),
            (lane_v >= h * VH) & (lane_v < (h + 1) * VH),
        )
        for h in range(heads)
    ]


def query_mask(scal_ref, place_ref, tok, row):
    offset = scal_ref[1 + row]
    pos = scal_ref[0] + lax.broadcasted_iota(jnp.int32, (tok, 1), 0)
    low = jnp.where(pos >= offset, offset, 0)
    other = place_ref[...]
    return (other >= low) & (other <= pos)


def key_mask(scal_ref, place_ref, tok, row):
    offset = scal_ref[1 + row]
    pos = scal_ref[0] + lax.broadcasted_iota(jnp.int32, (tok, 1), 0)
    high = jnp.where(pos >= offset, jnp.int32(1 << 30), offset)
    other = place_ref[...]
    return (other >= pos) & (other < high)


def attend_kernel(scal_ref, place_ref, q_ref, k_ref, v_ref, out_ref):
    q, k, v = q_ref[0], k_ref[0], v_ref[0]
    mask = query_mask(scal_ref, place_ref, q.shape[0], pl.program_id(0))
    total = jnp.zeros((q.shape[0], v.shape[1]), F32)
    for in_q, in_v in head_masks(q.shape[1], v.shape[1]):
        s = dot(jnp.where(in_q, q, jnp.zeros_like(q)), k, 1, 1) * (QK**-0.5)
        w = jnp.where(mask, 1.0 + s + 0.5 * s * s, 0.0)
        den = jnp.sum(w, axis=1, keepdims=True)
        total = total + jnp.where(in_v, dot(w.astype(BF), v, 1, 0) / den, 0.0)
    out_ref[0] = total.astype(BF)


def query_back_kernel(scal_ref, place_ref, q_ref, k_ref, v_ref, da_ref, dq_ref, dan_ref, extra_ref):
    q, k, v = q_ref[0], k_ref[0], v_ref[0]
    da = da_ref[0]
    tok = q.shape[0]
    mask = query_mask(scal_ref, place_ref, tok, pl.program_id(0))
    lane = lax.broadcasted_iota(jnp.int32, (1, q.shape[1]), 1)
    heads = q.shape[1] // QK
    dq = jnp.zeros(q.shape, F32)
    dan_all = jnp.zeros(da.shape, F32)
    extra = jnp.zeros(q.shape, F32)
    for h, (in_q, in_v) in enumerate(head_masks(q.shape[1], v.shape[1])):
        s = dot(jnp.where(in_q, q, jnp.zeros_like(q)), k, 1, 1) * (QK**-0.5)
        w = jnp.where(mask, 1.0 + s + 0.5 * s * s, 0.0)
        den = jnp.sum(w, axis=1, keepdims=True)
        att = dot(w.astype(BF), v, 1, 0) / den
        dan = jnp.where(in_v, da / den, 0.0).astype(BF)
        dan_f = dan.astype(F32)
        delta = jnp.sum(dan_f * att, axis=1, keepdims=True)
        d_kernel = dot(dan, v, 1, 1) - delta
        ds = jnp.where(mask, d_kernel * (1.0 + s), 0.0).astype(BF)
        dq = dq + jnp.where(in_q, dot(ds, k, 1, 0) * (QK**-0.5), 0.0)
        dan_all = dan_all + dan_f
        high = delta.astype(BF).astype(F32)
        extra = extra + jnp.where(lane == h, high, 0.0)
        extra = extra + jnp.where(lane == heads + h, delta - high, 0.0)
    dq_ref[0] = dq.astype(BF)
    dan_ref[0] = dan_all.astype(BF)
    extra_ref[0] = extra.astype(BF)


def key_back_kernel(scal_ref, place_ref, k_ref, v_ref, q_ref, dan_ref, extra_ref, dk_ref, dv_ref):
    k, v = k_ref[0], v_ref[0]
    q, dan, extra = q_ref[0], dan_ref[0], extra_ref[0]
    tok = k.shape[0]
    mask = key_mask(scal_ref, place_ref, tok, pl.program_id(0))
    lane = lax.broadcasted_iota(jnp.int32, (tok, k.shape[1]), 1)
    heads = k.shape[1] // QK
    dk = jnp.zeros(k.shape, F32)
    dv = jnp.zeros(v.shape, F32)
    for h, (in_q, in_v) in enumerate(head_masks(k.shape[1], v.shape[1])):
        s = dot(jnp.where(in_q, k, jnp.zeros_like(k)), q, 1, 1) * (QK**-0.5)
        w = jnp.where(mask, 1.0 + s + 0.5 * s * s, 0.0).astype(BF)
        dv = dv + jnp.where(in_v, dot(w, dan, 1, 0), 0.0)
        pick = jnp.where((lane == h) | (lane == heads + h), 1.0, 0.0).astype(BF)
        d_kernel = dot(jnp.where(in_v, v, jnp.zeros_like(v)), dan, 1, 1) - dot(pick, extra, 1, 1)
        ds = jnp.where(mask, d_kernel * (1.0 + s), 0.0).astype(BF)
        dk = dk + jnp.where(in_q, dot(ds, q, 1, 0) * (QK**-0.5), 0.0)
    dk_ref[0] = dk.astype(BF)
    dv_ref[0] = dv.astype(BF)


class Exchange:
    def __init__(self, n, at, name, block, place):
        self.n, self.block, self.place = n, block, place
        self.send, self.recv = at[name + ".send"], at[name + ".recv"]
        self.me = lax.axis_index("seq")

    def copy(self, k):
        partner = lax.rem(self.me + k, self.n)
        return pltpu.make_async_remote_copy(
            src_ref=self.block(partner),
            dst_ref=self.place(self.me),
            send_sem=self.send.at[k],
            recv_sem=self.recv.at[k],
            device_id={"seq": partner},
            device_id_type=MESH,
        )

    def own(self):
        return pltpu.make_async_copy(self.block(self.me), self.place(self.me), self.send.at[0])

    def start(self):
        for k in range(1, self.n):
            self.copy(k).start()
        self.own().start()

    def wait(self):
        self.own().wait()
        for k in range(1, self.n):
            self.copy(k).wait_recv()

    def wait_sent(self):
        for k in range(1, self.n):
            self.copy(k).wait_send()


def to_pair(ref, features, tok):
    def block(partner):
        rows = pl.ds(pl.multiple_of(lax.rem(partner, 2) * features, 16), features)
        return ref.at[rows, pl.ds(pl.multiple_of((partner // 2) * tok, 128), tok)]

    return block


def at_positions(ref, tok):
    return lambda device: ref.at[:, pl.ds(pl.multiple_of(device * tok, 128), tok)]


def causal(offset, i, tok):
    shape = ((i + 1) * tok, tok)
    earlier = lax.broadcasted_iota(jnp.int32, shape, 0)
    pos = i * tok + lax.broadcasted_iota(jnp.int32, shape, 1)
    return (earlier <= pos) & ((earlier >= offset) | (pos < offset))


def attend_pairs(off, weight, normed, carried, call_id):
    n = lax.axis_size("seq")
    count = normed.shape[0]
    tok = count * 2 // n
    features = weight.shape[1] // 2
    vf = features - 4 * QK
    call = Call(call_id)
    call.take("off", off, pltpu.SMEM)
    call.take("weight", weight)
    call.take("normed", normed)
    call.hold("qkv", (2 * features, count), BF)
    call.hold("mixed_t", (2 * vf, count), BF)
    for j, a in enumerate(carried):
        call.gather_blocks(f"c{j}", a, j % 2 == 1)
    call.give("mixed", (count, 2 * vf), BF)
    call.give("all", (features, n * tok), BF)
    call.give("att", (vf, n * tok), F32)
    call.give("den", (8, n * tok), F32)
    call.hold("own", (vf, n * tok), BF)
    call.exchange("in")
    call.exchange("out")

    def incoming(at):
        return Exchange(n, at, "in", to_pair(at["qkv"], features, tok), at_positions(at["all"], tok))

    def body(at, rings):
        def turn():
            for ring in rings.values():
                ring.step()

        turn()
        half = count // 2
        for p in range(2):
            part = dot(at["normed"][p * half : (p + 1) * half], at["weight"][...], 1, 0)
            at["qkv"][:, p * half : (p + 1) * half] = part.T.astype(BF)
        arriving = incoming(at)
        arriving.start()
        arriving.wait()
        turn()
        me = lax.axis_index("seq")
        offset = at["off"][me // 2]
        whole = at["all"]
        at["den"][...] = jnp.ones_like(at["den"])
        for h in range(2):
            lines = slice(h * vf // 2, (h + 1) * vf // 2)
            for i in range(n):
                here, upto = slice(i * tok, (i + 1) * tok), slice(0, (i + 1) * tok)
                q = whole[h * QK : (h + 1) * QK, here]
                k = whole[(2 + h) * QK : (3 + h) * QK, upto]
                v = whole[4 * QK + h * vf // 2 : 4 * QK + (h + 1) * vf // 2, upto]
                s = dot(k, q, 0, 0) * (QK**-0.5)
                w = jnp.where(causal(offset, i, tok), 1.0 + s + 0.5 * s * s, 0.0)
                den = jnp.sum(w, axis=0, keepdims=True)
                att = dot(v, w.astype(BF), 1, 0) / den
                at["att"][lines, here] = att
                at["den"][h : h + 1, here] = den
                at["own"][lines, here] = att.astype(BF)
        leaving = Exchange(
            n, at, "out", at_positions(at["own"], tok), lambda me: to_pair(at["mixed_t"], vf, tok)(me)
        )
        leaving.start()
        for _ in range(n // 2):
            turn()
        arriving.wait_sent()
        leaving.wait()
        at["mixed"][...] = at["mixed_t"][...].astype(F32).T.astype(BF)
        leaving.wait_sent()

    out = call.run(body)
    return out, [out[f"c{j}"] for j in range(len(carried))]


def attend_pairs_back(off, grad, out_t, weight, kept, scatters, call_id):
    n = lax.axis_size("seq")
    whole = kept["all"]
    features, tok = whole.shape[0], whole.shape[1] // n
    vf = features - 4 * QK
    call = Call(call_id)
    call.take("off", off, pltpu.SMEM)
    call.take("grad", grad)
    call.take("out_t", out_t)
    call.take("weight", weight)
    count, width = grad.shape
    call.hold("da", (2 * vf, count), BF)
    for name in ("all", "att", "den"):
        call.take(name, kept[name])
    lefts, pairs = scatters
    for i, a in enumerate(lefts):
        call.left(f"left{i}", a)
    for j, (i, right) in enumerate(pairs):
        call.scatter(f"s{j}", f"left{i}", right, j % 2 == 1)
    call.give("d", (count, 2 * features), BF)
    call.give("part", (count, width), BF)
    call.hold("d_t", (2 * features, count), BF)
    call.hold("da_all", (vf, n * tok), BF)
    call.hold("sum", (2 * QK + vf, n * tok), F32)
    call.hold("own", (features, n * tok), BF)
    call.exchange("in")
    call.exchange("out")

    def incoming(at):
        return Exchange(n, at, "in", to_pair(at["da"], vf, tok), at_positions(at["da_all"], tok))

    def body(at, rings):
        half = count // 2
        for p in range(2):
            part = dot(at["grad"][p * half : (p + 1) * half], at["out_t"][:, : 2 * vf], 1, 0)
            at["da"][:, p * half : (p + 1) * half] = part.T.astype(BF)
        arriving = incoming(at)
        arriving.start()
        arriving.wait()
        for ring in rings.values():
            ring.step()
        me = lax.axis_index("seq")
        offset = at["off"][me // 2]
        whole = at["all"]
        total = at["sum"]
        for h in range(2):
            lines = slice(h * vf // 2, (h + 1) * vf // 2)
            k_lines = slice(h * QK, (h + 1) * QK)
            v_lines = slice(2 * QK + h * vf // 2, 2 * QK + (h + 1) * vf // 2)
            for i in range(n - 1, -1, -1):
                here, upto = slice(i * tok, (i + 1) * tok), slice(0, (i + 1) * tok)
                q = whole[h * QK : (h + 1) * QK, here]
                k = whole[(2 + h) * QK : (3 + h) * QK, upto]
                v = whole[4 * QK + h * vf // 2 : 4 * QK + (h + 1) * vf // 2, upto]
                mask = causal(offset, i, tok)
                s = dot(k, q, 0, 0) * (QK**-0.5)
                w = jnp.where(mask, 1.0 + s + 0.5 * s * s, 0.0).astype(BF)
                dan = (at["da_all"][lines, here].astype(F32) / at["den"][h : h + 1, here]).astype(BF)
                delta = jnp.sum(dan.astype(F32) * at["att"][lines, here], axis=0, keepdims=True)
                ds = jnp.where(mask, (dot(v, dan, 0, 0) - delta) * (1.0 + s), 0.0).astype(BF)
                dq = dot(k, ds, 1, 0) * (QK**-0.5)
                at["own"][h * QK : (h + 1) * QK, here] = dq.astype(BF)
                dk = dot(q, ds, 1, 1) * (QK**-0.5)
                dv = dot(dan, w, 1, 1)
                if i == n - 1:
                    total[k_lines, upto] = dk
                    total[v_lines, upto] = dv
                else:
                    total[k_lines, upto] += dk
                    total[v_lines, upto] += dv
        at["own"][2 * QK :, :] = total[...].astype(BF)
        leaving = Exchange(
            n, at, "out", at_positions(at["own"], tok), lambda me: to_pair(at["d_t"], features, tok)(me)
        )
        leaving.start()
        for ring in rings.values():
            ring.step()
        leaving.wait()
        at["d"][...] = at["d_t"][...].astype(F32).T.astype(BF)
        for j in range(width // 256):
            lines = slice(j * 256, (j + 1) * 256)
            at["part"][:, lines] = dot(at["d"][...], at["weight"][lines, :], 1, 1).astype(BF)
        for _ in range(n // 2):
            for ring in rings.values():
                ring.step()
        arriving.wait_sent()
        leaving.wait_sent()

    out = call.run(body)
    return out["d"], out["part"], [out[f"s{j}"] for j in range(len(pairs))]


def by_rows(kernel, scal, place, operands, widths, kinds):
    rows = operands[0].shape[0]
    tok = operands[0].shape[1]
    specs = [
        pl.BlockSpec(memory_space=pltpu.SMEM),
        pl.BlockSpec(place.shape, lambda r: (0, 0)),
    ]
    specs += [pl.BlockSpec((1,) + a.shape[1:], lambda r: (r, 0, 0)) for a in operands]
    return pl.pallas_call(
        kernel,
        grid=(rows,),
        in_specs=specs,
        out_specs=[pl.BlockSpec((1, tok, w), lambda r: (r, 0, 0)) for w in widths],
        out_shape=[jax.ShapeDtypeStruct((rows, tok, w), t) for w, t in zip(widths, kinds)],
        compiler_params=pltpu.CompilerParams(vmem_limit_bytes=48 * 1024 * 1024),
    )(scal, place, *operands)


def rms_scale(x):
    return lax.rsqrt(jnp.mean(x * x, axis=-1, keepdims=True) + EPSILON)


def rms_norm(x, gain):
    return x * rms_scale(x) * gain


def rms_back(x, gain, dn):
    scale = rms_scale(x)
    unit = x * scale
    gain_grad = jnp.sum(dn * unit, axis=0)
    dg = dn * gain
    dx = scale * (dg - unit * jnp.mean(dg * unit, axis=-1, keepdims=True))
    return dx, gain_grad


def closing_kernel(count, *refs):
    x_ref, dn_ref, grad_ref, gain_ref, qkv_ref, small_ref = refs[:6]
    srcs, turned, refs = refs[6 : 6 + count], refs[6 + count : 8 + count], refs[8 + count :]
    out_ref, (q_ref, k_ref, v_ref), gains_ref, taps_ref = refs[0], refs[1:4], refs[4], refs[5]
    across, dsts = refs[6:8], refs[8:]
    gain = gain_ref[:1].astype(F32)
    dx, _ = rms_back(x_ref[...].astype(F32), gain, dn_ref[...].astype(F32))
    out_ref[...] = grad_ref[...] + dx
    for src, dst in zip(srcs, dsts):
        dst[...] = src[...]

    @pl.when(pl.program_id(0) == 0)
    def _():
        q, v = q_ref.shape[0] // 2, v_ref.shape[1] // 2
        halves = [qkv_ref[:, g * (2 * q + v) : (g + 1) * (2 * q + v)] for g in range(2)]
        q_ref[...] = jnp.concatenate([a[:, :q] for a in halves], axis=1).T
        k_ref[...] = jnp.concatenate([a[:, q : 2 * q] for a in halves], axis=1).T
        v_ref[...] = jnp.concatenate([a[:, 2 * q :] for a in halves], axis=1)
        norms = gains_ref.shape[0]
        gains_ref[...] = small_ref[:norms]
        taps_ref[...] = small_ref[norms : norms + taps_ref.shape[0], : taps_ref.shape[1]]

    for i in range(2):

        @pl.when(pl.program_id(0) == i + 1)
        def _():
            across[i][...] = turned[i][...].T


def closing(x, dn, grad, gains, qkv, widths, small, taps, results, turned):
    steps = 4

    def rows(a):
        return pl.BlockSpec((a.shape[0] // steps, a.shape[1]), lambda i: (i, 0))

    def whole(a):
        return pl.BlockSpec(a.shape, lambda i: (0, 0))

    height = qkv.shape[0]
    fixed = [(widths[0], height), (widths[1], height), (height, widths[2]), gains.shape, taps.shape]
    fixed += [r.shape[::-1] for r in turned]
    fixed = [jax.ShapeDtypeStruct(k, F32) for k in fixed]
    same = [jax.ShapeDtypeStruct(r.shape, F32) for r in results]
    shape = jax.ShapeDtypeStruct(x.shape, F32)
    out = pl.pallas_call(
        partial(closing_kernel, len(results)),
        grid=(steps,),
        in_specs=[rows(x), rows(dn), rows(grad), whole(gains), whole(qkv), whole(small)]
        + [rows(r) for r in results]
        + [whole(r) for r in turned],
        out_specs=[rows(shape)] + [whole(k) for k in fixed] + [rows(a) for a in same],
        out_shape=[shape] + fixed + same,
        compiler_params=pltpu.CompilerParams(vmem_limit_bytes=58 * MIB),
    )(x, dn, grad, gains, qkv, small, *results, *turned)
    return out[0], (out[1].T, out[2].T, out[3]), out[4], out[5], out[6:8], out[8:]


def head_total(partial_sum):
    return lax.psum(partial_sum, "head").astype(F32)


def tie(xs, *others):
    return list(lax.optimization_barrier((tuple(xs), tuple(others)))[0])


def mlp_forward(resid, gain, weights):
    gate_w, up_w, down_t = weights
    normed = rms_norm(resid, gain).astype(BF)
    gate_val = dot(normed, gate_w, 1, 0)
    up_val = dot(normed, up_w, 1, 0)
    hidden = (gate_val * jax.nn.sigmoid(gate_val) * up_val).astype(BF)
    return dot(hidden, down_t, 1, 1).astype(BF), (normed, gate_val, up_val, hidden)


def mlp_scatter(kept, call_id, *others):
    (normed, grad_b), d_gate, d_up, hidden = kept
    normed, grad_b = tie((normed, grad_b), *others)
    return scatter_all((normed, grad_b), ((0, d_gate), (0, d_up), (1, hidden)), call_id)


def mlp_backward(grad_b, saved, weights):
    gate_w, up_w, down_t = weights
    normed, gate_val, up_val, hidden = saved
    dh = dot(grad_b, down_t, 1, 0)
    sig = jax.nn.sigmoid(gate_val)
    silu = gate_val * sig
    d_gate = (dh * up_val * (sig * (1.0 + gate_val * (1.0 - sig)))).astype(BF)
    d_up = (dh * silu).astype(BF)
    dn_part = (dot(d_gate, gate_w, 1, 1) + dot(d_up, up_w, 1, 1)).astype(BF)
    return dn_part, ((normed, grad_b), d_gate, d_up, hidden)


def shifted(block, before, shift):
    if shift == 0:
        return block
    return jnp.concatenate([before[:, before.shape[1] - shift :], block[:, :-shift]], axis=1)


def advanced(block, after, shift):
    if shift == 0:
        return block
    return jnp.concatenate([block[:, shift:], after[:, :shift]], axis=1)


def per_device(
    activations,
    offsets,
    cotangent,
    attn_query,
    attn_key,
    attn_value,
    attn_output,
    ffn1_gate,
    ffn1_up,
    ffn1_down,
    conv_input,
    conv_gate,
    conv_output,
    conv_kernel,
    ffn2_gate,
    ffn2_up,
    ffn2_down,
    norm_gains,
):
    n = lax.axis_size("seq")
    micro, row_count, tok, width = activations.shape
    rows = micro * row_count
    count = rows * tok
    qw, vw = attn_query.shape[1], attn_value.shape[1]
    cw = conv_input.shape[1]
    taps = conv_kernel.shape[0]
    here = lax.axis_index("seq")
    start = here * tok
    off = offsets.reshape(rows)

    paired = ring_size(n) and 2 * rows == n and qw == 4 * QK
    gains = norm_gains.astype(F32)
    kernel_f = conv_kernel.astype(F32)
    acts_flat = activations.reshape(count, width)
    inputs = acts_flat.astype(F32)
    grad_four = cotangent.reshape(count, width)
    if paired:
        normed_a, qkv_w, outs_s = first_gather(
            acts_flat,
            norm_gains,
            (attn_query.T, attn_key.T, attn_value),
            (attn_output, conv_output),
            1,
        )
    else:
        normed_a = rms_norm(inputs, gains[0]).astype(BF)
        qkv_s = jnp.concatenate([attn_query, attn_key, attn_value], axis=1)
        (qkv_w,) = gather_all([qkv_s], 1)
        outs_s = jnp.concatenate([attn_output.T, conv_output.T], axis=1)

    scal = jnp.concatenate([start[None].astype(jnp.int32), off])
    place = jnp.arange(n * tok, dtype=jnp.int32).reshape(1, n * tok)

    def by_sequence(blocks):
        return jnp.swapaxes(blocks.reshape(n, rows, tok, -1), 0, 1).reshape(rows, n * tok, -1)

    if paired:
        attention, (outs_t, gate_1) = attend_pairs(off, qkv_w, normed_a, (outs_s, ffn1_gate), 2)
        mixed = attention["mixed"]
    else:
        qkv = dot(normed_a, qkv_w, 1, 0).astype(BF)
        qkv_all = by_sequence(gather_all([qkv], 2)[0])
        own = qkv.reshape(rows, tok, -1)
        q_own, k_own, v_own = own[..., :qw], own[..., qw : 2 * qw], own[..., 2 * qw :]
        q_all, k_all, v_all = qkv_all[..., :qw], qkv_all[..., qw : 2 * qw], qkv_all[..., 2 * qw :]
        (mixed,) = by_rows(attend_kernel, scal, place, (q_own, k_all, v_all), (vw,), (BF,))
        mixed = mixed.reshape(count, vw)
        outs_t, gate_1 = gather_all((outs_s, ffn1_gate), 11)
    out_t, conv_out_t = outs_t[:, :vw], outs_t[:, vw:]
    attn_part = dot(mixed, out_t, 1, 1).astype(BF)
    attn_sum = head_total(attn_part)
    ffn1 = [gate_1] + gather_all(tie((ffn1_up, ffn1_down.T), attn_part), 12)
    resid_one = inputs + attn_sum
    part, kept_one = mlp_forward(resid_one, gains[1], ffn1)
    ffn1_sum = head_total(part)
    inner_w, gate_w, gate_2 = gather_all(tie((conv_input, conv_gate, ffn2_gate), part), 4)
    resid_two = resid_one + ffn1_sum

    normed_c = rms_norm(resid_two, gains[2]).astype(BF)
    inner = dot(normed_c, inner_w, 1, 0).reshape(rows, tok, cw)
    gate_c = dot(normed_c, gate_w, 1, 0).reshape(rows, tok, cw)
    pos = start + jnp.arange(tok + taps - 1, dtype=jnp.int32)
    current = pos[None, :] >= off[:, None]

    def valid(t, first, length):
        p = pos[None, first : first + length]
        source = p - t
        same = (source >= off[:, None]) == current[:, first : first + length]
        return ((source >= 0) & same).astype(F32)[:, :, None]

    edge = lax.ppermute(inner[:, tok - (taps - 1) :], "seq", [(i, i + 1) for i in range(n - 1)])
    moved = [shifted(inner, edge, t) * valid(t, 0, tok) for t in range(taps)]
    conv = sum(kernel_f[t][None, None, :] * moved[t] for t in range(taps))
    product = (conv * gate_c).astype(BF).reshape(count, cw)
    conv_part = dot(product, conv_out_t, 1, 1).astype(BF)
    conv_sum = head_total(conv_part)
    ffn2 = [gate_2] + gather_all(tie((ffn2_up, ffn2_down.T), conv_part), 12)
    resid_three = resid_two + conv_sum
    out_part, kept_two = mlp_forward(resid_three, gains[3], ffn2)

    dn_part, grads_two = mlp_backward(grad_four, kept_two, ffn2)
    both = lax.psum(jnp.concatenate([dn_part, out_part]), "head")
    dn, out_sum = both[:count].astype(F32), both[count:]
    sums_two = mlp_scatter(grads_two, 5, dn_part, out_part)
    (dn,) = tie((dn,), *sums_two)
    block_output = (resid_three + out_sum.astype(F32)).astype(BF).reshape(activations.shape)
    dx, gain_four = rms_back(resid_three, gains[3], dn)
    grad_three = grad_four.astype(F32) + dx
    grad_b = grad_three.astype(BF)
    d_product = dot(grad_b, conv_out_t, 1, 0).reshape(rows, tok, cw)
    d_gate_c = (d_product * conv).astype(BF).reshape(count, cw)
    d_conv = d_product * gate_c
    next_rows = lax.ppermute(d_conv[:, : taps - 1], "seq", [(i + 1, i) for i in range(n - 1)])
    d_inner = sum(
        kernel_f[t][None, None, :] * advanced(d_conv, next_rows, t) * valid(t, t, tok)
        for t in range(taps)
    )
    d_inner = d_inner.astype(BF).reshape(count, cw)
    kernel_grad = jnp.stack([jnp.sum(d_conv * moved[t], axis=(0, 1)) for t in range(taps)])
    dn_part = (dot(d_inner, inner_w, 1, 1) + dot(d_gate_c, gate_w, 1, 1)).astype(BF)
    dn = head_total(dn_part)
    sums_conv = scatter_all(
        tie((normed_c, grad_b), dn_part),
        ((0, d_inner), (0, d_gate_c), (1, product)),
        6,
        1,
    )
    (dn,) = tie((dn,), *sums_conv)
    dx, gain_three = rms_back(resid_two, gains[2], dn)
    grad_two = grad_three + dx
    dn_part, grads_one = mlp_backward(grad_two.astype(BF), kept_one, ffn1)
    dn = head_total(dn_part)
    (normed_1, grad_b1), d_gate_1, d_up_1, hidden_1 = grads_one
    if ring_size(n):
        sums_one = scatter_all(tie((normed_1,), dn_part), ((0, d_gate_1),), 9)
        (dn,) = tie((dn,), *sums_one)
    dx, gain_two = rms_back(resid_one, gains[1], dn)
    grad_one = grad_two + dx

    grad_b = grad_one.astype(BF)
    later = ((normed_1, grad_b1), ((0, d_up_1), (1, hidden_1)))
    if paired:
        d_qkv, dn_part, more = attend_pairs_back(off, grad_b, outs_t, qkv_w, attention, later, 7)
        sums_one = sums_one + more
    else:
        da = dot(grad_b, out_t, 1, 0).reshape(rows, tok, vw)
        dq, dan, extra = by_rows(
            query_back_kernel, scal, place, (q_own, k_all, v_all, da), (qw, vw, qw), (BF, BF, BF)
        )
        back = jnp.concatenate([dan, extra], axis=-1).reshape(count, vw + qw)
        back_all = by_sequence(gather_all([back], 7, 1)[0])
        dk, dv = by_rows(
            key_back_kernel,
            scal,
            place,
            (k_own, v_own, q_all, back_all[..., :vw], back_all[..., vw:]),
            (qw, vw),
            (BF, BF),
        )
        sums_one = scatter_all((normed_1,), ((0, d_gate_1),), 9) + scatter_all(*later, 10)
        d_qkv = jnp.concatenate([dq, dk, dv], axis=-1).reshape(count, 2 * qw + vw)
        dn_part = dot(d_qkv, qkv_w, 1, 1).astype(BF)
    dn = lax.psum(dn_part, "head")
    unit = inputs * rms_scale(inputs)
    gain_one = small_sum(jnp.sum(dn_part.astype(F32) * unit, axis=0), "head")
    small = jnp.concatenate(
        [
            jnp.stack([gain_one, gain_two, gain_three, gain_four]),
            jnp.pad(kernel_grad, ((0, 0), (0, width - cw))),
            jnp.zeros((8 - 4 - taps, width), F32),
        ]
    )
    sums_attn = scatter_all(
        tie((normed_a, grad_b), dn_part), ((0, d_qkv), (1, mixed)), 8, 0, small
    )
    gains_grad, kernel_grad = sums_attn[2][:4], sums_attn[2][4 : 4 + taps, :cw]
    qkv_sum = sums_attn[0]
    straight = (sums_one[0], sums_one[1], sums_conv[0], sums_conv[1], sums_two[0], sums_two[1])
    straight += (sums_one[2], sums_two[2])
    turned = (sums_conv[2], sums_attn[1])
    if paired:
        input_grad, by_kind, gains_grad, kernel_grad, turned, straight = closing(
            acts_flat,
            dn,
            grad_one,
            norm_gains,
            qkv_sum,
            (qw, qw, vw),
            sums_attn[2],
            conv_kernel,
            straight,
            turned,
        )
    else:
        input_grad = grad_one + rms_back(inputs, gains[0], dn.astype(F32))[0]
        by_kind = (qkv_sum[:, :qw], qkv_sum[:, qw : 2 * qw], qkv_sum[:, 2 * qw :])
        turned = [r.T for r in turned]
    input_grad = input_grad.reshape(activations.shape)
    return (
        block_output,
        input_grad,
        *by_kind,
        turned[1],
        straight[0],
        straight[1],
        straight[6].T,
        straight[2],
        straight[3],
        turned[0],
        kernel_grad,
        straight[4],
        straight[5],
        straight[7].T,
        gains_grad,
    )


def solution(mesh):
    rows_in = P("seq", "head")
    rows_out = P("head", "seq")
    tokens = P(None, None, "seq", None)
    in_specs = (
        (tokens, P(), tokens)
        + (rows_in, rows_in, rows_in, rows_out)
        + (rows_in, rows_in, rows_out)
        + (rows_in, rows_in, rows_out)
        + (P(None, "head"),)
        + (rows_in, rows_in, rows_out)
        + (P(),)
    )
    out_specs = (
        (tokens, tokens)
        + (rows_in, rows_in, rows_in, rows_out)
        + (rows_in, rows_in, rows_out)
        + (rows_in, rows_in, rows_out)
        + (P(None, "head"),)
        + (rows_in, rows_in, rows_out)
        + (P(),)
    )
    return jax.shard_map(
        per_device, mesh=mesh, in_specs=in_specs, out_specs=out_specs, check_vma=False
    )
```

```python
from functools import partial

import jax
import jax.numpy as jnp
from jax import lax
from jax.experimental import pallas as pl
from jax.experimental.pallas import tpu as pltpu
from jax.sharding import PartitionSpec as P

QK = 16
VH = 112
EPSILON = 1e-05
BF = jnp.bfloat16
F32 = jnp.float32


MESH = pl.DeviceIdType.MESH
ANY = pl.BlockSpec(memory_space=pl.ANY)


def ring_device(p):
    return jnp.where(p < 4, 2 * p, 15 - 2 * p)


def ring_position(s):
    return jnp.where(lax.rem(s, 2) == 0, s // 2, 7 - s // 2)


def ring_size(n):
    return n == 8


def greet(n, everyone=False):
    me = lax.axis_index("seq")
    pos = ring_position(me)
    right = ring_device(lax.rem(pos + 1, n))
    left = ring_device(lax.rem(pos + n - 1, n))
    barrier = pltpu.get_barrier_semaphore()
    partners = [lax.rem(me + k, n) for k in range(1, n)] if everyone else [left, right]
    for partner in partners:
        pl.semaphore_signal(barrier, inc=1, device_id={"seq": partner}, device_id_type=MESH)
    pl.semaphore_wait(barrier, len(partners))
    return pos, right, left


class GatherRing:
    def __init__(self, n, where, src, out, place, send, recv, local, flip):
        self.n, self.src, self.out, self.place = n, src, out, place
        self.send, self.recv, self.local = send, recv, local
        self.pos, self.right, self.left = where
        self.flip = flip
        self.steps = n // 2
        self.done = 0

    def block(self, r):
        return self.place(self.out, ring_device(lax.rem(self.pos + (r % self.n), self.n)))

    def copy(self, k, d):
        block = self.block(-d * (k - 1))
        i = 0 if d == 1 else 1
        return pltpu.make_async_remote_copy(
            src_ref=self.src if k == 1 else block,
            dst_ref=block,
            send_sem=self.send.at[i, k - 1],
            recv_sem=self.recv.at[i, k - 1],
            device_id={"seq": self.right if d == 1 else self.left},
            device_id_type=MESH,
        )

    def ways(self, k):
        if k <= (self.n - 1) // 2:
            return (1, -1)
        return (-1,) if self.flip else (1,)

    def step(self):
        if self.done == self.steps:
            return
        if self.done == 0:
            pltpu.make_async_copy(self.src, self.block(0), self.local).start()
        self.done += 1
        k = self.done
        for d in self.ways(k):
            if k > 1:
                self.copy(k - 1, d).wait_recv()
            self.copy(k, d).start()

    def finish(self):
        while self.done < self.steps:
            self.step()
        pltpu.make_async_copy(self.src, self.block(0), self.local).wait()
        last = {d: max(k for k in range(1, self.steps + 1) if d in self.ways(k)) for d in (1, -1)}
        for d in (1, -1):
            self.copy(last[d], d).wait_recv()
        for k in range(1, self.steps + 1):
            for d in self.ways(k):
                self.copy(k, d).wait_send()


def by_block(height, first=0, rows=None):
    rows = height if rows is None else rows
    unit = 8 if height % 16 else 16
    return lambda ref, owner: ref.at[pl.ds(pl.multiple_of(owner * height + first, unit), rows)]


def by_position(tok):
    return lambda ref, owner: ref.at[:, pl.ds(pl.multiple_of(owner * tok, 16), tok)]


VMEM = pltpu.VMEM
MIB = 1024 * 1024


class Call:
    def __init__(self, call_id):
        self.n = lax.axis_size("seq")
        self.call_id = call_id
        self.ins, self.outs, self.scratch = {}, {}, {}
        self.gathers, self.scatters = {}, {}
        self.exchanges = []

    def exchange(self, name):
        self.sems(name + ".send", self.n)
        self.sems(name + ".recv", self.n)
        self.exchanges.append(name)

    def take(self, name, array, space=VMEM):
        self.ins[name] = (array, pl.BlockSpec(memory_space=space))
        return name

    def give(self, name, shape, kind, space=VMEM):
        self.outs[name] = (jax.ShapeDtypeStruct(shape, kind), pl.BlockSpec(memory_space=space))
        return name

    def hold(self, name, shape, kind):
        self.scratch[name] = VMEM(shape, kind)
        return name

    def sems(self, name, *shape):
        self.scratch[name] = pltpu.SemaphoreType.DMA(shape)

    def gather_blocks(self, name, array, flip=False):
        height = array.shape[0]
        self.take(name + ".src", array, pl.ANY)
        self.give(name, (self.n * height,) + array.shape[1:], array.dtype, pl.ANY)
        half = height // 2
        for p in range(2):
            self.gather(
                f"{name}.{p}",
                name + ".src",
                name,
                by_block(height, p * half, half),
                bool(p) != flip,
                (p * half, half),
            )

    def gather(self, name, src, out, place, flip=False, rows=None):
        half = self.n // 2
        self.sems(name + ".send", 2, half)
        self.sems(name + ".recv", 2, half)
        self.sems(name + ".local", 1)
        self.gathers[name] = (src, out, place, flip, rows)

    def left(self, name, array):
        self.take(name, array)
        rows, width = array.shape
        self.hold(name + ".blocked", (self.n, rows, width // self.n), BF)

    def scatter(self, name, left, right, flip=False, axis=0):
        n = self.n
        height = self.ins[left][0].shape[1] // n
        width = right.shape[1 - axis]
        self.take(name + ".right", right)
        self.give(name, (height, width), F32)
        cut = -(-width // 256) * 128
        for p, span in enumerate(((0, cut), (cut, width))):
            part = f"{name}.{p}"
            block = (height, span[1] - span[0])
            self.hold(part + ".sums", (2, n // 2) + block, BF)
            self.hold(part + ".slots", (2, n // 2) + block, BF)
            self.sems(part + ".send", 2, n // 2)
            self.sems(part + ".recv", 2, n // 2)
            self.scatters[part] = (name, left, bool(p) != flip, axis, span)

    def kernel(self, body, *refs):
        names = list(self.ins) + list(self.outs) + list(self.scratch)
        at = dict(zip(names, refs))
        where = greet(self.n, bool(self.exchanges))
        rings = {}
        for name, (src, out, place, flip, rows) in self.gathers.items():
            rings[name] = GatherRing(
                self.n,
                where,
                at[src] if rows is None else at[src].at[pl.ds(*rows)],
                at[out],
                place,
                at[name + ".send"],
                at[name + ".recv"],
                at[name + ".local"].at[0],
                flip,
            )
        ready = set()
        for name, (whole, left, flip, axis, span) in self.scatters.items():
            blocked = at[left + ".blocked"]
            if left not in ready:
                ready.add(left)
                width = blocked.shape[2]
                for b in range(self.n):
                    blocked[b] = at[left][:, b * width : (b + 1) * width]
            rings[name] = ScatterRing(
                self.n,
                where,
                blocked,
                at[whole + ".right"],
                at[whole],
                at[name + ".sums"],
                at[name + ".slots"],
                at[name + ".send"],
                at[name + ".recv"],
                flip,
                axis,
                span,
            )
            rings[name].step()
        body(at, rings)
        for ring in rings.values():
            ring.finish()

    def run(self, body):
        outs = pl.pallas_call(
            partial(self.kernel, body),
            in_specs=[spec for _, spec in self.ins.values()],
            out_specs=[spec for _, spec in self.outs.values()],
            out_shape=[shape for shape, _ in self.outs.values()],
            scratch_shapes=list(self.scratch.values()),
            compiler_params=pltpu.CompilerParams(
                collective_id=self.call_id, has_side_effects=True, vmem_limit_bytes=58 * MIB
            ),
        )(*[array for array, _ in self.ins.values()])
        return dict(zip(self.outs, outs))


def in_turn(n):
    def body(at, rings):
        for _ in range(n // 2):
            for ring in rings.values():
                ring.step()

    return body


def gather_all(arrays, call_id, flip=0):
    n = lax.axis_size("seq")
    if not ring_size(n):
        return [lax.all_gather(a, "seq", axis=0, tiled=True) for a in arrays]
    call = Call(call_id)
    names = [str(j) for j in range(len(arrays))]
    for j, (name, a) in enumerate(zip(names, arrays)):
        call.gather_blocks(name, a, (j + flip) % 2 == 1)
    out = call.run(in_turn(n))
    return [out[name] for name in names]


def first_gather(x, gain, parts, paired_outs, call_id):
    n = lax.axis_size("seq")
    call = Call(call_id)
    call.take("x", x)
    call.take("gain", gain)
    height = parts[2].shape[0]
    for name, a in zip("qkv", parts):
        call.take(name, a)
    for i, a in enumerate(paired_outs):
        call.take(f"o{i}", a)
    call.give("normed", x.shape, BF)
    call.give("outs", (height, sum(a.shape[0] for a in paired_outs)), BF)
    width = parts[0].shape[0] + parts[1].shape[0] + parts[2].shape[1]
    call.hold("src", (height, width), BF)
    call.give("w", (n * height, width), BF, pl.ANY)
    half = height // 2
    for p in range(2):
        call.gather(f"w.{p}", "src", "w", by_block(height, p * half, half), p == 1, (p * half, half))
    rows = x.shape[0] // n

    def body(at, rings):
        first = at["gain"][:1].astype(F32)
        kinds = [at["q"][...].astype(F32).T, at["k"][...].astype(F32).T, at["v"][...].astype(F32)]
        pieces = []
        for g in range(2):
            for a in kinds:
                size = a.shape[1] // 2
                pieces.append(a[:, g * size : (g + 1) * size])
        at["src"][...] = jnp.concatenate(pieces, axis=1).astype(BF)
        for k in range(n):
            if k % 2 == 0:
                for ring in rings.values():
                    ring.step()
            lines = slice(k * rows, (k + 1) * rows)
            at["normed"][lines] = rms_norm(at["x"][lines].astype(F32), first).astype(BF)
            if k == 1:
                both = [at[f"o{i}"][...].astype(F32) for i in range(len(paired_outs))]
                at["outs"][...] = jnp.concatenate(both, axis=0).T.astype(BF)

    out = call.run(body)
    return out["normed"], out["w"], out["outs"]


class ScatterRing:
    def __init__(self, n, where, left, right, out, sums, slots, send, recv, flip, axis, span):
        self.axis, self.span = axis, slice(*span)
        self.n, self.left_ref, self.right_ref, self.out = n, left, right, out
        self.sums, self.slots, self.send, self.recv = sums, slots, send, recv
        self.pos, self.right, self.left = where
        d = -1 if flip else 1
        self.hops = {d: n // 2, -d: (n - 1) // 2}
        self.order = (d, -d)
        self.done = 0
        self.steps = n // 2

    def term(self, r):
        owner = ring_device(lax.rem(self.pos + (r % self.n), self.n))
        right = self.right_ref[:, self.span] if self.axis == 0 else self.right_ref[self.span]
        return dot(self.left_ref[owner], right, 0, self.axis)

    def copy(self, d, h):
        i = 0 if d == 1 else 1
        return pltpu.make_async_remote_copy(
            src_ref=self.sums.at[i, h - 1],
            dst_ref=self.slots.at[i, h - 1],
            send_sem=self.send.at[i, h - 1],
            recv_sem=self.recv.at[i, h - 1],
            device_id={"seq": self.right if d == 1 else self.left},
            device_id_type=MESH,
        )

    def step(self):
        if self.done == self.steps:
            return
        self.done += 1
        h = self.done
        for d in self.order:
            if h > self.hops[d]:
                continue
            i = 0 if d == 1 else 1
            total = self.term(d * (self.hops[d] - h + 1))
            if h > 1:
                self.copy(d, h - 1).wait_recv()
                total = total + self.slots[i, h - 2].astype(F32)
            self.sums[i, h - 1] = total.astype(BF)
            self.copy(d, h).start()

    def finish(self):
        while self.done < self.steps:
            self.step()
        total = self.term(0)
        for d in self.order:
            i, h = (0 if d == 1 else 1), self.hops[d]
            self.copy(d, h).wait_recv()
            total = total + self.slots[i, h - 1].astype(F32)
        self.out[:, self.span] = total
        for d in self.order:
            for h in range(1, self.hops[d] + 1):
                self.copy(d, h).wait_send()


def scatter_all(lefts, pairs, call_id, flip=0, small=None, after=()):
    n = lax.axis_size("seq")
    pairs = [p if len(p) == 3 else p + (0,) for p in pairs]
    if not ring_size(n):
        sums = [
            lax.psum_scatter(
                dot(lefts[i], right, 0, axis).astype(BF), "seq", scatter_dimension=0, tiled=True
            ).astype(F32)
            for i, right, axis in pairs
        ]
        return sums if small is None else sums + [lax.psum(small.astype(BF), "seq").astype(F32)]
    call = Call(call_id)
    names = [str(j) for j in range(len(pairs))]
    for j, a in enumerate(after):
        call.take(f"after{j}", a, pl.ANY)
    if small is not None:
        call.take("small.src", small)
        call.hold("small.all", (n * small.shape[0], small.shape[1]), F32)
        call.gather("small", "small.src", "small.all", by_block(small.shape[0]))
    for i, a in enumerate(lefts):
        call.left(f"left{i}", a)
    for j, (i, right, axis) in enumerate(pairs):
        call.scatter(names[j], f"left{i}", right, (j + flip) % 2 == 1, axis)
    if small is not None:
        names.append(call.give("small.sum", small.shape, F32))

    def body(at, rings):
        in_turn(n)(at, rings)
        if small is not None:
            rings["small"].finish()
            rows = small.shape[0]
            blocks = [at["small.all"][b * rows : (b + 1) * rows] for b in range(n)]
            at["small.sum"][...] = sum(blocks[1:], blocks[0])
            del rings["small"]

    out = call.run(body)
    return [out[name] for name in names]


def small_sum(x, axis):
    size = lax.axis_size(axis)
    if size > 8:
        return lax.psum(x.astype(BF), axis).astype(F32)
    sent = x.astype(BF)
    routes = [[(i, (i + k) % size) for i in range(size)] for k in range(1, size)]
    return x + sum(lax.ppermute(sent, axis, r).astype(F32) for r in routes)


def dot(a, b, ca, cb):
    return lax.dot_general(a, b, (((ca,), (cb,)), ((), ())), preferred_element_type=F32)


def head_masks(query_width, value_width):
    lane_q = lax.broadcasted_iota(jnp.int32, (1, query_width), 1)
    lane_v = lax.broadcasted_iota(jnp.int32, (1, value_width), 1)
    heads = query_width // QK
    return [
        (
            (lane_q >= h * QK) & (lane_q < (h + 1) * QK),
            (lane_v >= h * VH) & (lane_v < (h + 1) * VH),
        )
        for h in range(heads)
    ]


def query_mask(scal_ref, place_ref, tok, row):
    offset = scal_ref[1 + row]
    pos = scal_ref[0] + lax.broadcasted_iota(jnp.int32, (tok, 1), 0)
    low = jnp.where(pos >= offset, offset, 0)
    other = place_ref[...]
    return (other >= low) & (other <= pos)


def key_mask(scal_ref, place_ref, tok, row):
    offset = scal_ref[1 + row]
    pos = scal_ref[0] + lax.broadcasted_iota(jnp.int32, (tok, 1), 0)
    high = jnp.where(pos >= offset, jnp.int32(1 << 30), offset)
    other = place_ref[...]
    return (other >= pos) & (other < high)


def attend_kernel(scal_ref, place_ref, q_ref, k_ref, v_ref, out_ref):
    q, k, v = q_ref[0], k_ref[0], v_ref[0]
    mask = query_mask(scal_ref, place_ref, q.shape[0], pl.program_id(0))
    total = jnp.zeros((q.shape[0], v.shape[1]), F32)
    for in_q, in_v in head_masks(q.shape[1], v.shape[1]):
        s = dot(jnp.where(in_q, q, jnp.zeros_like(q)), k, 1, 1) * (QK**-0.5)
        w = jnp.where(mask, 1.0 + s + 0.5 * s * s, 0.0)
        den = jnp.sum(w, axis=1, keepdims=True)
        total = total + jnp.where(in_v, dot(w.astype(BF), v, 1, 0) / den, 0.0)
    out_ref[0] = total.astype(BF)


def query_back_kernel(scal_ref, place_ref, q_ref, k_ref, v_ref, da_ref, dq_ref, dan_ref, extra_ref):
    q, k, v = q_ref[0], k_ref[0], v_ref[0]
    da = da_ref[0]
    tok = q.shape[0]
    mask = query_mask(scal_ref, place_ref, tok, pl.program_id(0))
    lane = lax.broadcasted_iota(jnp.int32, (1, q.shape[1]), 1)
    heads = q.shape[1] // QK
    dq = jnp.zeros(q.shape, F32)
    dan_all = jnp.zeros(da.shape, F32)
    extra = jnp.zeros(q.shape, F32)
    for h, (in_q, in_v) in enumerate(head_masks(q.shape[1], v.shape[1])):
        s = dot(jnp.where(in_q, q, jnp.zeros_like(q)), k, 1, 1) * (QK**-0.5)
        w = jnp.where(mask, 1.0 + s + 0.5 * s * s, 0.0)
        den = jnp.sum(w, axis=1, keepdims=True)
        att = dot(w.astype(BF), v, 1, 0) / den
        dan = jnp.where(in_v, da / den, 0.0).astype(BF)
        dan_f = dan.astype(F32)
        delta = jnp.sum(dan_f * att, axis=1, keepdims=True)
        d_kernel = dot(dan, v, 1, 1) - delta
        ds = jnp.where(mask, d_kernel * (1.0 + s), 0.0).astype(BF)
        dq = dq + jnp.where(in_q, dot(ds, k, 1, 0) * (QK**-0.5), 0.0)
        dan_all = dan_all + dan_f
        high = delta.astype(BF).astype(F32)
        extra = extra + jnp.where(lane == h, high, 0.0)
        extra = extra + jnp.where(lane == heads + h, delta - high, 0.0)
    dq_ref[0] = dq.astype(BF)
    dan_ref[0] = dan_all.astype(BF)
    extra_ref[0] = extra.astype(BF)


def key_back_kernel(scal_ref, place_ref, k_ref, v_ref, q_ref, dan_ref, extra_ref, dk_ref, dv_ref):
    k, v = k_ref[0], v_ref[0]
    q, dan, extra = q_ref[0], dan_ref[0], extra_ref[0]
    tok = k.shape[0]
    mask = key_mask(scal_ref, place_ref, tok, pl.program_id(0))
    lane = lax.broadcasted_iota(jnp.int32, (tok, k.shape[1]), 1)
    heads = k.shape[1] // QK
    dk = jnp.zeros(k.shape, F32)
    dv = jnp.zeros(v.shape, F32)
    for h, (in_q, in_v) in enumerate(head_masks(k.shape[1], v.shape[1])):
        s = dot(jnp.where(in_q, k, jnp.zeros_like(k)), q, 1, 1) * (QK**-0.5)
        w = jnp.where(mask, 1.0 + s + 0.5 * s * s, 0.0).astype(BF)
        dv = dv + jnp.where(in_v, dot(w, dan, 1, 0), 0.0)
        pick = jnp.where((lane == h) | (lane == heads + h), 1.0, 0.0).astype(BF)
        d_kernel = dot(jnp.where(in_v, v, jnp.zeros_like(v)), dan, 1, 1) - dot(pick, extra, 1, 1)
        ds = jnp.where(mask, d_kernel * (1.0 + s), 0.0).astype(BF)
        dk = dk + jnp.where(in_q, dot(ds, q, 1, 0) * (QK**-0.5), 0.0)
    dk_ref[0] = dk.astype(BF)
    dv_ref[0] = dv.astype(BF)


class Exchange:
    def __init__(self, n, at, name, block, place):
        self.n, self.block, self.place = n, block, place
        self.send, self.recv = at[name + ".send"], at[name + ".recv"]
        self.me = lax.axis_index("seq")

    def copy(self, k):
        partner = lax.rem(self.me + k, self.n)
        return pltpu.make_async_remote_copy(
            src_ref=self.block(partner),
            dst_ref=self.place(self.me),
            send_sem=self.send.at[k],
            recv_sem=self.recv.at[k],
            device_id={"seq": partner},
            device_id_type=MESH,
        )

    def own(self):
        return pltpu.make_async_copy(self.block(self.me), self.place(self.me), self.send.at[0])

    def start(self):
        for k in range(1, self.n):
            self.copy(k).start()
        self.own().start()

    def wait(self):
        self.own().wait()
        for k in range(1, self.n):
            self.copy(k).wait_recv()

    def wait_sent(self):
        for k in range(1, self.n):
            self.copy(k).wait_send()


def to_pair(ref, features, tok):
    def block(partner):
        rows = pl.ds(pl.multiple_of(lax.rem(partner, 2) * features, 16), features)
        return ref.at[rows, pl.ds(pl.multiple_of((partner // 2) * tok, 128), tok)]

    return block


def at_positions(ref, tok):
    return lambda device: ref.at[:, pl.ds(pl.multiple_of(device * tok, 128), tok)]


def causal(offset, i, tok):
    shape = ((i + 1) * tok, tok)
    earlier = lax.broadcasted_iota(jnp.int32, shape, 0)
    pos = i * tok + lax.broadcasted_iota(jnp.int32, shape, 1)
    return (earlier <= pos) & ((earlier >= offset) | (pos < offset))


def attend_pairs(off, weight, normed, carried, call_id):
    n = lax.axis_size("seq")
    count = normed.shape[0]
    tok = count * 2 // n
    features = weight.shape[1] // 2
    vf = features - 4 * QK
    call = Call(call_id)
    call.take("off", off, pltpu.SMEM)
    call.take("weight", weight)
    call.take("normed", normed)
    call.hold("qkv", (2 * features, count), BF)
    call.hold("mixed_t", (2 * vf, count), BF)
    for j, a in enumerate(carried):
        call.gather_blocks(f"c{j}", a, j % 2 == 1)
    call.give("mixed", (count, 2 * vf), BF)
    call.give("all", (features, n * tok), BF)
    call.give("att", (vf, n * tok), F32)
    call.give("den", (8, n * tok), F32)
    call.hold("own", (vf, n * tok), BF)
    call.exchange("in")
    call.exchange("out")

    def incoming(at):
        return Exchange(n, at, "in", to_pair(at["qkv"], features, tok), at_positions(at["all"], tok))

    def body(at, rings):
        def turn():
            for ring in rings.values():
                ring.step()

        turn()
        half = count // 2
        for p in range(2):
            part = dot(at["normed"][p * half : (p + 1) * half], at["weight"][...], 1, 0)
            at["qkv"][:, p * half : (p + 1) * half] = part.T.astype(BF)
        arriving = incoming(at)
        arriving.start()
        arriving.wait()
        turn()
        me = lax.axis_index("seq")
        offset = at["off"][me // 2]
        whole = at["all"]
        at["den"][...] = jnp.ones_like(at["den"])
        for h in range(2):
            lines = slice(h * vf // 2, (h + 1) * vf // 2)
            for i in range(n):
                here, upto = slice(i * tok, (i + 1) * tok), slice(0, (i + 1) * tok)
                q = whole[h * QK : (h + 1) * QK, here]
                k = whole[(2 + h) * QK : (3 + h) * QK, upto]
                v = whole[4 * QK + h * vf // 2 : 4 * QK + (h + 1) * vf // 2, upto]
                s = dot(k, q, 0, 0) * (QK**-0.5)
                w = jnp.where(causal(offset, i, tok), 1.0 + s + 0.5 * s * s, 0.0)
                den = jnp.sum(w, axis=0, keepdims=True)
                att = dot(v, w.astype(BF), 1, 0) / den
                at["att"][lines, here] = att
                at["den"][h : h + 1, here] = den
                at["own"][lines, here] = att.astype(BF)
        leaving = Exchange(
            n, at, "out", at_positions(at["own"], tok), lambda me: to_pair(at["mixed_t"], vf, tok)(me)
        )
        leaving.start()
        for _ in range(n // 2):
            turn()
        arriving.wait_sent()
        leaving.wait()
        at["mixed"][...] = at["mixed_t"][...].astype(F32).T.astype(BF)
        leaving.wait_sent()

    out = call.run(body)
    return out, [out[f"c{j}"] for j in range(len(carried))]


def attend_pairs_back(off, grad, out_t, weight, kept, scatters, call_id):
    n = lax.axis_size("seq")
    whole = kept["all"]
    features, tok = whole.shape[0], whole.shape[1] // n
    vf = features - 4 * QK
    call = Call(call_id)
    call.take("off", off, pltpu.SMEM)
    call.take("grad", grad)
    call.take("out_t", out_t)
    call.take("weight", weight)
    count, width = grad.shape
    call.hold("da", (2 * vf, count), BF)
    for name in ("all", "att", "den"):
        call.take(name, kept[name])
    lefts, pairs = scatters
    for i, a in enumerate(lefts):
        call.left(f"left{i}", a)
    for j, (i, right) in enumerate(pairs):
        call.scatter(f"s{j}", f"left{i}", right, j % 2 == 1)
    call.give("d", (count, 2 * features), BF)
    call.give("part", (count, width), BF)
    call.hold("d_t", (2 * features, count), BF)
    call.hold("da_all", (vf, n * tok), BF)
    call.hold("sum", (2 * QK + vf, n * tok), F32)
    call.hold("own", (features, n * tok), BF)
    call.exchange("in")
    call.exchange("out")

    def incoming(at):
        return Exchange(n, at, "in", to_pair(at["da"], vf, tok), at_positions(at["da_all"], tok))

    def body(at, rings):
        half = count // 2
        for p in range(2):
            part = dot(at["grad"][p * half : (p + 1) * half], at["out_t"][:, : 2 * vf], 1, 0)
            at["da"][:, p * half : (p + 1) * half] = part.T.astype(BF)
        arriving = incoming(at)
        arriving.start()
        arriving.wait()
        for ring in rings.values():
            ring.step()
        me = lax.axis_index("seq")
        offset = at["off"][me // 2]
        whole = at["all"]
        total = at["sum"]
        for h in range(2):
            lines = slice(h * vf // 2, (h + 1) * vf // 2)
            k_lines = slice(h * QK, (h + 1) * QK)
            v_lines = slice(2 * QK + h * vf // 2, 2 * QK + (h + 1) * vf // 2)
            for i in range(n - 1, -1, -1):
                here, upto = slice(i * tok, (i + 1) * tok), slice(0, (i + 1) * tok)
                q = whole[h * QK : (h + 1) * QK, here]
                k = whole[(2 + h) * QK : (3 + h) * QK, upto]
                v = whole[4 * QK + h * vf // 2 : 4 * QK + (h + 1) * vf // 2, upto]
                mask = causal(offset, i, tok)
                s = dot(k, q, 0, 0) * (QK**-0.5)
                w = jnp.where(mask, 1.0 + s + 0.5 * s * s, 0.0).astype(BF)
                dan = (at["da_all"][lines, here].astype(F32) / at["den"][h : h + 1, here]).astype(BF)
                delta = jnp.sum(dan.astype(F32) * at["att"][lines, here], axis=0, keepdims=True)
                ds = jnp.where(mask, (dot(v, dan, 0, 0) - delta) * (1.0 + s), 0.0).astype(BF)
                dq = dot(k, ds, 1, 0) * (QK**-0.5)
                at["own"][h * QK : (h + 1) * QK, here] = dq.astype(BF)
                dk = dot(q, ds, 1, 1) * (QK**-0.5)
                dv = dot(dan, w, 1, 1)
                if i == n - 1:
                    total[k_lines, upto] = dk
                    total[v_lines, upto] = dv
                else:
                    total[k_lines, upto] += dk
                    total[v_lines, upto] += dv
        at["own"][2 * QK :, :] = total[...].astype(BF)
        leaving = Exchange(
            n, at, "out", at_positions(at["own"], tok), lambda me: to_pair(at["d_t"], features, tok)(me)
        )
        leaving.start()
        for ring in rings.values():
            ring.step()
        leaving.wait()
        at["d"][...] = at["d_t"][...].astype(F32).T.astype(BF)
        for j in range(width // 256):
            lines = slice(j * 256, (j + 1) * 256)
            at["part"][:, lines] = dot(at["d"][...], at["weight"][lines, :], 1, 1).astype(BF)
        for _ in range(n // 2):
            for ring in rings.values():
                ring.step()
        arriving.wait_sent()
        leaving.wait_sent()

    out = call.run(body)
    return out["d"], out["part"], [out[f"s{j}"] for j in range(len(pairs))]


def by_rows(kernel, scal, place, operands, widths, kinds):
    rows = operands[0].shape[0]
    tok = operands[0].shape[1]
    specs = [
        pl.BlockSpec(memory_space=pltpu.SMEM),
        pl.BlockSpec(place.shape, lambda r: (0, 0)),
    ]
    specs += [pl.BlockSpec((1,) + a.shape[1:], lambda r: (r, 0, 0)) for a in operands]
    return pl.pallas_call(
        kernel,
        grid=(rows,),
        in_specs=specs,
        out_specs=[pl.BlockSpec((1, tok, w), lambda r: (r, 0, 0)) for w in widths],
        out_shape=[jax.ShapeDtypeStruct((rows, tok, w), t) for w, t in zip(widths, kinds)],
        compiler_params=pltpu.CompilerParams(vmem_limit_bytes=48 * 1024 * 1024),
    )(scal, place, *operands)


def rms_scale(x):
    return lax.rsqrt(jnp.mean(x * x, axis=-1, keepdims=True) + EPSILON)


def rms_norm(x, gain):
    return x * rms_scale(x) * gain


def rms_back(x, gain, dn):
    scale = rms_scale(x)
    unit = x * scale
    gain_grad = jnp.sum(dn * unit, axis=0)
    dg = dn * gain
    dx = scale * (dg - unit * jnp.mean(dg * unit, axis=-1, keepdims=True))
    return dx, gain_grad


def closing_kernel(count, *refs):
    x_ref, dn_ref, grad_ref, gain_ref, qkv_ref, small_ref = refs[:6]
    srcs, turned, refs = refs[6 : 6 + count], refs[6 + count : 8 + count], refs[8 + count :]
    out_ref, (q_ref, k_ref, v_ref), gains_ref, taps_ref = refs[0], refs[1:4], refs[4], refs[5]
    across, dsts = refs[6:8], refs[8:]
    gain = gain_ref[:1].astype(F32)
    dx, _ = rms_back(x_ref[...].astype(F32), gain, dn_ref[...].astype(F32))
    out_ref[...] = grad_ref[...] + dx
    for src, dst in zip(srcs, dsts):
        dst[...] = src[...]

    @pl.when(pl.program_id(0) == 0)
    def _():
        q, v = q_ref.shape[0] // 2, v_ref.shape[1] // 2
        halves = [qkv_ref[:, g * (2 * q + v) : (g + 1) * (2 * q + v)] for g in range(2)]
        q_ref[...] = jnp.concatenate([a[:, :q] for a in halves], axis=1).T
        k_ref[...] = jnp.concatenate([a[:, q : 2 * q] for a in halves], axis=1).T
        v_ref[...] = jnp.concatenate([a[:, 2 * q :] for a in halves], axis=1)
        norms = gains_ref.shape[0]
        gains_ref[...] = small_ref[:norms]
        taps_ref[...] = small_ref[norms : norms + taps_ref.shape[0], : taps_ref.shape[1]]

    for i in range(2):

        @pl.when(pl.program_id(0) == i + 1)
        def _():
            across[i][...] = turned[i][...].T


def closing(x, dn, grad, gains, qkv, widths, small, taps, results, turned):
    steps = 4

    def rows(a):
        return pl.BlockSpec((a.shape[0] // steps, a.shape[1]), lambda i: (i, 0))

    def whole(a):
        return pl.BlockSpec(a.shape, lambda i: (0, 0))

    height = qkv.shape[0]
    fixed = [(widths[0], height), (widths[1], height), (height, widths[2]), gains.shape, taps.shape]
    fixed += [r.shape[::-1] for r in turned]
    fixed = [jax.ShapeDtypeStruct(k, F32) for k in fixed]
    same = [jax.ShapeDtypeStruct(r.shape, F32) for r in results]
    shape = jax.ShapeDtypeStruct(x.shape, F32)
    out = pl.pallas_call(
        partial(closing_kernel, len(results)),
        grid=(steps,),
        in_specs=[rows(x), rows(dn), rows(grad), whole(gains), whole(qkv), whole(small)]
        + [rows(r) for r in results]
        + [whole(r) for r in turned],
        out_specs=[rows(shape)] + [whole(k) for k in fixed] + [rows(a) for a in same],
        out_shape=[shape] + fixed + same,
        compiler_params=pltpu.CompilerParams(vmem_limit_bytes=58 * MIB),
    )(x, dn, grad, gains, qkv, small, *results, *turned)
    return out[0], (out[1].T, out[2].T, out[3]), out[4], out[5], out[6:8], out[8:]


def head_total(partial_sum):
    return lax.psum(partial_sum, "head").astype(F32)


def tie(xs, *others):
    return list(lax.optimization_barrier((tuple(xs), tuple(others)))[0])


def mlp_forward(resid, gain, weights):
    gate_w, up_w, down_t = weights
    normed = rms_norm(resid, gain).astype(BF)
    gate_val = dot(normed, gate_w, 1, 0)
    up_val = dot(normed, up_w, 1, 0)
    hidden = (gate_val * jax.nn.sigmoid(gate_val) * up_val).astype(BF)
    return dot(hidden, down_t, 1, 1).astype(BF), (normed, gate_val, up_val, hidden)


def mlp_scatter(kept, call_id, *others):
    (normed, grad_b), d_gate, d_up, hidden = kept
    normed, grad_b = tie((normed, grad_b), *others)
    return scatter_all((normed, grad_b), ((0, d_gate), (0, d_up), (1, hidden)), call_id)


def mlp_backward(grad_b, saved, weights):
    gate_w, up_w, down_t = weights
    normed, gate_val, up_val, hidden = saved
    dh = dot(grad_b, down_t, 1, 0)
    sig = jax.nn.sigmoid(gate_val)
    silu = gate_val * sig
    d_gate = (dh * up_val * (sig * (1.0 + gate_val * (1.0 - sig)))).astype(BF)
    d_up = (dh * silu).astype(BF)
    dn_part = (dot(d_gate, gate_w, 1, 1) + dot(d_up, up_w, 1, 1)).astype(BF)
    return dn_part, ((normed, grad_b), d_gate, d_up, hidden)


def shifted(block, before, shift):
    if shift == 0:
        return block
    return jnp.concatenate([before[:, before.shape[1] - shift :], block[:, :-shift]], axis=1)


def advanced(block, after, shift):
    if shift == 0:
        return block
    return jnp.concatenate([block[:, shift:], after[:, :shift]], axis=1)


def per_device(
    activations,
    offsets,
    cotangent,
    attn_query,
    attn_key,
    attn_value,
    attn_output,
    ffn1_gate,
    ffn1_up,
    ffn1_down,
    conv_input,
    conv_gate,
    conv_output,
    conv_kernel,
    ffn2_gate,
    ffn2_up,
    ffn2_down,
    norm_gains,
):
    n = lax.axis_size("seq")
    micro, row_count, tok, width = activations.shape
    rows = micro * row_count
    count = rows * tok
    qw, vw = attn_query.shape[1], attn_value.shape[1]
    cw = conv_input.shape[1]
    taps = conv_kernel.shape[0]
    here = lax.axis_index("seq")
    start = here * tok
    off = offsets.reshape(rows)

    paired = ring_size(n) and 2 * rows == n and qw == 4 * QK
    gains = norm_gains.astype(F32)
    kernel_f = conv_kernel.astype(F32)
    acts_flat = activations.reshape(count, width)
    inputs = acts_flat.astype(F32)
    grad_four = cotangent.reshape(count, width)
    if paired:
        normed_a, qkv_w, outs_s = first_gather(
            acts_flat,
            norm_gains,
            (attn_query.T, attn_key.T, attn_value),
            (attn_output, conv_output),
            1,
        )
    else:
        normed_a = rms_norm(inputs, gains[0]).astype(BF)
        qkv_s = jnp.concatenate([attn_query, attn_key, attn_value], axis=1)
        (qkv_w,) = gather_all([qkv_s], 1)
        outs_s = jnp.concatenate([attn_output.T, conv_output.T], axis=1)

    scal = jnp.concatenate([start[None].astype(jnp.int32), off])
    place = jnp.arange(n * tok, dtype=jnp.int32).reshape(1, n * tok)

    def by_sequence(blocks):
        return jnp.swapaxes(blocks.reshape(n, rows, tok, -1), 0, 1).reshape(rows, n * tok, -1)

    if paired:
        attention, (outs_t, gate_1) = attend_pairs(off, qkv_w, normed_a, (outs_s, ffn1_gate), 2)
        mixed = attention["mixed"]
    else:
        qkv = dot(normed_a, qkv_w, 1, 0).astype(BF)
        qkv_all = by_sequence(gather_all([qkv], 2)[0])
        own = qkv.reshape(rows, tok, -1)
        q_own, k_own, v_own = own[..., :qw], own[..., qw : 2 * qw], own[..., 2 * qw :]
        q_all, k_all, v_all = qkv_all[..., :qw], qkv_all[..., qw : 2 * qw], qkv_all[..., 2 * qw :]
        (mixed,) = by_rows(attend_kernel, scal, place, (q_own, k_all, v_all), (vw,), (BF,))
        mixed = mixed.reshape(count, vw)
        outs_t, gate_1 = gather_all((outs_s, ffn1_gate), 11)
    out_t, conv_out_t = outs_t[:, :vw], outs_t[:, vw:]
    attn_part = dot(mixed, out_t, 1, 1).astype(BF)
    attn_sum = head_total(attn_part)
    ffn1 = [gate_1] + gather_all(tie((ffn1_up, ffn1_down.T), attn_part), 12)
    resid_one = inputs + attn_sum
    part, kept_one = mlp_forward(resid_one, gains[1], ffn1)
    ffn1_sum = head_total(part)
    pair_s = jnp.concatenate([conv_input, conv_gate], axis=1)
    pair_w, gate_2 = gather_all(tie((pair_s, ffn2_gate), part), 4)
    resid_two = resid_one + ffn1_sum

    normed_c = rms_norm(resid_two, gains[2]).astype(BF)
    pair_c = dot(normed_c, pair_w, 1, 0)
    inner = pair_c[:, :cw].reshape(rows, tok, cw)
    gate_c = pair_c[:, cw:].reshape(rows, tok, cw)
    pos = start + jnp.arange(tok + taps - 1, dtype=jnp.int32)
    current = pos[None, :] >= off[:, None]

    def valid(t, first, length):
        p = pos[None, first : first + length]
        source = p - t
        same = (source >= off[:, None]) == current[:, first : first + length]
        return ((source >= 0) & same).astype(F32)[:, :, None]

    edge = lax.ppermute(inner[:, tok - (taps - 1) :], "seq", [(i, i + 1) for i in range(n - 1)])
    moved = [shifted(inner, edge, t) * valid(t, 0, tok) for t in range(taps)]
    conv = sum(kernel_f[t][None, None, :] * moved[t] for t in range(taps))
    product = (conv * gate_c).astype(BF).reshape(count, cw)
    conv_part = dot(product, conv_out_t, 1, 1).astype(BF)
    conv_sum = head_total(conv_part)
    ffn2 = [gate_2] + gather_all(tie((ffn2_up, ffn2_down.T), conv_part), 12)
    resid_three = resid_two + conv_sum
    out_part, kept_two = mlp_forward(resid_three, gains[3], ffn2)

    dn_part, grads_two = mlp_backward(grad_four, kept_two, ffn2)
    both = lax.psum(jnp.concatenate([dn_part, out_part]), "head")
    dn, out_sum = both[:count].astype(F32), both[count:]
    sums_two = mlp_scatter(grads_two, 5, dn_part, out_part)
    (dn,) = tie((dn,), *sums_two)
    block_output = (resid_three + out_sum.astype(F32)).astype(BF).reshape(activations.shape)
    dx, gain_four = rms_back(resid_three, gains[3], dn)
    grad_three = grad_four.astype(F32) + dx
    grad_b = grad_three.astype(BF)
    d_product = dot(grad_b, conv_out_t, 1, 0).reshape(rows, tok, cw)
    d_gate_c = (d_product * conv).astype(BF).reshape(count, cw)
    d_conv = d_product * gate_c
    next_rows = lax.ppermute(d_conv[:, : taps - 1], "seq", [(i + 1, i) for i in range(n - 1)])
    d_inner = sum(
        kernel_f[t][None, None, :] * advanced(d_conv, next_rows, t) * valid(t, t, tok)
        for t in range(taps)
    )
    d_inner = d_inner.astype(BF).reshape(count, cw)
    kernel_grad = jnp.stack([jnp.sum(d_conv * moved[t], axis=(0, 1)) for t in range(taps)])
    d_pair = jnp.concatenate([d_inner, d_gate_c], axis=1)
    dn_part = dot(d_pair, pair_w, 1, 1).astype(BF)
    dn = head_total(dn_part)
    sums_conv = scatter_all(
        tie((normed_c, grad_b), dn_part),
        ((0, d_pair), (1, product)),
        6,
        1,
    )
    (dn,) = tie((dn,), *sums_conv)
    dx, gain_three = rms_back(resid_two, gains[2], dn)
    grad_two = grad_three + dx
    dn_part, grads_one = mlp_backward(grad_two.astype(BF), kept_one, ffn1)
    dn = head_total(dn_part)
    (normed_1, grad_b1), d_gate_1, d_up_1, hidden_1 = grads_one
    if ring_size(n):
        sums_one = scatter_all(tie((normed_1,), dn_part), ((0, d_gate_1),), 9)
        (dn,) = tie((dn,), *sums_one)
    dx, gain_two = rms_back(resid_one, gains[1], dn)
    grad_one = grad_two + dx

    grad_b = grad_one.astype(BF)
    later = ((normed_1, grad_b1), ((0, d_up_1), (1, hidden_1)))
    if paired:
        d_qkv, dn_part, more = attend_pairs_back(off, grad_b, outs_t, qkv_w, attention, later, 7)
        sums_one = sums_one + more
    else:
        da = dot(grad_b, out_t, 1, 0).reshape(rows, tok, vw)
        dq, dan, extra = by_rows(
            query_back_kernel, scal, place, (q_own, k_all, v_all, da), (qw, vw, qw), (BF, BF, BF)
        )
        back = jnp.concatenate([dan, extra], axis=-1).reshape(count, vw + qw)
        back_all = by_sequence(gather_all([back], 7, 1)[0])
        dk, dv = by_rows(
            key_back_kernel,
            scal,
            place,
            (k_own, v_own, q_all, back_all[..., :vw], back_all[..., vw:]),
            (qw, vw),
            (BF, BF),
        )
        sums_one = scatter_all((normed_1,), ((0, d_gate_1),), 9) + scatter_all(*later, 10)
        d_qkv = jnp.concatenate([dq, dk, dv], axis=-1).reshape(count, 2 * qw + vw)
        dn_part = dot(d_qkv, qkv_w, 1, 1).astype(BF)
    dn = lax.psum(dn_part, "head")
    unit = inputs * rms_scale(inputs)
    gain_one = small_sum(jnp.sum(dn_part.astype(F32) * unit, axis=0), "head")
    small = jnp.concatenate(
        [
            jnp.stack([gain_one, gain_two, gain_three, gain_four]),
            jnp.pad(kernel_grad, ((0, 0), (0, width - cw))),
            jnp.zeros((8 - 4 - taps, width), F32),
        ]
    )
    sums_attn = scatter_all(
        tie((normed_a, grad_b), dn_part), ((0, d_qkv), (1, mixed)), 8, 0, small
    )
    gains_grad, kernel_grad = sums_attn[2][:4], sums_attn[2][4 : 4 + taps, :cw]
    qkv_sum = sums_attn[0]
    straight = (sums_one[0], sums_one[1], sums_two[0], sums_two[1], sums_one[2], sums_two[2])
    turned = (sums_conv[1], sums_attn[1])
    if paired:
        input_grad, by_kind, gains_grad, kernel_grad, turned, straight = closing(
            acts_flat,
            dn,
            grad_one,
            norm_gains,
            qkv_sum,
            (qw, qw, vw),
            sums_attn[2],
            conv_kernel,
            straight,
            turned,
        )
    else:
        input_grad = grad_one + rms_back(inputs, gains[0], dn.astype(F32))[0]
        by_kind = (qkv_sum[:, :qw], qkv_sum[:, qw : 2 * qw], qkv_sum[:, 2 * qw :])
        turned = [r.T for r in turned]
    input_grad = input_grad.reshape(activations.shape)
    return (
        block_output,
        input_grad,
        *by_kind,
        turned[1],
        straight[0],
        straight[1],
        straight[4].T,
        sums_conv[0][:, :cw],
        sums_conv[0][:, cw:],
        turned[0],
        kernel_grad,
        straight[2],
        straight[3],
        straight[5].T,
        gains_grad,
    )


def solution(mesh):
    rows_in = P("seq", "head")
    rows_out = P("head", "seq")
    tokens = P(None, None, "seq", None)
    in_specs = (
        (tokens, P(), tokens)
        + (rows_in, rows_in, rows_in, rows_out)
        + (rows_in, rows_in, rows_out)
        + (rows_in, rows_in, rows_out)
        + (P(None, "head"),)
        + (rows_in, rows_in, rows_out)
        + (P(),)
    )
    out_specs = (
        (tokens, tokens)
        + (rows_in, rows_in, rows_in, rows_out)
        + (rows_in, rows_in, rows_out)
        + (rows_in, rows_in, rows_out)
        + (P(None, "head"),)
        + (rows_in, rows_in, rows_out)
        + (P(),)
    )
    return jax.shard_map(
        per_device, mesh=mesh, in_specs=in_specs, out_specs=out_specs, check_vma=False
    )
```

```python
from functools import partial

import jax
import jax.numpy as jnp
from jax import lax
from jax.experimental import pallas as pl
from jax.experimental.pallas import tpu as pltpu
from jax.sharding import PartitionSpec as P

QK = 16
VH = 112
EPSILON = 1e-05
BF = jnp.bfloat16
F32 = jnp.float32


MESH = pl.DeviceIdType.MESH
ANY = pl.BlockSpec(memory_space=pl.ANY)


def ring_device(p):
    return jnp.where(p < 4, 2 * p, 15 - 2 * p)


def ring_position(s):
    return jnp.where(lax.rem(s, 2) == 0, s // 2, 7 - s // 2)


def ring_size(n):
    return n == 8


def greet(n, everyone=False):
    me = lax.axis_index("seq")
    pos = ring_position(me)
    right = ring_device(lax.rem(pos + 1, n))
    left = ring_device(lax.rem(pos + n - 1, n))
    barrier = pltpu.get_barrier_semaphore()
    partners = [lax.rem(me + k, n) for k in range(1, n)] if everyone else [left, right]
    for partner in partners:
        pl.semaphore_signal(barrier, inc=1, device_id={"seq": partner}, device_id_type=MESH)
    pl.semaphore_wait(barrier, len(partners))
    return pos, right, left


class GatherRing:
    def __init__(self, n, where, src, out, place, send, recv, local, flip):
        self.n, self.src, self.out, self.place = n, src, out, place
        self.send, self.recv, self.local = send, recv, local
        self.pos, self.right, self.left = where
        self.flip = flip
        self.steps = n // 2
        self.done = 0

    def block(self, r):
        return self.place(self.out, ring_device(lax.rem(self.pos + (r % self.n), self.n)))

    def copy(self, k, d):
        block = self.block(-d * (k - 1))
        i = 0 if d == 1 else 1
        return pltpu.make_async_remote_copy(
            src_ref=self.src if k == 1 else block,
            dst_ref=block,
            send_sem=self.send.at[i, k - 1],
            recv_sem=self.recv.at[i, k - 1],
            device_id={"seq": self.right if d == 1 else self.left},
            device_id_type=MESH,
        )

    def ways(self, k):
        if k <= (self.n - 1) // 2:
            return (1, -1)
        return (-1,) if self.flip else (1,)

    def step(self):
        if self.done == self.steps:
            return
        if self.done == 0:
            pltpu.make_async_copy(self.src, self.block(0), self.local).start()
        self.done += 1
        k = self.done
        for d in self.ways(k):
            if k > 1:
                self.copy(k - 1, d).wait_recv()
            self.copy(k, d).start()

    def finish(self):
        while self.done < self.steps:
            self.step()
        pltpu.make_async_copy(self.src, self.block(0), self.local).wait()
        last = {d: max(k for k in range(1, self.steps + 1) if d in self.ways(k)) for d in (1, -1)}
        for d in (1, -1):
            self.copy(last[d], d).wait_recv()
        for k in range(1, self.steps + 1):
            for d in self.ways(k):
                self.copy(k, d).wait_send()


def by_block(height, first=0, rows=None):
    rows = height if rows is None else rows
    unit = 8 if height % 16 else 16
    return lambda ref, owner: ref.at[pl.ds(pl.multiple_of(owner * height + first, unit), rows)]


def by_position(tok):
    return lambda ref, owner: ref.at[:, pl.ds(pl.multiple_of(owner * tok, 16), tok)]


VMEM = pltpu.VMEM
MIB = 1024 * 1024


class Call:
    def __init__(self, call_id):
        self.n = lax.axis_size("seq")
        self.call_id = call_id
        self.ins, self.outs, self.scratch = {}, {}, {}
        self.gathers, self.scatters = {}, {}
        self.exchanges = []

    def exchange(self, name):
        self.sems(name + ".send", self.n)
        self.sems(name + ".recv", self.n)
        self.exchanges.append(name)

    def take(self, name, array, space=VMEM):
        self.ins[name] = (array, pl.BlockSpec(memory_space=space))
        return name

    def give(self, name, shape, kind, space=VMEM):
        self.outs[name] = (jax.ShapeDtypeStruct(shape, kind), pl.BlockSpec(memory_space=space))
        return name

    def hold(self, name, shape, kind):
        self.scratch[name] = VMEM(shape, kind)
        return name

    def sems(self, name, *shape):
        self.scratch[name] = pltpu.SemaphoreType.DMA(shape)

    def gather_blocks(self, name, array, flip=False):
        height = array.shape[0]
        self.take(name + ".src", array, pl.ANY)
        self.give(name, (self.n * height,) + array.shape[1:], array.dtype, pl.ANY)
        half = height // 2
        for p in range(2):
            self.gather(
                f"{name}.{p}",
                name + ".src",
                name,
                by_block(height, p * half, half),
                bool(p) != flip,
                (p * half, half),
            )

    def gather(self, name, src, out, place, flip=False, rows=None):
        half = self.n // 2
        self.sems(name + ".send", 2, half)
        self.sems(name + ".recv", 2, half)
        self.sems(name + ".local", 1)
        self.gathers[name] = (src, out, place, flip, rows)

    def left(self, name, array):
        self.take(name, array)
        rows, width = array.shape
        self.hold(name + ".blocked", (self.n, rows, width // self.n), BF)

    def scatter(self, name, left, right, flip=False, axis=0):
        n = self.n
        height = self.ins[left][0].shape[1] // n
        width = right.shape[1 - axis]
        self.take(name + ".right", right)
        self.give(name, (height, width), F32)
        cut = -(-width // 256) * 128
        for p, span in enumerate(((0, cut), (cut, width))):
            part = f"{name}.{p}"
            block = (height, span[1] - span[0])
            self.hold(part + ".sums", (2, n // 2) + block, BF)
            self.hold(part + ".slots", (2, n // 2) + block, BF)
            self.sems(part + ".send", 2, n // 2)
            self.sems(part + ".recv", 2, n // 2)
            self.scatters[part] = (name, left, bool(p) != flip, axis, span)

    def kernel(self, body, *refs):
        names = list(self.ins) + list(self.outs) + list(self.scratch)
        at = dict(zip(names, refs))
        where = greet(self.n, bool(self.exchanges))
        rings = {}
        for name, (src, out, place, flip, rows) in self.gathers.items():
            rings[name] = GatherRing(
                self.n,
                where,
                at[src] if rows is None else at[src].at[pl.ds(*rows)],
                at[out],
                place,
                at[name + ".send"],
                at[name + ".recv"],
                at[name + ".local"].at[0],
                flip,
            )
        ready = set()
        for name, (whole, left, flip, axis, span) in self.scatters.items():
            blocked = at[left + ".blocked"]
            if left not in ready:
                ready.add(left)
                width = blocked.shape[2]
                for b in range(self.n):
                    blocked[b] = at[left][:, b * width : (b + 1) * width]
            rings[name] = ScatterRing(
                self.n,
                where,
                blocked,
                at[whole + ".right"],
                at[whole],
                at[name + ".sums"],
                at[name + ".slots"],
                at[name + ".send"],
                at[name + ".recv"],
                flip,
                axis,
                span,
            )
            rings[name].step()
        body(at, rings)
        for ring in rings.values():
            ring.finish()

    def run(self, body):
        outs = pl.pallas_call(
            partial(self.kernel, body),
            in_specs=[spec for _, spec in self.ins.values()],
            out_specs=[spec for _, spec in self.outs.values()],
            out_shape=[shape for shape, _ in self.outs.values()],
            scratch_shapes=list(self.scratch.values()),
            compiler_params=pltpu.CompilerParams(
                collective_id=self.call_id, has_side_effects=True, vmem_limit_bytes=58 * MIB
            ),
        )(*[array for array, _ in self.ins.values()])
        return dict(zip(self.outs, outs))


def in_turn(n):
    def body(at, rings):
        for _ in range(n // 2):
            for ring in rings.values():
                ring.step()

    return body


def gather_all(arrays, call_id, flip=0):
    n = lax.axis_size("seq")
    if not ring_size(n):
        return [lax.all_gather(a, "seq", axis=0, tiled=True) for a in arrays]
    call = Call(call_id)
    names = [str(j) for j in range(len(arrays))]
    for j, (name, a) in enumerate(zip(names, arrays)):
        call.gather_blocks(name, a, (j + flip) % 2 == 1)
    out = call.run(in_turn(n))
    return [out[name] for name in names]


def first_gather(x, gain, parts, paired_outs, call_id):
    n = lax.axis_size("seq")
    call = Call(call_id)
    call.take("x", x)
    call.take("gain", gain)
    height = parts[2].shape[0]
    for name, a in zip("qkv", parts):
        call.take(name, a)
    for i, a in enumerate(paired_outs):
        call.take(f"o{i}", a)
    call.give("normed", x.shape, BF)
    call.give("outs", (height, sum(a.shape[0] for a in paired_outs)), BF)
    width = parts[0].shape[0] + parts[1].shape[0] + parts[2].shape[1]
    call.hold("src", (height, width), BF)
    call.give("w", (n * height, width), BF, pl.ANY)
    half = height // 2
    for p in range(2):
        call.gather(f"w.{p}", "src", "w", by_block(height, p * half, half), p == 1, (p * half, half))
    rows = x.shape[0] // n

    def body(at, rings):
        first = at["gain"][:1].astype(F32)
        kinds = [at["q"][...].astype(F32).T, at["k"][...].astype(F32).T, at["v"][...].astype(F32)]
        pieces = []
        for g in range(2):
            for a in kinds:
                size = a.shape[1] // 2
                pieces.append(a[:, g * size : (g + 1) * size])
        at["src"][...] = jnp.concatenate(pieces, axis=1).astype(BF)
        for k in range(n):
            if k % 2 == 0:
                for ring in rings.values():
                    ring.step()
            lines = slice(k * rows, (k + 1) * rows)
            at["normed"][lines] = rms_norm(at["x"][lines].astype(F32), first).astype(BF)
            if k == 1:
                both = [at[f"o{i}"][...].astype(F32) for i in range(len(paired_outs))]
                at["outs"][...] = jnp.concatenate(both, axis=0).T.astype(BF)

    out = call.run(body)
    return out["normed"], out["w"], out["outs"]


class ScatterRing:
    def __init__(self, n, where, left, right, out, sums, slots, send, recv, flip, axis, span):
        self.axis, self.span = axis, slice(*span)
        self.n, self.left_ref, self.right_ref, self.out = n, left, right, out
        self.sums, self.slots, self.send, self.recv = sums, slots, send, recv
        self.pos, self.right, self.left = where
        d = -1 if flip else 1
        self.hops = {d: n // 2, -d: (n - 1) // 2}
        self.order = (d, -d)
        self.done = 0
        self.steps = n // 2

    def term(self, r):
        owner = ring_device(lax.rem(self.pos + (r % self.n), self.n))
        right = self.right_ref[:, self.span] if self.axis == 0 else self.right_ref[self.span]
        return dot(self.left_ref[owner], right, 0, self.axis)

    def copy(self, d, h):
        i = 0 if d == 1 else 1
        return pltpu.make_async_remote_copy(
            src_ref=self.sums.at[i, h - 1],
            dst_ref=self.slots.at[i, h - 1],
            send_sem=self.send.at[i, h - 1],
            recv_sem=self.recv.at[i, h - 1],
            device_id={"seq": self.right if d == 1 else self.left},
            device_id_type=MESH,
        )

    def step(self):
        if self.done == self.steps:
            return
        self.done += 1
        h = self.done
        for d in self.order:
            if h > self.hops[d]:
                continue
            i = 0 if d == 1 else 1
            total = self.term(d * (self.hops[d] - h + 1))
            if h > 1:
                self.copy(d, h - 1).wait_recv()
                total = total + self.slots[i, h - 2].astype(F32)
            self.sums[i, h - 1] = total.astype(BF)
            self.copy(d, h).start()

    def finish(self):
        while self.done < self.steps:
            self.step()
        total = self.term(0)
        for d in self.order:
            i, h = (0 if d == 1 else 1), self.hops[d]
            self.copy(d, h).wait_recv()
            total = total + self.slots[i, h - 1].astype(F32)
        self.out[:, self.span] = total
        for d in self.order:
            for h in range(1, self.hops[d] + 1):
                self.copy(d, h).wait_send()


def scatter_all(lefts, pairs, call_id, flip=0, small=None, after=()):
    n = lax.axis_size("seq")
    pairs = [p if len(p) == 3 else p + (0,) for p in pairs]
    if not ring_size(n):
        sums = [
            lax.psum_scatter(
                dot(lefts[i], right, 0, axis).astype(BF), "seq", scatter_dimension=0, tiled=True
            ).astype(F32)
            for i, right, axis in pairs
        ]
        return sums if small is None else sums + [lax.psum(small.astype(BF), "seq").astype(F32)]
    call = Call(call_id)
    names = [str(j) for j in range(len(pairs))]
    for j, a in enumerate(after):
        call.take(f"after{j}", a, pl.ANY)
    if small is not None:
        call.take("small.src", small)
        call.hold("small.all", (n * small.shape[0], small.shape[1]), F32)
        call.gather("small", "small.src", "small.all", by_block(small.shape[0]))
    for i, a in enumerate(lefts):
        call.left(f"left{i}", a)
    for j, (i, right, axis) in enumerate(pairs):
        call.scatter(names[j], f"left{i}", right, (j + flip) % 2 == 1, axis)
    if small is not None:
        names.append(call.give("small.sum", small.shape, F32))

    def body(at, rings):
        if small is not None:
            rings["small"] = rings.pop("small")
        in_turn(n)(at, rings)
        if small is not None:
            rings["small"].finish()
            rows = small.shape[0]
            blocks = [at["small.all"][b * rows : (b + 1) * rows] for b in range(n)]
            at["small.sum"][...] = sum(blocks[1:], blocks[0])
            del rings["small"]

    out = call.run(body)
    return [out[name] for name in names]


def small_sum(x, axis):
    size = lax.axis_size(axis)
    if size > 8:
        return lax.psum(x.astype(BF), axis).astype(F32)
    sent = x.astype(BF)
    routes = [[(i, (i + k) % size) for i in range(size)] for k in range(1, size)]
    return x + sum(lax.ppermute(sent, axis, r).astype(F32) for r in routes)


def dot(a, b, ca, cb):
    return lax.dot_general(a, b, (((ca,), (cb,)), ((), ())), preferred_element_type=F32)


def head_masks(query_width, value_width):
    lane_q = lax.broadcasted_iota(jnp.int32, (1, query_width), 1)
    lane_v = lax.broadcasted_iota(jnp.int32, (1, value_width), 1)
    heads = query_width // QK
    return [
        (
            (lane_q >= h * QK) & (lane_q < (h + 1) * QK),
            (lane_v >= h * VH) & (lane_v < (h + 1) * VH),
        )
        for h in range(heads)
    ]


def query_mask(scal_ref, place_ref, tok, row):
    offset = scal_ref[1 + row]
    pos = scal_ref[0] + lax.broadcasted_iota(jnp.int32, (tok, 1), 0)
    low = jnp.where(pos >= offset, offset, 0)
    other = place_ref[...]
    return (other >= low) & (other <= pos)


def key_mask(scal_ref, place_ref, tok, row):
    offset = scal_ref[1 + row]
    pos = scal_ref[0] + lax.broadcasted_iota(jnp.int32, (tok, 1), 0)
    high = jnp.where(pos >= offset, jnp.int32(1 << 30), offset)
    other = place_ref[...]
    return (other >= pos) & (other < high)


def attend_kernel(scal_ref, place_ref, q_ref, k_ref, v_ref, out_ref):
    q, k, v = q_ref[0], k_ref[0], v_ref[0]
    mask = query_mask(scal_ref, place_ref, q.shape[0], pl.program_id(0))
    total = jnp.zeros((q.shape[0], v.shape[1]), F32)
    for in_q, in_v in head_masks(q.shape[1], v.shape[1]):
        s = dot(jnp.where(in_q, q, jnp.zeros_like(q)), k, 1, 1) * (QK**-0.5)
        w = jnp.where(mask, 1.0 + s + 0.5 * s * s, 0.0)
        den = jnp.sum(w, axis=1, keepdims=True)
        total = total + jnp.where(in_v, dot(w.astype(BF), v, 1, 0) / den, 0.0)
    out_ref[0] = total.astype(BF)


def query_back_kernel(scal_ref, place_ref, q_ref, k_ref, v_ref, da_ref, dq_ref, dan_ref, extra_ref):
    q, k, v = q_ref[0], k_ref[0], v_ref[0]
    da = da_ref[0]
    tok = q.shape[0]
    mask = query_mask(scal_ref, place_ref, tok, pl.program_id(0))
    lane = lax.broadcasted_iota(jnp.int32, (1, q.shape[1]), 1)
    heads = q.shape[1] // QK
    dq = jnp.zeros(q.shape, F32)
    dan_all = jnp.zeros(da.shape, F32)
    extra = jnp.zeros(q.shape, F32)
    for h, (in_q, in_v) in enumerate(head_masks(q.shape[1], v.shape[1])):
        s = dot(jnp.where(in_q, q, jnp.zeros_like(q)), k, 1, 1) * (QK**-0.5)
        w = jnp.where(mask, 1.0 + s + 0.5 * s * s, 0.0)
        den = jnp.sum(w, axis=1, keepdims=True)
        att = dot(w.astype(BF), v, 1, 0) / den
        dan = jnp.where(in_v, da / den, 0.0).astype(BF)
        dan_f = dan.astype(F32)
        delta = jnp.sum(dan_f * att, axis=1, keepdims=True)
        d_kernel = dot(dan, v, 1, 1) - delta
        ds = jnp.where(mask, d_kernel * (1.0 + s), 0.0).astype(BF)
        dq = dq + jnp.where(in_q, dot(ds, k, 1, 0) * (QK**-0.5), 0.0)
        dan_all = dan_all + dan_f
        high = delta.astype(BF).astype(F32)
        extra = extra + jnp.where(lane == h, high, 0.0)
        extra = extra + jnp.where(lane == heads + h, delta - high, 0.0)
    dq_ref[0] = dq.astype(BF)
    dan_ref[0] = dan_all.astype(BF)
    extra_ref[0] = extra.astype(BF)


def key_back_kernel(scal_ref, place_ref, k_ref, v_ref, q_ref, dan_ref, extra_ref, dk_ref, dv_ref):
    k, v = k_ref[0], v_ref[0]
    q, dan, extra = q_ref[0], dan_ref[0], extra_ref[0]
    tok = k.shape[0]
    mask = key_mask(scal_ref, place_ref, tok, pl.program_id(0))
    lane = lax.broadcasted_iota(jnp.int32, (tok, k.shape[1]), 1)
    heads = k.shape[1] // QK
    dk = jnp.zeros(k.shape, F32)
    dv = jnp.zeros(v.shape, F32)
    for h, (in_q, in_v) in enumerate(head_masks(k.shape[1], v.shape[1])):
        s = dot(jnp.where(in_q, k, jnp.zeros_like(k)), q, 1, 1) * (QK**-0.5)
        w = jnp.where(mask, 1.0 + s + 0.5 * s * s, 0.0).astype(BF)
        dv = dv + jnp.where(in_v, dot(w, dan, 1, 0), 0.0)
        pick = jnp.where((lane == h) | (lane == heads + h), 1.0, 0.0).astype(BF)
        d_kernel = dot(jnp.where(in_v, v, jnp.zeros_like(v)), dan, 1, 1) - dot(pick, extra, 1, 1)
        ds = jnp.where(mask, d_kernel * (1.0 + s), 0.0).astype(BF)
        dk = dk + jnp.where(in_q, dot(ds, q, 1, 0) * (QK**-0.5), 0.0)
    dk_ref[0] = dk.astype(BF)
    dv_ref[0] = dv.astype(BF)


class Exchange:
    def __init__(self, n, at, name, block, place):
        self.n, self.block, self.place = n, block, place
        self.send, self.recv = at[name + ".send"], at[name + ".recv"]
        self.me = lax.axis_index("seq")

    def copy(self, k):
        partner = lax.rem(self.me + k, self.n)
        return pltpu.make_async_remote_copy(
            src_ref=self.block(partner),
            dst_ref=self.place(self.me),
            send_sem=self.send.at[k],
            recv_sem=self.recv.at[k],
            device_id={"seq": partner},
            device_id_type=MESH,
        )

    def own(self):
        return pltpu.make_async_copy(self.block(self.me), self.place(self.me), self.send.at[0])

    def start(self):
        for k in range(1, self.n):
            self.copy(k).start()
        self.own().start()

    def wait(self):
        self.own().wait()
        for k in range(1, self.n):
            self.copy(k).wait_recv()

    def wait_sent(self):
        for k in range(1, self.n):
            self.copy(k).wait_send()


def to_pair(ref, features, tok):
    def block(partner):
        rows = pl.ds(pl.multiple_of(lax.rem(partner, 2) * features, 16), features)
        return ref.at[rows, pl.ds(pl.multiple_of((partner // 2) * tok, 128), tok)]

    return block


def at_positions(ref, tok):
    return lambda device: ref.at[:, pl.ds(pl.multiple_of(device * tok, 128), tok)]


def causal(offset, i, tok):
    shape = ((i + 1) * tok, tok)
    earlier = lax.broadcasted_iota(jnp.int32, shape, 0)
    pos = i * tok + lax.broadcasted_iota(jnp.int32, shape, 1)
    return (earlier <= pos) & ((earlier >= offset) | (pos < offset))


def attend_pairs(off, weight, normed, carried, call_id):
    n = lax.axis_size("seq")
    count = normed.shape[0]
    tok = count * 2 // n
    features = weight.shape[1] // 2
    vf = features - 4 * QK
    call = Call(call_id)
    call.take("off", off, pltpu.SMEM)
    call.take("weight", weight)
    call.take("normed", normed)
    call.hold("qkv", (2 * features, count), BF)
    call.hold("mixed_t", (2 * vf, count), BF)
    for j, a in enumerate(carried):
        call.gather_blocks(f"c{j}", a, j % 2 == 1)
    call.give("mixed", (count, 2 * vf), BF)
    call.give("all", (features, n * tok), BF)
    call.give("att", (vf, n * tok), F32)
    call.give("den", (8, n * tok), F32)
    call.hold("own", (vf, n * tok), BF)
    call.exchange("in")
    call.exchange("out")

    def incoming(at):
        return Exchange(n, at, "in", to_pair(at["qkv"], features, tok), at_positions(at["all"], tok))

    def body(at, rings):
        def turn():
            for ring in rings.values():
                ring.step()

        turn()
        half = count // 2
        for p in range(2):
            part = dot(at["normed"][p * half : (p + 1) * half], at["weight"][...], 1, 0)
            at["qkv"][:, p * half : (p + 1) * half] = part.T.astype(BF)
        arriving = incoming(at)
        arriving.start()
        arriving.wait()
        turn()
        me = lax.axis_index("seq")
        offset = at["off"][me // 2]
        whole = at["all"]
        at["den"][...] = jnp.ones_like(at["den"])
        for h in range(2):
            lines = slice(h * vf // 2, (h + 1) * vf // 2)
            for i in range(n):
                here, upto = slice(i * tok, (i + 1) * tok), slice(0, (i + 1) * tok)
                q = whole[h * QK : (h + 1) * QK, here]
                k = whole[(2 + h) * QK : (3 + h) * QK, upto]
                v = whole[4 * QK + h * vf // 2 : 4 * QK + (h + 1) * vf // 2, upto]
                s = dot(k, q, 0, 0) * (QK**-0.5)
                w = jnp.where(causal(offset, i, tok), 1.0 + s + 0.5 * s * s, 0.0)
                den = jnp.sum(w, axis=0, keepdims=True)
                att = dot(v, w.astype(BF), 1, 0) / den
                at["att"][lines, here] = att
                at["den"][h : h + 1, here] = den
                at["own"][lines, here] = att.astype(BF)
        leaving = Exchange(
            n, at, "out", at_positions(at["own"], tok), lambda me: to_pair(at["mixed_t"], vf, tok)(me)
        )
        leaving.start()
        for _ in range(n // 2):
            turn()
        arriving.wait_sent()
        leaving.wait()
        at["mixed"][...] = at["mixed_t"][...].astype(F32).T.astype(BF)
        leaving.wait_sent()

    out = call.run(body)
    return out, [out[f"c{j}"] for j in range(len(carried))]


def attend_pairs_back(off, grad, out_t, weight, kept, scatters, call_id):
    n = lax.axis_size("seq")
    whole = kept["all"]
    features, tok = whole.shape[0], whole.shape[1] // n
    vf = features - 4 * QK
    call = Call(call_id)
    call.take("off", off, pltpu.SMEM)
    call.take("grad", grad)
    call.take("out_t", out_t)
    call.take("weight", weight)
    count, width = grad.shape
    call.hold("da", (2 * vf, count), BF)
    for name in ("all", "att", "den"):
        call.take(name, kept[name])
    lefts, pairs = scatters
    for i, a in enumerate(lefts):
        call.left(f"left{i}", a)
    for j, (i, right) in enumerate(pairs):
        call.scatter(f"s{j}", f"left{i}", right, j % 2 == 1)
    call.give("d", (count, 2 * features), BF)
    call.give("part", (count, width), BF)
    call.hold("d_t", (2 * features, count), BF)
    call.hold("da_all", (vf, n * tok), BF)
    call.hold("sum", (2 * QK + vf, n * tok), F32)
    call.hold("own", (features, n * tok), BF)
    call.exchange("in")
    call.exchange("out")

    def incoming(at):
        return Exchange(n, at, "in", to_pair(at["da"], vf, tok), at_positions(at["da_all"], tok))

    def body(at, rings):
        half = count // 2
        for p in range(2):
            part = dot(at["grad"][p * half : (p + 1) * half], at["out_t"][:, : 2 * vf], 1, 0)
            at["da"][:, p * half : (p + 1) * half] = part.T.astype(BF)
        arriving = incoming(at)
        arriving.start()
        arriving.wait()
        for ring in rings.values():
            ring.step()
        me = lax.axis_index("seq")
        offset = at["off"][me // 2]
        whole = at["all"]
        total = at["sum"]
        for h in range(2):
            lines = slice(h * vf // 2, (h + 1) * vf // 2)
            k_lines = slice(h * QK, (h + 1) * QK)
            v_lines = slice(2 * QK + h * vf // 2, 2 * QK + (h + 1) * vf // 2)
            for i in range(n - 1, -1, -1):
                here, upto = slice(i * tok, (i + 1) * tok), slice(0, (i + 1) * tok)
                q = whole[h * QK : (h + 1) * QK, here]
                k = whole[(2 + h) * QK : (3 + h) * QK, upto]
                v = whole[4 * QK + h * vf // 2 : 4 * QK + (h + 1) * vf // 2, upto]
                mask = causal(offset, i, tok)
                s = dot(k, q, 0, 0) * (QK**-0.5)
                w = jnp.where(mask, 1.0 + s + 0.5 * s * s, 0.0).astype(BF)
                dan = (at["da_all"][lines, here].astype(F32) / at["den"][h : h + 1, here]).astype(BF)
                delta = jnp.sum(dan.astype(F32) * at["att"][lines, here], axis=0, keepdims=True)
                ds = jnp.where(mask, (dot(v, dan, 0, 0) - delta) * (1.0 + s), 0.0).astype(BF)
                dq = dot(k, ds, 1, 0) * (QK**-0.5)
                at["own"][h * QK : (h + 1) * QK, here] = dq.astype(BF)
                dk = dot(q, ds, 1, 1) * (QK**-0.5)
                dv = dot(dan, w, 1, 1)
                if i == n - 1:
                    total[k_lines, upto] = dk
                    total[v_lines, upto] = dv
                else:
                    total[k_lines, upto] += dk
                    total[v_lines, upto] += dv
        at["own"][2 * QK :, :] = total[...].astype(BF)
        leaving = Exchange(
            n, at, "out", at_positions(at["own"], tok), lambda me: to_pair(at["d_t"], features, tok)(me)
        )
        leaving.start()
        for ring in rings.values():
            ring.step()
        leaving.wait()
        at["d"][...] = at["d_t"][...].astype(F32).T.astype(BF)
        for j in range(width // 256):
            lines = slice(j * 256, (j + 1) * 256)
            at["part"][:, lines] = dot(at["d"][...], at["weight"][lines, :], 1, 1).astype(BF)
        for _ in range(n // 2):
            for ring in rings.values():
                ring.step()
        arriving.wait_sent()
        leaving.wait_sent()

    out = call.run(body)
    return out["d"], out["part"], [out[f"s{j}"] for j in range(len(pairs))]


def by_rows(kernel, scal, place, operands, widths, kinds):
    rows = operands[0].shape[0]
    tok = operands[0].shape[1]
    specs = [
        pl.BlockSpec(memory_space=pltpu.SMEM),
        pl.BlockSpec(place.shape, lambda r: (0, 0)),
    ]
    specs += [pl.BlockSpec((1,) + a.shape[1:], lambda r: (r, 0, 0)) for a in operands]
    return pl.pallas_call(
        kernel,
        grid=(rows,),
        in_specs=specs,
        out_specs=[pl.BlockSpec((1, tok, w), lambda r: (r, 0, 0)) for w in widths],
        out_shape=[jax.ShapeDtypeStruct((rows, tok, w), t) for w, t in zip(widths, kinds)],
        compiler_params=pltpu.CompilerParams(vmem_limit_bytes=48 * 1024 * 1024),
    )(scal, place, *operands)


def rms_scale(x):
    return lax.rsqrt(jnp.mean(x * x, axis=-1, keepdims=True) + EPSILON)


def rms_norm(x, gain):
    return x * rms_scale(x) * gain


def rms_back(x, gain, dn):
    scale = rms_scale(x)
    unit = x * scale
    gain_grad = jnp.sum(dn * unit, axis=0)
    dg = dn * gain
    dx = scale * (dg - unit * jnp.mean(dg * unit, axis=-1, keepdims=True))
    return dx, gain_grad


def closing_kernel(count, *refs):
    x_ref, dn_ref, grad_ref, gain_ref, qkv_ref, small_ref = refs[:6]
    srcs, turned, refs = refs[6 : 6 + count], refs[6 + count : 8 + count], refs[8 + count :]
    out_ref, (q_ref, k_ref, v_ref), gains_ref, taps_ref = refs[0], refs[1:4], refs[4], refs[5]
    across, dsts = refs[6:8], refs[8:]
    gain = gain_ref[:1].astype(F32)
    dx, _ = rms_back(x_ref[...].astype(F32), gain, dn_ref[...].astype(F32))
    out_ref[...] = grad_ref[...] + dx
    for src, dst in zip(srcs, dsts):
        dst[...] = src[...]

    @pl.when(pl.program_id(0) == 0)
    def _():
        q, v = q_ref.shape[0] // 2, v_ref.shape[1] // 2
        halves = [qkv_ref[:, g * (2 * q + v) : (g + 1) * (2 * q + v)] for g in range(2)]
        q_ref[...] = jnp.concatenate([a[:, :q] for a in halves], axis=1).T
        k_ref[...] = jnp.concatenate([a[:, q : 2 * q] for a in halves], axis=1).T
        v_ref[...] = jnp.concatenate([a[:, 2 * q :] for a in halves], axis=1)
        norms = gains_ref.shape[0]
        gains_ref[...] = small_ref[:norms]
        taps_ref[...] = small_ref[norms : norms + taps_ref.shape[0], : taps_ref.shape[1]]

    for i in range(2):

        @pl.when(pl.program_id(0) == i + 1)
        def _():
            across[i][...] = turned[i][...].T


def closing(x, dn, grad, gains, qkv, widths, small, taps, results, turned):
    steps = 4

    def rows(a):
        return pl.BlockSpec((a.shape[0] // steps, a.shape[1]), lambda i: (i, 0))

    def whole(a):
        return pl.BlockSpec(a.shape, lambda i: (0, 0))

    height = qkv.shape[0]
    fixed = [(widths[0], height), (widths[1], height), (height, widths[2]), gains.shape, taps.shape]
    fixed += [r.shape[::-1] for r in turned]
    fixed = [jax.ShapeDtypeStruct(k, F32) for k in fixed]
    same = [jax.ShapeDtypeStruct(r.shape, F32) for r in results]
    shape = jax.ShapeDtypeStruct(x.shape, F32)
    out = pl.pallas_call(
        partial(closing_kernel, len(results)),
        grid=(steps,),
        in_specs=[rows(x), rows(dn), rows(grad), whole(gains), whole(qkv), whole(small)]
        + [rows(r) for r in results]
        + [whole(r) for r in turned],
        out_specs=[rows(shape)] + [whole(k) for k in fixed] + [rows(a) for a in same],
        out_shape=[shape] + fixed + same,
        compiler_params=pltpu.CompilerParams(vmem_limit_bytes=58 * MIB),
    )(x, dn, grad, gains, qkv, small, *results, *turned)
    return out[0], (out[1].T, out[2].T, out[3]), out[4], out[5], out[6:8], out[8:]


def head_total(partial_sum):
    return lax.psum(partial_sum, "head").astype(F32)


def tie(xs, *others):
    return list(lax.optimization_barrier((tuple(xs), tuple(others)))[0])


def mlp_forward(resid, gain, weights):
    gate_w, up_w, down_t = weights
    normed = rms_norm(resid, gain).astype(BF)
    gate_val = dot(normed, gate_w, 1, 0)
    up_val = dot(normed, up_w, 1, 0)
    hidden = (gate_val * jax.nn.sigmoid(gate_val) * up_val).astype(BF)
    return dot(hidden, down_t, 1, 1).astype(BF), (normed, gate_val, up_val, hidden)


def mlp_scatter(kept, call_id, *others):
    (normed, grad_b), d_gate, d_up, hidden = kept
    normed, grad_b = tie((normed, grad_b), *others)
    return scatter_all((normed, grad_b), ((0, d_gate), (0, d_up), (1, hidden)), call_id)


def mlp_backward(grad_b, saved, weights):
    gate_w, up_w, down_t = weights
    normed, gate_val, up_val, hidden = saved
    dh = dot(grad_b, down_t, 1, 0)
    sig = jax.nn.sigmoid(gate_val)
    silu = gate_val * sig
    d_gate = (dh * up_val * (sig * (1.0 + gate_val * (1.0 - sig)))).astype(BF)
    d_up = (dh * silu).astype(BF)
    dn_part = (dot(d_gate, gate_w, 1, 1) + dot(d_up, up_w, 1, 1)).astype(BF)
    return dn_part, ((normed, grad_b), d_gate, d_up, hidden)


def shifted(block, before, shift):
    if shift == 0:
        return block
    return jnp.concatenate([before[:, before.shape[1] - shift :], block[:, :-shift]], axis=1)


def advanced(block, after, shift):
    if shift == 0:
        return block
    return jnp.concatenate([block[:, shift:], after[:, :shift]], axis=1)


def per_device(
    activations,
    offsets,
    cotangent,
    attn_query,
    attn_key,
    attn_value,
    attn_output,
    ffn1_gate,
    ffn1_up,
    ffn1_down,
    conv_input,
    conv_gate,
    conv_output,
    conv_kernel,
    ffn2_gate,
    ffn2_up,
    ffn2_down,
    norm_gains,
):
    n = lax.axis_size("seq")
    micro, row_count, tok, width = activations.shape
    rows = micro * row_count
    count = rows * tok
    qw, vw = attn_query.shape[1], attn_value.shape[1]
    cw = conv_input.shape[1]
    taps = conv_kernel.shape[0]
    here = lax.axis_index("seq")
    start = here * tok
    off = offsets.reshape(rows)

    paired = ring_size(n) and 2 * rows == n and qw == 4 * QK
    gains = norm_gains.astype(F32)
    kernel_f = conv_kernel.astype(F32)
    acts_flat = activations.reshape(count, width)
    inputs = acts_flat.astype(F32)
    grad_four = cotangent.reshape(count, width)
    if paired:
        normed_a, qkv_w, outs_s = first_gather(
            acts_flat,
            norm_gains,
            (attn_query.T, attn_key.T, attn_value),
            (attn_output, conv_output),
            1,
        )
    else:
        normed_a = rms_norm(inputs, gains[0]).astype(BF)
        qkv_s = jnp.concatenate([attn_query, attn_key, attn_value], axis=1)
        (qkv_w,) = gather_all([qkv_s], 1)
        outs_s = jnp.concatenate([attn_output.T, conv_output.T], axis=1)

    scal = jnp.concatenate([start[None].astype(jnp.int32), off])
    place = jnp.arange(n * tok, dtype=jnp.int32).reshape(1, n * tok)

    def by_sequence(blocks):
        return jnp.swapaxes(blocks.reshape(n, rows, tok, -1), 0, 1).reshape(rows, n * tok, -1)

    if paired:
        attention, (outs_t, gate_1) = attend_pairs(off, qkv_w, normed_a, (outs_s, ffn1_gate), 2)
        mixed = attention["mixed"]
    else:
        qkv = dot(normed_a, qkv_w, 1, 0).astype(BF)
        qkv_all = by_sequence(gather_all([qkv], 2)[0])
        own = qkv.reshape(rows, tok, -1)
        q_own, k_own, v_own = own[..., :qw], own[..., qw : 2 * qw], own[..., 2 * qw :]
        q_all, k_all, v_all = qkv_all[..., :qw], qkv_all[..., qw : 2 * qw], qkv_all[..., 2 * qw :]
        (mixed,) = by_rows(attend_kernel, scal, place, (q_own, k_all, v_all), (vw,), (BF,))
        mixed = mixed.reshape(count, vw)
        outs_t, gate_1 = gather_all((outs_s, ffn1_gate), 11)
    out_t, conv_out_t = outs_t[:, :vw], outs_t[:, vw:]
    attn_part = dot(mixed, out_t, 1, 1).astype(BF)
    attn_sum = head_total(attn_part)
    ffn1 = [gate_1] + gather_all(tie((ffn1_up, ffn1_down.T), attn_part), 12)
    resid_one = inputs + attn_sum
    part, kept_one = mlp_forward(resid_one, gains[1], ffn1)
    ffn1_sum = head_total(part)
    pair_s = jnp.concatenate([conv_input, conv_gate], axis=1)
    pair_w, gate_2 = gather_all(tie((pair_s, ffn2_gate), part), 4)
    resid_two = resid_one + ffn1_sum

    normed_c = rms_norm(resid_two, gains[2]).astype(BF)
    pair_c = dot(normed_c, pair_w, 1, 0)
    inner = pair_c[:, :cw].reshape(rows, tok, cw)
    gate_c = pair_c[:, cw:].reshape(rows, tok, cw)
    pos = start + jnp.arange(tok + taps - 1, dtype=jnp.int32)
    current = pos[None, :] >= off[:, None]

    def valid(t, first, length):
        p = pos[None, first : first + length]
        source = p - t
        same = (source >= off[:, None]) == current[:, first : first + length]
        return ((source >= 0) & same).astype(F32)[:, :, None]

    edge = lax.ppermute(inner[:, tok - (taps - 1) :], "seq", [(i, i + 1) for i in range(n - 1)])
    moved = [shifted(inner, edge, t) * valid(t, 0, tok) for t in range(taps)]
    conv = sum(kernel_f[t][None, None, :] * moved[t] for t in range(taps))
    product = (conv * gate_c).astype(BF).reshape(count, cw)
    conv_part = dot(product, conv_out_t, 1, 1).astype(BF)
    conv_sum = head_total(conv_part)
    ffn2 = [gate_2] + gather_all(tie((ffn2_up, ffn2_down.T), conv_part), 12)
    resid_three = resid_two + conv_sum
    out_part, kept_two = mlp_forward(resid_three, gains[3], ffn2)

    dn_part, grads_two = mlp_backward(grad_four, kept_two, ffn2)
    both = lax.psum(jnp.concatenate([dn_part, out_part]), "head")
    dn, out_sum = both[:count].astype(F32), both[count:]
    sums_two = mlp_scatter(grads_two, 5, dn_part, out_part)
    (dn,) = tie((dn,), *sums_two)
    block_output = (resid_three + out_sum.astype(F32)).astype(BF).reshape(activations.shape)
    dx, gain_four = rms_back(resid_three, gains[3], dn)
    grad_three = grad_four.astype(F32) + dx
    grad_b = grad_three.astype(BF)
    d_product = dot(grad_b, conv_out_t, 1, 0).reshape(rows, tok, cw)
    d_gate_c = (d_product * conv).astype(BF).reshape(count, cw)
    d_conv = d_product * gate_c
    next_rows = lax.ppermute(d_conv[:, : taps - 1], "seq", [(i + 1, i) for i in range(n - 1)])
    d_inner = sum(
        kernel_f[t][None, None, :] * advanced(d_conv, next_rows, t) * valid(t, t, tok)
        for t in range(taps)
    )
    d_inner = d_inner.astype(BF).reshape(count, cw)
    kernel_grad = jnp.stack([jnp.sum(d_conv * moved[t], axis=(0, 1)) for t in range(taps)])
    d_pair = jnp.concatenate([d_inner, d_gate_c], axis=1)
    dn_part = dot(d_pair, pair_w, 1, 1).astype(BF)
    dn = head_total(dn_part)
    sums_conv = scatter_all(
        tie((normed_c, grad_b), dn_part),
        ((0, d_pair), (1, product)),
        6,
        1,
    )
    (dn,) = tie((dn,), *sums_conv)
    dx, gain_three = rms_back(resid_two, gains[2], dn)
    grad_two = grad_three + dx
    dn_part, grads_one = mlp_backward(grad_two.astype(BF), kept_one, ffn1)
    dn = head_total(dn_part)
    (normed_1, grad_b1), d_gate_1, d_up_1, hidden_1 = grads_one
    if ring_size(n):
        sums_one = scatter_all(tie((normed_1,), dn_part), ((0, d_gate_1),), 9)
        (dn,) = tie((dn,), *sums_one)
    dx, gain_two = rms_back(resid_one, gains[1], dn)
    grad_one = grad_two + dx

    grad_b = grad_one.astype(BF)
    later = ((normed_1, grad_b1), ((0, d_up_1), (1, hidden_1)))
    if paired:
        d_qkv, dn_part, more = attend_pairs_back(off, grad_b, outs_t, qkv_w, attention, later, 7)
        sums_one = sums_one + more
    else:
        da = dot(grad_b, out_t, 1, 0).reshape(rows, tok, vw)
        dq, dan, extra = by_rows(
            query_back_kernel, scal, place, (q_own, k_all, v_all, da), (qw, vw, qw), (BF, BF, BF)
        )
        back = jnp.concatenate([dan, extra], axis=-1).reshape(count, vw + qw)
        back_all = by_sequence(gather_all([back], 7, 1)[0])
        dk, dv = by_rows(
            key_back_kernel,
            scal,
            place,
            (k_own, v_own, q_all, back_all[..., :vw], back_all[..., vw:]),
            (qw, vw),
            (BF, BF),
        )
        sums_one = scatter_all((normed_1,), ((0, d_gate_1),), 9) + scatter_all(*later, 10)
        d_qkv = jnp.concatenate([dq, dk, dv], axis=-1).reshape(count, 2 * qw + vw)
        dn_part = dot(d_qkv, qkv_w, 1, 1).astype(BF)
    dn = lax.psum(dn_part, "head")
    unit = inputs * rms_scale(inputs)
    gain_one = small_sum(jnp.sum(dn_part.astype(F32) * unit, axis=0), "head")
    small = jnp.concatenate(
        [
            jnp.stack([gain_one, gain_two, gain_three, gain_four]),
            jnp.pad(kernel_grad, ((0, 0), (0, width - cw))),
            jnp.zeros((8 - 4 - taps, width), F32),
        ]
    )
    sums_attn = scatter_all(
        tie((normed_a, grad_b), dn_part), ((0, d_qkv), (1, mixed)), 8, 0, small
    )
    gains_grad, kernel_grad = sums_attn[2][:4], sums_attn[2][4 : 4 + taps, :cw]
    qkv_sum = sums_attn[0]
    straight = (sums_one[0], sums_one[1], sums_two[0], sums_two[1], sums_one[2], sums_two[2])
    turned = (sums_conv[1], sums_attn[1])
    if paired:
        input_grad, by_kind, gains_grad, kernel_grad, turned, straight = closing(
            acts_flat,
            dn,
            grad_one,
            norm_gains,
            qkv_sum,
            (qw, qw, vw),
            sums_attn[2],
            conv_kernel,
            straight,
            turned,
        )
    else:
        input_grad = grad_one + rms_back(inputs, gains[0], dn.astype(F32))[0]
        by_kind = (qkv_sum[:, :qw], qkv_sum[:, qw : 2 * qw], qkv_sum[:, 2 * qw :])
        turned = [r.T for r in turned]
    input_grad = input_grad.reshape(activations.shape)
    return (
        block_output,
        input_grad,
        *by_kind,
        turned[1],
        straight[0],
        straight[1],
        straight[4].T,
        sums_conv[0][:, :cw],
        sums_conv[0][:, cw:],
        turned[0],
        kernel_grad,
        straight[2],
        straight[3],
        straight[5].T,
        gains_grad,
    )


def solution(mesh):
    rows_in = P("seq", "head")
    rows_out = P("head", "seq")
    tokens = P(None, None, "seq", None)
    in_specs = (
        (tokens, P(), tokens)
        + (rows_in, rows_in, rows_in, rows_out)
        + (rows_in, rows_in, rows_out)
        + (rows_in, rows_in, rows_out)
        + (P(None, "head"),)
        + (rows_in, rows_in, rows_out)
        + (P(),)
    )
    out_specs = (
        (tokens, tokens)
        + (rows_in, rows_in, rows_in, rows_out)
        + (rows_in, rows_in, rows_out)
        + (rows_in, rows_in, rows_out)
        + (P(None, "head"),)
        + (rows_in, rows_in, rows_out)
        + (P(),)
    )
    return jax.shard_map(
        per_device, mesh=mesh, in_specs=in_specs, out_specs=out_specs, check_vma=False
    )
```
